32 devices in a mesh: row: 2 (over y), col: 16 (over z, x, core).
Axes of the slice: x: 2, y: 2, z: 4, core: 2. Of those that a mesh axis runs over, the one named last changes fastest.
Arguments:
- queries: bfloat16 [4096, 256], P(('row', 'col')), may hold values from -6 to 6
- keys: bfloat16 [4096, 256], P('col', 'row'), may hold values from -6 to 6
- values: bfloat16 [4096, 256], P('col', 'row'), may hold values from -0.59765625 to 0.59765625
- outputs: bfloat16 [4096, 256], P(('row', 'col')), may hold values from -0.59765625 to 0.59765625
- d_out: bfloat16 [4096, 256], P(('row', 'col')), may hold values from -6 to 6
- lse: float32 [2, 4096], P(None, ('row', 'col')), may hold values from 4 to 6
Outputs:
- d_queries: bfloat16 [4096, 256], P(('row', 'col'))
- d_keys: bfloat16 [4096, 256], P('col', 'row')
- d_values: bfloat16 [4096, 256], P('col', 'row')
The draws below stay inside these ranges and needn't reach their ends.
All inputs are finite; a program needn't handle non-finite values.
Results may differ from the reference program's by a relative error of at most 0.0049.
Values may be sent and summed in bfloat16 or wider, within the bound.
A program may use at most 64 MiB of HBM per device.

```python
import math
import jax
import jax.numpy as jnp
from jax import lax

HEAD_DIM = 128
HEADS = 2
SEQ = 4096
HD = 256


def steps_of(own_key, dims, pieces, low, largest):
    loudness, own = 1.0, jax.random.fold_in(own_key, 6)
    for dim, parts in pieces:
        draws = jnp.exp(jax.random.uniform(jax.random.fold_in(own, dim), (parts,), jnp.float32, low / len(pieces), largest / len(pieces)))
        loudness = loudness * jnp.repeat(draws, dims[dim] // parts).reshape([-1 if axis == dim else 1 for axis in range(len(dims))])
    return loudness


def scatter_about(key, dims, width, limit, shards=(), dtype=jnp.bfloat16):
    drawn = width * jax.random.normal(key, dims, jnp.float32)
    if shards:
        drawn = drawn * steps_of(key, dims, shards, -0.22, 0.18)
    return jnp.clip(drawn, -limit, limit).astype(dtype)


def setup_inputs(seed: int = 0) -> dict:
    key_of = jax.random.split(jax.random.key(seed), 7)
    return {
        "queries": scatter_about(key_of[0], (SEQ, HD), 1.0, 6.0, ((0, 32),)),
        "keys": scatter_about(key_of[1], (SEQ, HD), 1.0, 6.0, ((0, 16), (1, 2))),
        "values": scatter_about(key_of[2], (SEQ, HD), 0.1, 0.59765625, ((0, 16), (1, 2))),
        "outputs": scatter_about(key_of[3], (SEQ, HD), 0.1, 0.59765625, ((0, 32),)),
        "d_out": scatter_about(key_of[4], (SEQ, HD), 1.0, 6.0, ((0, 32),)),
        "lse": jnp.clip(4.0 + 2.0 * jax.random.uniform(key_of[5], (HEADS, SEQ), jnp.float32) ** steps_of(key_of[5], (HEADS, SEQ), ((1, 32),), -0.2, 0.2), 4.0, 6.0),
    }


def contract_rows(left, right):
    return lax.dot_general(left, right, (((0,), (0,)), ((), ())), preferred_element_type=jnp.float32)


def head_pass(query_head, key_head, value_head, grad_head, lse_head, delta_head):
    scaling = HEAD_DIM ** -0.5
    block_rows = math.gcd(SEQ, 1024)
    steps_total = SEQ // block_rows
    query_blocks = query_head.reshape(steps_total, block_rows, HEAD_DIM)
    grad_blocks = grad_head.reshape(steps_total, block_rows, HEAD_DIM)
    lse_blocks = lse_head.reshape(steps_total, block_rows)
    delta_blocks = delta_head.reshape(steps_total, block_rows)

    def advance(running, inputs):
        key_sum, value_sum = running
        query_rows, grad_rows, lse_rows, delta_rows = inputs
        scores = jnp.dot(query_rows, key_head.T, preferred_element_type=jnp.float32)
        probs = jnp.exp(scores * scaling - lse_rows[:, None])
        probs_low = probs.astype(jnp.bfloat16)
        grad_probs = jnp.dot(grad_rows, value_head.T, preferred_element_type=jnp.float32)
        grad_scores = (probs * (grad_probs - delta_rows[:, None])).astype(jnp.bfloat16)
        value_sum = value_sum + contract_rows(probs_low, grad_rows)
        key_sum = key_sum + contract_rows(grad_scores, query_rows)
        query_part = jnp.dot(grad_scores, key_head, preferred_element_type=jnp.float32)
        return (key_sum, value_sum), query_part

    empty_sums = jnp.zeros((SEQ, HEAD_DIM), jnp.float32)
    (key_sum, value_sum), query_parts = lax.scan(advance, (empty_sums, empty_sums), (query_blocks, grad_blocks, lse_blocks, delta_blocks))
    query_grad = query_parts.reshape(SEQ, HEAD_DIM) * scaling
    return query_grad, key_sum * scaling, value_sum


def reference(queries, keys, values, outputs, d_out, lse):
    product = d_out.astype(jnp.float32) * outputs.astype(jnp.float32)
    delta = jnp.sum(product.reshape(SEQ, HEADS, HEAD_DIM), axis=2).T
    query_list = []
    key_list = []
    value_list = []
    for head_index in range(HEADS):
        first_col = head_index * HEAD_DIM
        last_col = first_col + HEAD_DIM
        query_grad, key_grad, value_grad = head_pass(queries[:, first_col:last_col], keys[:, first_col:last_col], values[:, first_col:last_col], d_out[:, first_col:last_col], lse[head_index], delta[head_index])
        query_list.append(query_grad)
        key_list.append(key_grad)
        value_list.append(value_grad)
    d_queries = jnp.concatenate(query_list, axis=1).astype(jnp.bfloat16)
    d_keys = jnp.concatenate(key_list, axis=1).astype(jnp.bfloat16)
    d_values = jnp.concatenate(value_list, axis=1).astype(jnp.bfloat16)
    return (d_queries, d_keys, d_values)
```

```python
import functools

import jax
import jax.numpy as jnp
from jax import lax
from jax.experimental import pallas as pl
from jax.experimental.pallas import tpu as pltpu
from jax.sharding import PartitionSpec as P


def block_size(row_total):
    block_rows = row_total
    while block_rows > 512 and block_rows % 2 == 0:
        block_rows = block_rows // 2
    return block_rows


def head_slice(matrix, head_index, head_dim):
    return matrix[:, head_index * head_dim : (head_index + 1) * head_dim]


def contract_rows(left, right):
    return lax.dot_general(
        left, right, (((0,), (0,)), ((), ())), preferred_element_type=jnp.float32
    )


def score_terms(query_head, grad_head, lse_row, delta_row, key_head, value_head, scaling):
    scores = jnp.dot(query_head, key_head.T, preferred_element_type=jnp.float32)
    probs = jnp.exp(scores * scaling - lse_row[:, None])
    probs_low = probs.astype(jnp.bfloat16)
    grad_probs = jnp.dot(grad_head, value_head.T, preferred_element_type=jnp.float32)
    grad_scores = (probs * (grad_probs - delta_row[:, None])).astype(jnp.bfloat16)
    return (probs_low, grad_scores)


def block_grads(query_rows, grad_rows, lse_rows, delta_rows, key_all, value_all, head_dim):
    head_total = lse_rows.shape[0]
    scaling = head_dim ** (-0.5)
    key_terms = []
    value_terms = []
    for head_index in range(head_total):
        query_head = head_slice(query_rows, head_index, head_dim)
        grad_head = head_slice(grad_rows, head_index, head_dim)
        key_head = head_slice(key_all, head_index, head_dim)
        value_head = head_slice(value_all, head_index, head_dim)
        probs_low, grad_scores = score_terms(
            query_head,
            grad_head,
            lse_rows[head_index],
            delta_rows[head_index],
            key_head,
            value_head,
            scaling,
        )
        value_terms.append(contract_rows(probs_low, grad_head))
        key_terms.append(contract_rows(grad_scores, query_head))
    key_term = jnp.concatenate(key_terms, axis=1)
    value_term = jnp.concatenate(value_terms, axis=1)
    query_term = None
    return (key_term, value_term, query_term)


def split_blocks(query_all, grad_all, lse_all, delta_all):
    row_total, features = query_all.shape
    block_rows = block_size(row_total)
    steps_total = row_total // block_rows
    head_total = lse_all.shape[0]
    query_blocks = query_all.reshape(steps_total, block_rows, features)
    grad_blocks = grad_all.reshape(steps_total, block_rows, features)
    lse_blocks = lse_all.reshape(head_total, steps_total, block_rows).transpose(1, 0, 2)
    delta_blocks = delta_all.reshape(head_total, steps_total, block_rows).transpose(1, 0, 2)
    return (query_blocks, grad_blocks, lse_blocks, delta_blocks)


def query_pass(query_all, grad_all, lse_all, delta_all, key_all, value_all, head_dim):
    row_total, features = query_all.shape
    block_inputs = split_blocks(query_all, grad_all, lse_all, delta_all)
    empty_sums = jnp.zeros((key_all.shape[0], features), jnp.float32)

    def advance(running, inputs):
        key_sum, value_sum = running
        query_rows, grad_rows, lse_rows, delta_rows = inputs
        key_term, value_term, query_term = block_grads(
            query_rows, grad_rows, lse_rows, delta_rows, key_all, value_all, head_dim
        )
        return ((key_sum + key_term, value_sum + value_term), query_term)

    (key_sum, value_sum), query_terms = lax.scan(advance, (empty_sums, empty_sums), block_inputs)
    return (key_sum, value_sum, query_terms)


def query_only(query_rows, grad_rows, lse_rows, delta_rows, key_all, value_all, head_dim):
    row_total, features = query_rows.shape
    head_total = lse_rows.shape[0]
    scaling = head_dim ** (-0.5)
    block_inputs = split_blocks(query_rows, grad_rows, lse_rows, delta_rows)

    def one_block(inputs):
        query_part, grad_part, lse_part, delta_part = inputs
        pieces = []
        for head_index in range(head_total):
            query_head = head_slice(query_part, head_index, head_dim)
            grad_head = head_slice(grad_part, head_index, head_dim)
            key_head = head_slice(key_all, head_index, head_dim)
            value_head = head_slice(value_all, head_index, head_dim)
            probs_low, grad_scores = score_terms(
                query_head,
                grad_head,
                lse_part[head_index],
                delta_part[head_index],
                key_head,
                value_head,
                scaling,
            )
            pieces.append(jnp.dot(grad_scores, key_head, preferred_element_type=jnp.float32))
        return jnp.concatenate(pieces, axis=1)

    return lax.map(one_block, block_inputs).reshape(row_total, features)


def head_delta(d_out, outputs, head_total, head_dim):
    product = d_out.astype(jnp.float32) * outputs.astype(jnp.float32)
    return jnp.sum(product.reshape(product.shape[0], head_total, head_dim), axis=2).T


def per_device(queries, keys, values, outputs, d_out, lse):
    head_total = lse.shape[0]
    head_dim = queries.shape[1] // head_total
    scaling = head_dim ** (-0.5)
    delta = head_delta(d_out, outputs, head_total, head_dim)
    key_all, value_all = (
        lax.all_gather(keys, "row", axis=1, tiled=True),
        lax.all_gather(values, "row", axis=1, tiled=True),
    )
    query_all, grad_all = (
        lax.all_gather(queries, "col", axis=0, tiled=True),
        lax.all_gather(d_out, "col", axis=0, tiled=True),
    )
    lse_all, delta_all = (
        lax.all_gather(lse, "col", axis=1, tiled=True),
        lax.all_gather(delta, "col", axis=1, tiled=True),
    )
    key_sum, value_sum, unused_terms = query_pass(
        query_all, grad_all, lse_all, delta_all, key_all, value_all, head_dim
    )

    def query_term(first_row, row_total):
        return query_only(query_all, grad_all, lse_all, delta_all, key_all, value_all, head_dim)

    query_grad = lax.psum_scatter(
        query_term(jnp.int32(0), queries.shape[0] * lax.axis_size("col")),
        "col",
        scatter_dimension=0,
        tiled=True,
    )
    key_grad, value_grad = (
        lax.psum_scatter(key_sum, "row", scatter_dimension=1, tiled=True),
        lax.psum_scatter(value_sum, "row", scatter_dimension=1, tiled=True),
    )
    d_queries = (query_grad * scaling).astype(jnp.bfloat16)
    d_keys = (key_grad * scaling).astype(jnp.bfloat16)
    d_values = value_grad.astype(jnp.bfloat16)
    return (d_queries, d_keys, d_values)

LOG2E = 1.4426950408889634


def flip(index, bits):
    if bits == 1:
        return index + 1 - 2 * lax.rem(index, 2)
    if bits == 2:
        return lax.rem(index + 2, 4)
    if bits == 3:
        return 3 - index
    return index


def fused_kernel(
    head_total,
    q_ref,
    k_ref,
    v_ref,
    o_ref,
    g_ref,
    lse_ref,
    dq_ref,
    dk_ref,
    dv_ref,
    qd_out,
    qd_in,
    st_out,
    st_in,
    kv_in,
    kt_in,
    dk_acc,
    dv_acc,
    dq_out,
    dq_in,
    dkv_out,
    dkv_in,
    qd_ssem,
    qd_rsem,
    st_ssem,
    st_rsem,
    kv_ssem,
    kv_rsem,
    dq_ssem,
    dq_rsem,
    dkv_ssem,
    dkv_rsem,
):
    row = lax.axis_index("row")
    col = lax.axis_index("col")
    zone = col // 4
    lane = lax.rem(col, 4)
    other = 1 - row
    dim = k_ref.shape[1]
    scaling = dim ** (-0.5)
    MESH = pl.DeviceIdType.MESH

    def at(r, z, m):
        return (r, z * 4 + m)

    mates = [at(row, zone, flip(lane, j)) for j in (1, 2, 3)]
    owners = [at(other, zone, lane)]
    for s in (1, 2, 3):
        owners += [at(r, flip(zone, s), lane) for r in range(head_total)]
    barrier = pltpu.get_barrier_semaphore()
    for peer in mates + owners:
        pl.semaphore_signal(barrier, inc=1, device_id=peer, device_id_type=MESH)

    for h in range(head_total):
        cols = slice(h * dim, (h + 1) * dim)
        grad_part = g_ref[:, cols]
        qd_out[h, 0] = q_ref[:, cols]
        qd_out[h, 1] = grad_part
        product = grad_part.astype(jnp.float32) * o_ref[:, cols].astype(jnp.float32)
        delta = lax.dot_general(
            jnp.ones((8, dim), jnp.float32),
            product,
            (((1,), (1,)), ((), ())),
            precision=lax.Precision.HIGHEST,
            preferred_element_type=jnp.float32,
        )
        lse_rows = jnp.broadcast_to(lse_ref[h : h + 1, :] * LOG2E, delta.shape)
        upper = lax.broadcasted_iota(jnp.int32, delta.shape, 0) < 4
        st_out[h] = jnp.where(upper, lse_rows, delta)
    kv_in[lane, 0] = k_ref[...]
    kv_in[lane, 1] = v_ref[...]
    qd_in[zone, 0, row] = qd_out[row, 0]
    qd_in[zone, 1, row] = qd_out[row, 1]
    st_in[zone, row] = st_out[row]

    pl.semaphore_wait(barrier, len(mates) + len(owners))

    def kv_copy(j, slot):
        return pltpu.make_async_remote_copy(
            src_ref=kv_in.at[lane],
            dst_ref=kv_in.at[slot],
            send_sem=kv_ssem.at[j],
            recv_sem=kv_rsem.at[slot],
            device_id=at(row, zone, flip(lane, j)),
            device_id_type=MESH,
        )

    def qd_copies(s, r, slot_zone, slot_row):
        peer = at(r, flip(zone, s), lane)
        return (
            pltpu.make_async_remote_copy(
                src_ref=st_out.at[r],
                dst_ref=st_in.at[slot_zone, slot_row],
                send_sem=st_ssem.at[s, r],
                recv_sem=st_rsem.at[slot_zone, slot_row],
                device_id=peer,
                device_id_type=MESH,
            ),
            pltpu.make_async_remote_copy(
                src_ref=qd_out.at[r],
                dst_ref=qd_in.at[slot_zone, :, slot_row],
                send_sem=qd_ssem.at[s, r],
                recv_sem=qd_rsem.at[slot_zone, slot_row],
                device_id=peer,
                device_id_type=MESH,
            ),
        )

    def rows_of(s):
        return [other] if s == 0 else list(range(head_total))

    sends = []

    def launch(copy):
        copy.start()
        sends.append(copy)

    for j in (2, 3, 1):
        launch(kv_copy(j, lane))
    for s in (0, 2, 3, 1):
        for r in rows_of(s):
            for copy in qd_copies(s, r, zone, row):
                launch(copy)

    def dq_copy(s, r, slot_row, slot_zone):
        there = flip(zone, s)
        return pltpu.make_async_remote_copy(
            src_ref=dq_out.at[there, r],
            dst_ref=dq_in.at[slot_row, slot_zone],
            send_sem=dq_ssem.at[s, r],
            recv_sem=dq_rsem.at[slot_row, slot_zone],
            device_id=at(r, there, lane),
            device_id_type=MESH,
        )

    def dkv_copy(j, slot):
        there = flip(lane, j)
        return pltpu.make_async_remote_copy(
            src_ref=dkv_out.at[there],
            dst_ref=dkv_in.at[slot],
            send_sem=dkv_ssem.at[j],
            recv_sem=dkv_rsem.at[slot],
            device_id=at(row, zone, there),
            device_id_type=MESH,
        )

    steps = (0, 1, 2, 3)
    for s in steps:
        there = flip(zone, s)
        for r in rows_of(s):
            for copy in qd_copies(s, r, there, r):
                copy.wait_recv()
        rows2 = head_total * q_ref.shape[0]
        query = qd_in[there, 0].reshape(rows2, dim)
        grad = qd_in[there, 1].reshape(rows2, dim)
        lse_row = jnp.concatenate([st_in[there, r, 0:1, :] for r in range(head_total)], axis=1)
        delta_row = jnp.concatenate([st_in[there, r, 4:5, :] for r in range(head_total)], axis=1)
        query_sum = None
        order = (0, 1, 2, 3) if s < 3 else (2, 3, 1, 0)
        for j in order:
            slot = flip(lane, j)
            if s == 0:
                if j > 0:
                    kv_copy(j, slot).wait_recv()
                kt_in[slot] = kv_in[slot, 0].T
            key = kv_in[slot, 0]
            value = kv_in[slot, 1]
            dims = (((1,), (1,)), ((), ()))
            scores = lax.dot_general(key, query, dims, preferred_element_type=jnp.float32)
            grad_probs = lax.dot_general(value, grad, dims, preferred_element_type=jnp.float32)
            probs = jnp.exp2(scores * (scaling * LOG2E) - lse_row)
            probs_low = probs.astype(jnp.bfloat16)
            grad_scores = (probs * (grad_probs - delta_row)).astype(jnp.bfloat16)
            value_term = jnp.dot(probs_low, grad, preferred_element_type=jnp.float32)
            key_term = jnp.dot(grad_scores, query, preferred_element_type=jnp.float32)
            query_term = jnp.dot(kt_in[slot], grad_scores, preferred_element_type=jnp.float32)
            query_sum = query_term if query_sum is None else query_sum + query_term
            if s > 0:
                key_term = dk_acc[slot] + key_term
                value_term = dv_acc[slot] + value_term
            if s == 3 and j > 0:
                dkv_out[slot, 0] = key_term.astype(jnp.bfloat16)
                dkv_out[slot, 1] = value_term.astype(jnp.bfloat16)
                launch(dkv_copy(j, lane))
            else:
                dk_acc[slot] = key_term
                dv_acc[slot] = value_term
        query_low = query_sum.astype(jnp.bfloat16)
        block = q_ref.shape[0]
        for r in range(head_total):
            dq_out[there, r] = query_low[:, r * block : (r + 1) * block]
        if s == 0:
            dq_in[row, zone] = dq_out[zone, row]
        for r in rows_of(s):
            launch(dq_copy(s, r, row, zone))

    for s in steps:
        for r in rows_of(s):
            dq_copy(s, r, r, flip(zone, s)).wait_recv()
    for h in range(head_total):
        total = dq_in[h, 0].astype(jnp.float32)
        for z in range(1, 4):
            total = total + dq_in[h, z].astype(jnp.float32)
        dq_ref[:, h * dim : (h + 1) * dim] = (total * scaling).T.astype(jnp.bfloat16)

    key_sum = dk_acc[lane]
    value_sum = dv_acc[lane]
    for j in (1, 2, 3):
        slot = flip(lane, j)
        dkv_copy(j, slot).wait_recv()
        key_sum = key_sum + dkv_in[slot, 0].astype(jnp.float32)
        value_sum = value_sum + dkv_in[slot, 1].astype(jnp.float32)
    dk_ref[...] = (key_sum * scaling).astype(jnp.bfloat16)
    dv_ref[...] = value_sum.astype(jnp.bfloat16)
    for copy in sends:
        copy.wait_send()


def fused_device(queries, keys, values, outputs, d_out, lse):
    head_total = lse.shape[0]
    block = queries.shape[0]
    key_rows, dim = keys.shape
    zones, lanes = 4, 4
    bf16, f32 = jnp.bfloat16, jnp.float32
    dma = pltpu.SemaphoreType.DMA
    vmem = pl.BlockSpec(memory_space=pltpu.VMEM)
    pairs = head_total * block * zones * key_rows * lanes
    return pl.pallas_call(
        functools.partial(fused_kernel, head_total),
        out_shape=(
            jax.ShapeDtypeStruct(queries.shape, bf16),
            jax.ShapeDtypeStruct(keys.shape, bf16),
            jax.ShapeDtypeStruct(values.shape, bf16),
        ),
        in_specs=[vmem] * 6,
        out_specs=(vmem, vmem, vmem),
        scratch_shapes=[
            pltpu.VMEM((head_total, 2, block, dim), bf16),
            pltpu.VMEM((zones, 2, head_total, block, dim), bf16),
            pltpu.VMEM((head_total, 8, block), f32),
            pltpu.VMEM((zones, head_total, 8, block), f32),
            pltpu.VMEM((lanes, 2, key_rows, dim), bf16),
            pltpu.VMEM((lanes, dim, key_rows), bf16),
            pltpu.VMEM((lanes, key_rows, dim), f32),
            pltpu.VMEM((lanes, key_rows, dim), f32),
            pltpu.VMEM((zones, head_total, dim, block), bf16),
            pltpu.VMEM((head_total, zones, dim, block), bf16),
            pltpu.VMEM((lanes, 2, key_rows, dim), bf16),
            pltpu.VMEM((lanes, 2, key_rows, dim), bf16),
            dma((zones, head_total)),
            dma((zones, head_total)),
            dma((zones, head_total)),
            dma((zones, head_total)),
            dma((lanes,)),
            dma((lanes,)),
            dma((zones, head_total)),
            dma((head_total, zones)),
            dma((lanes,)),
            dma((lanes,)),
        ],
        compiler_params=pltpu.CompilerParams(
            collective_id=0, has_side_effects=True, vmem_limit_bytes=32 * 1024 * 1024
        ),
        cost_estimate=pl.CostEstimate(
            flops=10 * pairs * dim, bytes_accessed=9 * block * 2 * dim * 2, transcendentals=pairs
        ),
    )(queries, keys, values, outputs, d_out, lse)


def solution(mesh):
    placed = (
        P(("row", "col"), None),
        P("col", "row"),
        P("col", "row"),
        P(("row", "col"), None),
        P(("row", "col"), None),
        P(None, ("row", "col")),
    )
    fused = mesh.shape["row"] == 2 and mesh.shape["col"] == 16

    def local(queries, keys, values, outputs, d_out, lse):
        head_dim = queries.shape[1] // lse.shape[0]
        fits = lse.shape[0] == mesh.shape["row"] and head_dim == 128 and queries.shape[0] == 128
        chosen = fused_device if fused and fits else per_device
        return chosen(queries, keys, values, outputs, d_out, lse)

    return jax.shard_map(
        local,
        mesh=mesh,
        in_specs=placed,
        out_specs=(P(("row", "col"), None), P("col", "row"), P("col", "row")),
        check_vma=False,
    )
```

```python
import functools

import jax
import jax.numpy as jnp
from jax import lax
from jax.experimental import pallas as pl
from jax.experimental.pallas import tpu as pltpu
from jax.sharding import PartitionSpec as P


def block_size(row_total):
    block_rows = row_total
    while block_rows > 512 and block_rows % 2 == 0:
        block_rows = block_rows // 2
    return block_rows


def head_slice(matrix, head_index, head_dim):
    return matrix[:, head_index * head_dim : (head_index + 1) * head_dim]


def contract_rows(left, right):
    return lax.dot_general(
        left, right, (((0,), (0,)), ((), ())), preferred_element_type=jnp.float32
    )


def score_terms(query_head, grad_head, lse_row, delta_row, key_head, value_head, scaling):
    scores = jnp.dot(query_head, key_head.T, preferred_element_type=jnp.float32)
    probs = jnp.exp(scores * scaling - lse_row[:, None])
    probs_low = probs.astype(jnp.bfloat16)
    grad_probs = jnp.dot(grad_head, value_head.T, preferred_element_type=jnp.float32)
    grad_scores = (probs * (grad_probs - delta_row[:, None])).astype(jnp.bfloat16)
    return (probs_low, grad_scores)


def block_grads(query_rows, grad_rows, lse_rows, delta_rows, key_all, value_all, head_dim):
    head_total = lse_rows.shape[0]
    scaling = head_dim ** (-0.5)
    key_terms = []
    value_terms = []
    for head_index in range(head_total):
        query_head = head_slice(query_rows, head_index, head_dim)
        grad_head = head_slice(grad_rows, head_index, head_dim)
        key_head = head_slice(key_all, head_index, head_dim)
        value_head = head_slice(value_all, head_index, head_dim)
        probs_low, grad_scores = score_terms(
            query_head,
            grad_head,
            lse_rows[head_index],
            delta_rows[head_index],
            key_head,
            value_head,
            scaling,
        )
        value_terms.append(contract_rows(probs_low, grad_head))
        key_terms.append(contract_rows(grad_scores, query_head))
    key_term = jnp.concatenate(key_terms, axis=1)
    value_term = jnp.concatenate(value_terms, axis=1)
    query_term = None
    return (key_term, value_term, query_term)


def split_blocks(query_all, grad_all, lse_all, delta_all):
    row_total, features = query_all.shape
    block_rows = block_size(row_total)
    steps_total = row_total // block_rows
    head_total = lse_all.shape[0]
    query_blocks = query_all.reshape(steps_total, block_rows, features)
    grad_blocks = grad_all.reshape(steps_total, block_rows, features)
    lse_blocks = lse_all.reshape(head_total, steps_total, block_rows).transpose(1, 0, 2)
    delta_blocks = delta_all.reshape(head_total, steps_total, block_rows).transpose(1, 0, 2)
    return (query_blocks, grad_blocks, lse_blocks, delta_blocks)


def query_pass(query_all, grad_all, lse_all, delta_all, key_all, value_all, head_dim):
    row_total, features = query_all.shape
    block_inputs = split_blocks(query_all, grad_all, lse_all, delta_all)
    empty_sums = jnp.zeros((key_all.shape[0], features), jnp.float32)

    def advance(running, inputs):
        key_sum, value_sum = running
        query_rows, grad_rows, lse_rows, delta_rows = inputs
        key_term, value_term, query_term = block_grads(
            query_rows, grad_rows, lse_rows, delta_rows, key_all, value_all, head_dim
        )
        return ((key_sum + key_term, value_sum + value_term), query_term)

    (key_sum, value_sum), query_terms = lax.scan(advance, (empty_sums, empty_sums), block_inputs)
    return (key_sum, value_sum, query_terms)


def query_only(query_rows, grad_rows, lse_rows, delta_rows, key_all, value_all, head_dim):
    row_total, features = query_rows.shape
    head_total = lse_rows.shape[0]
    scaling = head_dim ** (-0.5)
    block_inputs = split_blocks(query_rows, grad_rows, lse_rows, delta_rows)

    def one_block(inputs):
        query_part, grad_part, lse_part, delta_part = inputs
        pieces = []
        for head_index in range(head_total):
            query_head = head_slice(query_part, head_index, head_dim)
            grad_head = head_slice(grad_part, head_index, head_dim)
            key_head = head_slice(key_all, head_index, head_dim)
            value_head = head_slice(value_all, head_index, head_dim)
            probs_low, grad_scores = score_terms(
                query_head,
                grad_head,
                lse_part[head_index],
                delta_part[head_index],
                key_head,
                value_head,
                scaling,
            )
            pieces.append(jnp.dot(grad_scores, key_head, preferred_element_type=jnp.float32))
        return jnp.concatenate(pieces, axis=1)

    return lax.map(one_block, block_inputs).reshape(row_total, features)


def head_delta(d_out, outputs, head_total, head_dim):
    product = d_out.astype(jnp.float32) * outputs.astype(jnp.float32)
    return jnp.sum(product.reshape(product.shape[0], head_total, head_dim), axis=2).T


def per_device(queries, keys, values, outputs, d_out, lse):
    head_total = lse.shape[0]
    head_dim = queries.shape[1] // head_total
    scaling = head_dim ** (-0.5)
    delta = head_delta(d_out, outputs, head_total, head_dim)
    key_all, value_all = (
        lax.all_gather(keys, "row", axis=1, tiled=True),
        lax.all_gather(values, "row", axis=1, tiled=True),
    )
    query_all, grad_all = (
        lax.all_gather(queries, "col", axis=0, tiled=True),
        lax.all_gather(d_out, "col", axis=0, tiled=True),
    )
    lse_all, delta_all = (
        lax.all_gather(lse, "col", axis=1, tiled=True),
        lax.all_gather(delta, "col", axis=1, tiled=True),
    )
    key_sum, value_sum, unused_terms = query_pass(
        query_all, grad_all, lse_all, delta_all, key_all, value_all, head_dim
    )

    def query_term(first_row, row_total):
        return query_only(query_all, grad_all, lse_all, delta_all, key_all, value_all, head_dim)

    query_grad = lax.psum_scatter(
        query_term(jnp.int32(0), queries.shape[0] * lax.axis_size("col")),
        "col",
        scatter_dimension=0,
        tiled=True,
    )
    key_grad, value_grad = (
        lax.psum_scatter(key_sum, "row", scatter_dimension=1, tiled=True),
        lax.psum_scatter(value_sum, "row", scatter_dimension=1, tiled=True),
    )
    d_queries = (query_grad * scaling).astype(jnp.bfloat16)
    d_keys = (key_grad * scaling).astype(jnp.bfloat16)
    d_values = value_grad.astype(jnp.bfloat16)
    return (d_queries, d_keys, d_values)

LOG2E = 1.4426950408889634


def flip(index, bits):
    if bits == 1:
        return index + 1 - 2 * lax.rem(index, 2)
    if bits == 2:
        return lax.rem(index + 2, 4)
    if bits == 3:
        return 3 - index
    return index


def fused_kernel(
    head_total,
    q_ref,
    k_ref,
    v_ref,
    o_ref,
    g_ref,
    lse_ref,
    dq_ref,
    dk_ref,
    dv_ref,
    qd_out,
    qd_in,
    st_out,
    st_in,
    kv_in,
    kt_in,
    dk_acc,
    dv_acc,
    dq_out,
    dq_in,
    dkv_out,
    dkv_in,
    qd_ssem,
    qd_rsem,
    st_ssem,
    st_rsem,
    kv_ssem,
    kv_rsem,
    dq_ssem,
    dq_rsem,
    dkv_ssem,
    dkv_rsem,
    o_in,
    lse_in,
    in_sem,
):
    row = lax.axis_index("row")
    col = lax.axis_index("col")
    zone = (col // 8) * 2 + lax.rem(col, 2)
    lane = lax.rem(col, 8) // 2
    other = 1 - row
    dim = k_ref.shape[1]
    scaling = dim ** (-0.5)
    MESH = pl.DeviceIdType.MESH

    def at(r, z, m):
        return (r, (z // 2) * 8 + m * 2 + lax.rem(z, 2))

    loads = []
    for h in range(head_total):
        cols = pl.ds(h * dim, dim)
        loads.append(pltpu.make_async_copy(q_ref.at[:, cols], qd_out.at[h, 0], in_sem.at[2 * h]))
        loads.append(pltpu.make_async_copy(g_ref.at[:, cols], qd_out.at[h, 1], in_sem.at[2 * h + 1]))
    key_loads = [
        pltpu.make_async_copy(k_ref, kv_in.at[lane, 0], in_sem.at[4]),
        pltpu.make_async_copy(v_ref, kv_in.at[lane, 1], in_sem.at[5]),
    ]
    row_loads = [
        pltpu.make_async_copy(o_ref, o_in, in_sem.at[6]),
        pltpu.make_async_copy(lse_ref, lse_in, in_sem.at[7]),
    ]
    for load in loads + key_loads + row_loads:
        load.start()

    mates = [at(row, zone, flip(lane, j)) for j in (1, 2, 3)]
    owners = [at(other, zone, lane)]
    for s in (1, 2, 3):
        owners += [at(r, flip(zone, s), lane) for r in range(head_total)]
    barrier = pltpu.get_barrier_semaphore()
    for peer in mates + owners:
        pl.semaphore_signal(barrier, inc=1, device_id=peer, device_id_type=MESH)

    def kv_copy(j, slot):
        return pltpu.make_async_remote_copy(
            src_ref=kv_in.at[lane],
            dst_ref=kv_in.at[slot],
            send_sem=kv_ssem.at[j],
            recv_sem=kv_rsem.at[slot],
            device_id=at(row, zone, flip(lane, j)),
            device_id_type=MESH,
        )

    def st_copy(s, r, slot_zone, slot_row):
        return pltpu.make_async_remote_copy(
            src_ref=st_out.at[r],
            dst_ref=st_in.at[slot_zone, slot_row],
            send_sem=st_ssem.at[s, r],
            recv_sem=st_rsem.at[slot_zone, slot_row],
            device_id=at(r, flip(zone, s), lane),
            device_id_type=MESH,
        )

    def qd_copy(s, r, slot_zone, slot_row):
        return pltpu.make_async_remote_copy(
            src_ref=qd_out.at[r],
            dst_ref=qd_in.at[slot_zone, :, slot_row],
            send_sem=qd_ssem.at[s, r],
            recv_sem=qd_rsem.at[slot_zone, slot_row],
            device_id=at(r, flip(zone, s), lane),
            device_id_type=MESH,
        )

    def pass_copy(s, r, slot_zone):
        return pltpu.make_async_remote_copy(
            src_ref=qd_in.at[slot_zone, :, r],
            dst_ref=qd_in.at[slot_zone, :, r],
            send_sem=qd_ssem.at[s + 1, r],
            recv_sem=qd_rsem.at[slot_zone, r],
            device_id=at(row, flip(zone, 1), lane),
            device_id_type=MESH,
        )

    def rows_of(s):
        return [other] if s == 0 else list(range(head_total))

    sends = []

    def launch(copy):
        copy.start()
        sends.append(copy)

    for load in loads:
        load.wait()
    pl.semaphore_wait(barrier, len(mates) + len(owners))
    for s in (2, 0):
        for r in rows_of(s):
            launch(qd_copy(s, r, zone, row))
    for load in key_loads:
        load.wait()
    for j in (1, 2, 3):
        launch(kv_copy(j, lane))
    qd_in[zone, 0, row] = qd_out[row, 0]
    qd_in[zone, 1, row] = qd_out[row, 1]
    launch(pass_copy(0, row, zone))

    for load in row_loads:
        load.wait()
    for h in range(head_total):
        cols = slice(h * dim, (h + 1) * dim)
        product = qd_out[h, 1].astype(jnp.float32) * o_in[:, cols].astype(jnp.float32)
        delta = lax.dot_general(
            jnp.ones((8, dim), jnp.float32),
            product,
            (((1,), (1,)), ((), ())),
            precision=lax.Precision.HIGHEST,
            preferred_element_type=jnp.float32,
        )
        lse_rows = jnp.broadcast_to(lse_in[h : h + 1, :] * LOG2E, delta.shape)
        upper = lax.broadcasted_iota(jnp.int32, delta.shape, 0) < 4
        st_out[h] = jnp.where(upper, lse_rows, delta)
    st_in[zone, row] = st_out[row]
    for s in (2, 0, 3, 1):
        for r in rows_of(s):
            launch(st_copy(s, r, zone, row))

    def dq_copy(s, r, slot_row, slot_zone):
        there = flip(zone, s)
        return pltpu.make_async_remote_copy(
            src_ref=dq_out.at[there, r],
            dst_ref=dq_in.at[slot_row, slot_zone],
            send_sem=dq_ssem.at[s, r],
            recv_sem=dq_rsem.at[slot_row, slot_zone],
            device_id=at(r, there, lane),
            device_id_type=MESH,
        )

    def dkv_copy(j, slot):
        there = flip(lane, j)
        return pltpu.make_async_remote_copy(
            src_ref=dkv_out.at[there],
            dst_ref=dkv_in.at[slot],
            send_sem=dkv_ssem.at[j],
            recv_sem=dkv_rsem.at[slot],
            device_id=at(row, zone, there),
            device_id_type=MESH,
        )

    steps = (0, 1, 2, 3)
    for s in steps:
        there = flip(zone, s)
        for r in rows_of(s):
            qd_copy(s, r, there, r).wait_recv()
            if s in (0, 2):
                launch(pass_copy(s, r, there))
        for r in rows_of(s):
            st_copy(s, r, there, r).wait_recv()
        rows2 = head_total * q_ref.shape[0]
        query = qd_in[there, 0].reshape(rows2, dim)
        grad = qd_in[there, 1].reshape(rows2, dim)
        lse_row = jnp.concatenate([st_in[there, r, 0:1, :] for r in range(head_total)], axis=1)
        delta_row = jnp.concatenate([st_in[there, r, 4:5, :] for r in range(head_total)], axis=1)
        query_sum = None
        order = (0, 1, 2, 3) if s < 3 else (2, 3, 1, 0)
        for j in order:
            slot = flip(lane, j)
            if s == 0:
                if j > 0:
                    kv_copy(j, slot).wait_recv()
                kt_in[slot] = kv_in[slot, 0].T
            key = kv_in[slot, 0]
            value = kv_in[slot, 1]
            dims = (((1,), (1,)), ((), ()))
            scores = lax.dot_general(key, query, dims, preferred_element_type=jnp.float32)
            grad_probs = lax.dot_general(value, grad, dims, preferred_element_type=jnp.float32)
            probs = jnp.exp2(scores * (scaling * LOG2E) - lse_row)
            probs_low = probs.astype(jnp.bfloat16)
            grad_scores = (probs * (grad_probs - delta_row)).astype(jnp.bfloat16)
            value_term = jnp.dot(probs_low, grad, preferred_element_type=jnp.float32)
            key_term = jnp.dot(grad_scores, query, preferred_element_type=jnp.float32)
            query_term = jnp.dot(kt_in[slot], grad_scores, preferred_element_type=jnp.float32)
            query_sum = query_term if query_sum is None else query_sum + query_term
            if s > 0:
                key_term = dk_acc[slot] + key_term
                value_term = dv_acc[slot] + value_term
            if s == 3 and j > 0:
                dkv_out[slot, 0] = key_term.astype(jnp.bfloat16)
                dkv_out[slot, 1] = value_term.astype(jnp.bfloat16)
                launch(dkv_copy(j, lane))
            else:
                dk_acc[slot] = key_term
                dv_acc[slot] = value_term
        query_low = query_sum.astype(jnp.bfloat16)
        block = q_ref.shape[0]
        for r in range(head_total):
            dq_out[there, r] = query_low[:, r * block : (r + 1) * block]
        if s == 0:
            dq_in[row, zone] = dq_out[zone, row]
        for r in rows_of(s):
            launch(dq_copy(s, r, row, zone))

    for s in steps:
        for r in rows_of(s):
            dq_copy(s, r, r, flip(zone, s)).wait_recv()
    for h in range(head_total):
        total = dq_in[h, 0].astype(jnp.float32)
        for z in range(1, 4):
            total = total + dq_in[h, z].astype(jnp.float32)
        dq_ref[:, h * dim : (h + 1) * dim] = (total * scaling).T.astype(jnp.bfloat16)

    key_sum = dk_acc[lane]
    value_sum = dv_acc[lane]
    for j in (1, 2, 3):
        slot = flip(lane, j)
        dkv_copy(j, slot).wait_recv()
        key_sum = key_sum + dkv_in[slot, 0].astype(jnp.float32)
        value_sum = value_sum + dkv_in[slot, 1].astype(jnp.float32)
    dk_ref[...] = (key_sum * scaling).astype(jnp.bfloat16)
    dv_ref[...] = value_sum.astype(jnp.bfloat16)
    for copy in sends:
        copy.wait_send()


def fused_device(queries, keys, values, outputs, d_out, lse):
    head_total = lse.shape[0]
    block = queries.shape[0]
    key_rows, dim = keys.shape
    zones, lanes = 4, 4
    bf16, f32 = jnp.bfloat16, jnp.float32
    dma = pltpu.SemaphoreType.DMA
    vmem = pl.BlockSpec(memory_space=pltpu.VMEM)
    pairs = head_total * block * zones * key_rows * lanes
    return pl.pallas_call(
        functools.partial(fused_kernel, head_total),
        out_shape=(
            jax.ShapeDtypeStruct(queries.shape, bf16),
            jax.ShapeDtypeStruct(keys.shape, bf16),
            jax.ShapeDtypeStruct(values.shape, bf16),
        ),
        in_specs=[pl.BlockSpec(memory_space=pltpu.HBM)] * 6,
        out_specs=(vmem, vmem, vmem),
        scratch_shapes=[
            pltpu.VMEM((head_total, 2, block, dim), bf16),
            pltpu.VMEM((zones, 2, head_total, block, dim), bf16),
            pltpu.VMEM((head_total, 8, block), f32),
            pltpu.VMEM((zones, head_total, 8, block), f32),
            pltpu.VMEM((lanes, 2, key_rows, dim), bf16),
            pltpu.VMEM((lanes, dim, key_rows), bf16),
            pltpu.VMEM((lanes, key_rows, dim), f32),
            pltpu.VMEM((lanes, key_rows, dim), f32),
            pltpu.VMEM((zones, head_total, dim, block), bf16),
            pltpu.VMEM((head_total, zones, dim, block), bf16),
            pltpu.VMEM((lanes, 2, key_rows, dim), bf16),
            pltpu.VMEM((lanes, 2, key_rows, dim), bf16),
            dma((zones, head_total)),
            dma((zones, head_total)),
            dma((zones, head_total)),
            dma((zones, head_total)),
            dma((lanes,)),
            dma((lanes,)),
            dma((zones, head_total)),
            dma((head_total, zones)),
            dma((lanes,)),
            dma((lanes,)),
            pltpu.VMEM(outputs.shape, bf16),
            pltpu.VMEM(lse.shape, f32),
            dma((8,)),
        ],
        compiler_params=pltpu.CompilerParams(
            collective_id=0, has_side_effects=True, vmem_limit_bytes=63 * 1024 * 1024
        ),
        cost_estimate=pl.CostEstimate(
            flops=10 * pairs * dim, bytes_accessed=9 * block * 2 * dim * 2, transcendentals=pairs
        ),
    )(queries, keys, values, outputs, d_out, lse)


def solution(mesh):
    placed = (
        P(("row", "col"), None),
        P("col", "row"),
        P("col", "row"),
        P(("row", "col"), None),
        P(("row", "col"), None),
        P(None, ("row", "col")),
    )
    fused = mesh.shape["row"] == 2 and mesh.shape["col"] == 16

    def local(queries, keys, values, outputs, d_out, lse):
        head_dim = queries.shape[1] // lse.shape[0]
        fits = lse.shape[0] == mesh.shape["row"] and head_dim == 128 and queries.shape[0] == 128
        chosen = fused_device if fused and fits else per_device
        return chosen(queries, keys, values, outputs, d_out, lse)

    return jax.shard_map(
        local,
        mesh=mesh,
        in_specs=placed,
        out_specs=(P(("row", "col"), None), P("col", "row"), P("col", "row")),
        check_vma=False,
    )
```

```python
import functools

import jax
import jax.numpy as jnp
from jax import lax
from jax.experimental import pallas as pl
from jax.experimental.pallas import tpu as pltpu
from jax.sharding import PartitionSpec as P


def block_size(row_total):
    block_rows = row_total
    while block_rows > 512 and block_rows % 2 == 0:
        block_rows = block_rows // 2
    return block_rows


def head_slice(matrix, head_index, head_dim):
    return matrix[:, head_index * head_dim : (head_index + 1) * head_dim]


def contract_rows(left, right):
    return lax.dot_general(
        left, right, (((0,), (0,)), ((), ())), preferred_element_type=jnp.float32
    )


def score_terms(query_head, grad_head, lse_row, delta_row, key_head, value_head, scaling):
    scores = jnp.dot(query_head, key_head.T, preferred_element_type=jnp.float32)
    probs = jnp.exp(scores * scaling - lse_row[:, None])
    probs_low = probs.astype(jnp.bfloat16)
    grad_probs = jnp.dot(grad_head, value_head.T, preferred_element_type=jnp.float32)
    grad_scores = (probs * (grad_probs - delta_row[:, None])).astype(jnp.bfloat16)
    return (probs_low, grad_scores)


def block_grads(query_rows, grad_rows, lse_rows, delta_rows, key_all, value_all, head_dim):
    head_total = lse_rows.shape[0]
    scaling = head_dim ** (-0.5)
    key_terms = []
    value_terms = []
    for head_index in range(head_total):
        query_head = head_slice(query_rows, head_index, head_dim)
        grad_head = head_slice(grad_rows, head_index, head_dim)
        key_head = head_slice(key_all, head_index, head_dim)
        value_head = head_slice(value_all, head_index, head_dim)
        probs_low, grad_scores = score_terms(
            query_head,
            grad_head,
            lse_rows[head_index],
            delta_rows[head_index],
            key_head,
            value_head,
            scaling,
        )
        value_terms.append(contract_rows(probs_low, grad_head))
        key_terms.append(contract_rows(grad_scores, query_head))
    key_term = jnp.concatenate(key_terms, axis=1)
    value_term = jnp.concatenate(value_terms, axis=1)
    query_term = None
    return (key_term, value_term, query_term)


def split_blocks(query_all, grad_all, lse_all, delta_all):
    row_total, features = query_all.shape
    block_rows = block_size(row_total)
    steps_total = row_total // block_rows
    head_total = lse_all.shape[0]
    query_blocks = query_all.reshape(steps_total, block_rows, features)
    grad_blocks = grad_all.reshape(steps_total, block_rows, features)
    lse_blocks = lse_all.reshape(head_total, steps_total, block_rows).transpose(1, 0, 2)
    delta_blocks = delta_all.reshape(head_total, steps_total, block_rows).transpose(1, 0, 2)
    return (query_blocks, grad_blocks, lse_blocks, delta_blocks)


def query_pass(query_all, grad_all, lse_all, delta_all, key_all, value_all, head_dim):
    row_total, features = query_all.shape
    block_inputs = split_blocks(query_all, grad_all, lse_all, delta_all)
    empty_sums = jnp.zeros((key_all.shape[0], features), jnp.float32)

    def advance(running, inputs):
        key_sum, value_sum = running
        query_rows, grad_rows, lse_rows, delta_rows = inputs
        key_term, value_term, query_term = block_grads(
            query_rows, grad_rows, lse_rows, delta_rows, key_all, value_all, head_dim
        )
        return ((key_sum + key_term, value_sum + value_term), query_term)

    (key_sum, value_sum), query_terms = lax.scan(advance, (empty_sums, empty_sums), block_inputs)
    return (key_sum, value_sum, query_terms)


def query_only(query_rows, grad_rows, lse_rows, delta_rows, key_all, value_all, head_dim):
    row_total, features = query_rows.shape
    head_total = lse_rows.shape[0]
    scaling = head_dim ** (-0.5)
    block_inputs = split_blocks(query_rows, grad_rows, lse_rows, delta_rows)

    def one_block(inputs):
        query_part, grad_part, lse_part, delta_part = inputs
        pieces = []
        for head_index in range(head_total):
            query_head = head_slice(query_part, head_index, head_dim)
            grad_head = head_slice(grad_part, head_index, head_dim)
            key_head = head_slice(key_all, head_index, head_dim)
            value_head = head_slice(value_all, head_index, head_dim)
            probs_low, grad_scores = score_terms(
                query_head,
                grad_head,
                lse_part[head_index],
                delta_part[head_index],
                key_head,
                value_head,
                scaling,
            )
            pieces.append(jnp.dot(grad_scores, key_head, preferred_element_type=jnp.float32))
        return jnp.concatenate(pieces, axis=1)

    return lax.map(one_block, block_inputs).reshape(row_total, features)


def head_delta(d_out, outputs, head_total, head_dim):
    product = d_out.astype(jnp.float32) * outputs.astype(jnp.float32)
    return jnp.sum(product.reshape(product.shape[0], head_total, head_dim), axis=2).T


def per_device(queries, keys, values, outputs, d_out, lse):
    head_total = lse.shape[0]
    head_dim = queries.shape[1] // head_total
    scaling = head_dim ** (-0.5)
    delta = head_delta(d_out, outputs, head_total, head_dim)
    key_all, value_all = (
        lax.all_gather(keys, "row", axis=1, tiled=True),
        lax.all_gather(values, "row", axis=1, tiled=True),
    )
    query_all, grad_all = (
        lax.all_gather(queries, "col", axis=0, tiled=True),
        lax.all_gather(d_out, "col", axis=0, tiled=True),
    )
    lse_all, delta_all = (
        lax.all_gather(lse, "col", axis=1, tiled=True),
        lax.all_gather(delta, "col", axis=1, tiled=True),
    )
    key_sum, value_sum, unused_terms = query_pass(
        query_all, grad_all, lse_all, delta_all, key_all, value_all, head_dim
    )

    def query_term(first_row, row_total):
        return query_only(query_all, grad_all, lse_all, delta_all, key_all, value_all, head_dim)

    query_grad = lax.psum_scatter(
        query_term(jnp.int32(0), queries.shape[0] * lax.axis_size("col")),
        "col",
        scatter_dimension=0,
        tiled=True,
    )
    key_grad, value_grad = (
        lax.psum_scatter(key_sum, "row", scatter_dimension=1, tiled=True),
        lax.psum_scatter(value_sum, "row", scatter_dimension=1, tiled=True),
    )
    d_queries = (query_grad * scaling).astype(jnp.bfloat16)
    d_keys = (key_grad * scaling).astype(jnp.bfloat16)
    d_values = value_grad.astype(jnp.bfloat16)
    return (d_queries, d_keys, d_values)

LOG2E = 1.4426950408889634


def flip(index, bits):
    if bits == 1:
        return index + 1 - 2 * lax.rem(index, 2)
    if bits == 2:
        return lax.rem(index + 2, 4)
    if bits == 3:
        return 3 - index
    return index


def fused_kernel(
    head_total,
    q_ref,
    k_ref,
    v_ref,
    o_ref,
    g_ref,
    lse_ref,
    dq_ref,
    dk_ref,
    dv_ref,
    qd_out,
    qd_in,
    st_out,
    st_in,
    kv_in,
    kt_in,
    dk_acc,
    dv_acc,
    dq_out,
    dq_in,
    dkv_out,
    dkv_in,
    qd_ssem,
    qd_rsem,
    st_ssem,
    st_rsem,
    kv_ssem,
    kv_rsem,
    dq_ssem,
    dq_rsem,
    dkv_ssem,
    dkv_rsem,
    o_in,
    lse_in,
    in_sem,
    relay_ssem,
):
    row = lax.axis_index("row")
    col = lax.axis_index("col")
    zone = col // 4
    lane = lax.rem(col, 4)
    inner = lax.rem(zone + 1, 4) // 2 == 1
    other = 1 - row
    dim = k_ref.shape[1]
    scaling = dim ** (-0.5)
    MESH = pl.DeviceIdType.MESH

    def at(r, z, m):
        return (r, z * 4 + m)

    loads = []
    for h in range(head_total):
        cols = pl.ds(h * dim, dim)
        loads.append(pltpu.make_async_copy(q_ref.at[:, cols], qd_out.at[h, 0], in_sem.at[2 * h]))
        loads.append(pltpu.make_async_copy(g_ref.at[:, cols], qd_out.at[h, 1], in_sem.at[2 * h + 1]))
    key_loads = [
        pltpu.make_async_copy(k_ref, kv_in.at[lane, 0], in_sem.at[4]),
        pltpu.make_async_copy(v_ref, kv_in.at[lane, 1], in_sem.at[5]),
    ]
    row_loads = [
        pltpu.make_async_copy(o_ref, o_in, in_sem.at[6]),
        pltpu.make_async_copy(lse_ref, lse_in, in_sem.at[7]),
    ]
    for load in loads + key_loads + row_loads:
        load.start()

    mates = [at(row, zone, flip(lane, j)) for j in (1, 2, 3)]
    owners = [at(other, zone, lane)]
    for s in (1, 2, 3):
        owners += [at(r, flip(zone, s), lane) for r in range(head_total)]
    barrier = pltpu.get_barrier_semaphore()
    for peer in mates + owners:
        pl.semaphore_signal(barrier, inc=1, device_id=peer, device_id_type=MESH)

    def kv_copy(j, slot):
        return pltpu.make_async_remote_copy(
            src_ref=kv_in.at[lane],
            dst_ref=kv_in.at[slot],
            send_sem=kv_ssem.at[j],
            recv_sem=kv_rsem.at[slot],
            device_id=at(row, zone, flip(lane, j)),
            device_id_type=MESH,
        )

    def st_copy(s, r, slot_zone, slot_row):
        return pltpu.make_async_remote_copy(
            src_ref=st_out.at[r],
            dst_ref=st_in.at[slot_zone, slot_row],
            send_sem=st_ssem.at[s, r],
            recv_sem=st_rsem.at[slot_zone, slot_row],
            device_id=at(r, flip(zone, s), lane),
            device_id_type=MESH,
        )

    def qd_copy(s, r, slot_zone, slot_row):
        return pltpu.make_async_remote_copy(
            src_ref=qd_out.at[r],
            dst_ref=qd_in.at[slot_zone, :, slot_row],
            send_sem=qd_ssem.at[s, r],
            recv_sem=qd_rsem.at[slot_zone, slot_row],
            device_id=at(r, flip(zone, s), lane),
            device_id_type=MESH,
        )

    def relay_copy(r):
        slot_zone = flip(zone, 2)
        return pltpu.make_async_remote_copy(
            src_ref=qd_in.at[slot_zone, :, r],
            dst_ref=qd_in.at[slot_zone, :, r],
            send_sem=relay_ssem.at[r],
            recv_sem=qd_rsem.at[slot_zone, r],
            device_id=at(row, flip(zone, 1), lane),
            device_id_type=MESH,
        )

    def rows_of(s):
        return [other] if s == 0 else list(range(head_total))

    sends = []

    def launch(copy):
        copy.start()
        sends.append(copy)

    for load in loads:
        load.wait()
    pl.semaphore_wait(barrier, len(mates) + len(owners))
    for r in rows_of(2):
        launch(qd_copy(2, r, zone, row))

    @pl.when(inner)
    def _():
        for r in rows_of(3):
            qd_copy(3, r, zone, row).start()

    for load in key_loads:
        load.wait()
    for j in (2, 3, 1):
        launch(kv_copy(j, lane))
    for s in (0, 1):
        for r in rows_of(s):
            launch(qd_copy(s, r, zone, row))
    qd_in[zone, 0, row] = qd_out[row, 0]
    qd_in[zone, 1, row] = qd_out[row, 1]

    for load in row_loads:
        load.wait()
    for h in range(head_total):
        cols = slice(h * dim, (h + 1) * dim)
        product = qd_out[h, 1].astype(jnp.float32) * o_in[:, cols].astype(jnp.float32)
        delta = lax.dot_general(
            jnp.ones((8, dim), jnp.float32),
            product,
            (((1,), (1,)), ((), ())),
            precision=lax.Precision.HIGHEST,
            preferred_element_type=jnp.float32,
        )
        lse_rows = jnp.broadcast_to(lse_in[h : h + 1, :] * LOG2E, delta.shape)
        upper = lax.broadcasted_iota(jnp.int32, delta.shape, 0) < 4
        st_out[h] = jnp.where(upper, lse_rows, delta)
    st_in[zone, row] = st_out[row]
    for s in (2, 0, 3, 1):
        for r in rows_of(s):
            launch(st_copy(s, r, zone, row))

    def dq_copy(s, r, slot_row, slot_zone):
        there = flip(zone, s)
        return pltpu.make_async_remote_copy(
            src_ref=dq_out.at[there, r],
            dst_ref=dq_in.at[slot_row, slot_zone],
            send_sem=dq_ssem.at[s, r],
            recv_sem=dq_rsem.at[slot_row, slot_zone],
            device_id=at(r, there, lane),
            device_id_type=MESH,
        )

    def dkv_copy(j, slot):
        there = flip(lane, j)
        return pltpu.make_async_remote_copy(
            src_ref=dkv_out.at[there],
            dst_ref=dkv_in.at[slot],
            send_sem=dkv_ssem.at[j],
            recv_sem=dkv_rsem.at[slot],
            device_id=at(row, zone, there),
            device_id_type=MESH,
        )

    steps = (0, 2, 1, 3)
    for s in steps:
        there = flip(zone, s)
        for r in rows_of(s):
            qd_copy(s, r, there, r).wait_recv()
        if s == 2:

            @pl.when(inner)
            def _():
                for r in rows_of(2):
                    relay_copy(r).start()

        for r in rows_of(s):
            st_copy(s, r, there, r).wait_recv()
        rows2 = head_total * q_ref.shape[0]
        query = qd_in[there, 0].reshape(rows2, dim)
        grad = qd_in[there, 1].reshape(rows2, dim)
        lse_row = jnp.concatenate([st_in[there, r, 0:1, :] for r in range(head_total)], axis=1)
        delta_row = jnp.concatenate([st_in[there, r, 4:5, :] for r in range(head_total)], axis=1)
        query_sum = None
        order = (0, 1, 2, 3) if s < 3 else (2, 3, 1, 0)
        for j in order:
            slot = flip(lane, j)
            if s == 0:
                if j > 0:
                    kv_copy(j, slot).wait_recv()
                kt_in[slot] = kv_in[slot, 0].T
            key = kv_in[slot, 0]
            value = kv_in[slot, 1]
            dims = (((1,), (1,)), ((), ()))
            scores = lax.dot_general(key, query, dims, preferred_element_type=jnp.float32)
            grad_probs = lax.dot_general(value, grad, dims, preferred_element_type=jnp.float32)
            probs = jnp.exp2(scores * (scaling * LOG2E) - lse_row)
            probs_low = probs.astype(jnp.bfloat16)
            grad_scores = (probs * (grad_probs - delta_row)).astype(jnp.bfloat16)
            value_term = jnp.dot(probs_low, grad, preferred_element_type=jnp.float32)
            key_term = jnp.dot(grad_scores, query, preferred_element_type=jnp.float32)
            query_term = jnp.dot(kt_in[slot], grad_scores, preferred_element_type=jnp.float32)
            query_sum = query_term if query_sum is None else query_sum + query_term
            if s > 0:
                key_term = dk_acc[slot] + key_term
                value_term = dv_acc[slot] + value_term
            if s == 3 and j > 0:
                dkv_out[slot, 0] = key_term.astype(jnp.bfloat16)
                dkv_out[slot, 1] = value_term.astype(jnp.bfloat16)
                launch(dkv_copy(j, lane))
            else:
                dk_acc[slot] = key_term
                dv_acc[slot] = value_term
        query_low = query_sum.astype(jnp.bfloat16)
        block = q_ref.shape[0]
        for r in range(head_total):
            dq_out[there, r] = query_low[:, r * block : (r + 1) * block]
        if s == 0:
            dq_in[row, zone] = dq_out[zone, row]
        for r in rows_of(s):
            launch(dq_copy(s, r, row, zone))

    for s in steps:
        for r in rows_of(s):
            dq_copy(s, r, r, flip(zone, s)).wait_recv()
    for h in range(head_total):
        total = dq_in[h, 0].astype(jnp.float32)
        for z in range(1, 4):
            total = total + dq_in[h, z].astype(jnp.float32)
        dq_ref[:, h * dim : (h + 1) * dim] = (total * scaling).T.astype(jnp.bfloat16)

    key_sum = dk_acc[lane]
    value_sum = dv_acc[lane]
    for j in (1, 2, 3):
        slot = flip(lane, j)
        dkv_copy(j, slot).wait_recv()
        key_sum = key_sum + dkv_in[slot, 0].astype(jnp.float32)
        value_sum = value_sum + dkv_in[slot, 1].astype(jnp.float32)
    dk_ref[...] = (key_sum * scaling).astype(jnp.bfloat16)
    dv_ref[...] = value_sum.astype(jnp.bfloat16)
    for copy in sends:
        copy.wait_send()

    @pl.when(inner)
    def _():
        for r in rows_of(3):
            qd_copy(3, r, zone, row).wait_send()
            relay_copy(r).wait_send()


def write_kernel(dq_ref, dk_ref, dv_ref, dq_out, dk_out, dv_out, sems):
    pairs = ((dq_ref, dq_out), (dk_ref, dk_out), (dv_ref, dv_out))
    copies = [pltpu.make_async_copy(src, dst, sems.at[i]) for i, (src, dst) in enumerate(pairs)]
    for copy in copies:
        copy.start()
    for copy in copies:
        copy.wait()


def fused_device(queries, keys, values, outputs, d_out, lse):
    head_total = lse.shape[0]
    block = queries.shape[0]
    key_rows, dim = keys.shape
    zones, lanes = 4, 4
    bf16, f32 = jnp.bfloat16, jnp.float32
    dma = pltpu.SemaphoreType.DMA
    vmem = pl.BlockSpec(memory_space=pltpu.VMEM)
    pairs = head_total * block * zones * key_rows * lanes
    hbm = pl.BlockSpec(memory_space=pltpu.HBM)
    results = pl.pallas_call(
        functools.partial(fused_kernel, head_total),
        out_shape=(
            jax.ShapeDtypeStruct(queries.shape, bf16),
            jax.ShapeDtypeStruct(keys.shape, bf16),
            jax.ShapeDtypeStruct(values.shape, bf16),
        ),
        in_specs=[hbm] * 6,
        out_specs=(vmem, vmem, vmem),
        scratch_shapes=[
            pltpu.VMEM((head_total, 2, block, dim), bf16),
            pltpu.VMEM((zones, 2, head_total, block, dim), bf16),
            pltpu.VMEM((head_total, 8, block), f32),
            pltpu.VMEM((zones, head_total, 8, block), f32),
            pltpu.VMEM((lanes, 2, key_rows, dim), bf16),
            pltpu.VMEM((lanes, dim, key_rows), bf16),
            pltpu.VMEM((lanes, key_rows, dim), f32),
            pltpu.VMEM((lanes, key_rows, dim), f32),
            pltpu.VMEM((zones, head_total, dim, block), bf16),
            pltpu.VMEM((head_total, zones, dim, block), bf16),
            pltpu.VMEM((lanes, 2, key_rows, dim), bf16),
            pltpu.VMEM((lanes, 2, key_rows, dim), bf16),
            dma((zones, head_total)),
            dma((zones, head_total)),
            dma((zones, head_total)),
            dma((zones, head_total)),
            dma((lanes,)),
            dma((lanes,)),
            dma((zones, head_total)),
            dma((head_total, zones)),
            dma((lanes,)),
            dma((lanes,)),
            pltpu.VMEM(outputs.shape, bf16),
            pltpu.VMEM(lse.shape, f32),
            dma((8,)),
            dma((head_total,)),
        ],
        compiler_params=pltpu.CompilerParams(
            collective_id=0, has_side_effects=True, vmem_limit_bytes=63 * 1024 * 1024
        ),
        cost_estimate=pl.CostEstimate(
            flops=10 * pairs * dim, bytes_accessed=9 * block * 2 * dim * 2, transcendentals=pairs
        ),
    )(queries, keys, values, outputs, d_out, lse)
    return pl.pallas_call(
        write_kernel,
        out_shape=tuple(jax.ShapeDtypeStruct(x.shape, x.dtype) for x in results),
        in_specs=[hbm] * 3,
        out_specs=(hbm, hbm, hbm),
        scratch_shapes=[dma((3,))],
        compiler_params=pltpu.CompilerParams(vmem_limit_bytes=63 * 1024 * 1024),
    )(*results)


def solution(mesh):
    placed = (
        P(("row", "col"), None),
        P("col", "row"),
        P("col", "row"),
        P(("row", "col"), None),
        P(("row", "col"), None),
        P(None, ("row", "col")),
    )
    fused = mesh.shape["row"] == 2 and mesh.shape["col"] == 16

    def local(queries, keys, values, outputs, d_out, lse):
        head_dim = queries.shape[1] // lse.shape[0]
        fits = lse.shape[0] == mesh.shape["row"] and head_dim == 128 and queries.shape[0] == 128
        chosen = fused_device if fused and fits else per_device
        return chosen(queries, keys, values, outputs, d_out, lse)

    return jax.shard_map(
        local,
        mesh=mesh,
        in_specs=placed,
        out_specs=(P(("row", "col"), None), P("col", "row"), P("col", "row")),
        check_vma=False,
    )
```

```python
import functools

import jax
import jax.numpy as jnp
from jax import lax
from jax.experimental import pallas as pl
from jax.experimental.pallas import tpu as pltpu
from jax.sharding import PartitionSpec as P


def block_size(row_total):
    block_rows = row_total
    while block_rows > 512 and block_rows % 2 == 0:
        block_rows = block_rows // 2
    return block_rows


def head_slice(matrix, head_index, head_dim):
    return matrix[:, head_index * head_dim : (head_index + 1) * head_dim]


def contract_rows(left, right):
    return lax.dot_general(
        left, right, (((0,), (0,)), ((), ())), preferred_element_type=jnp.float32
    )


def score_terms(query_head, grad_head, lse_row, delta_row, key_head, value_head, scaling):
    scores = jnp.dot(query_head, key_head.T, preferred_element_type=jnp.float32)
    probs = jnp.exp(scores * scaling - lse_row[:, None])
    probs_low = probs.astype(jnp.bfloat16)
    grad_probs = jnp.dot(grad_head, value_head.T, preferred_element_type=jnp.float32)
    grad_scores = (probs * (grad_probs - delta_row[:, None])).astype(jnp.bfloat16)
    return (probs_low, grad_scores)


def block_grads(query_rows, grad_rows, lse_rows, delta_rows, key_all, value_all, head_dim):
    head_total = lse_rows.shape[0]
    scaling = head_dim ** (-0.5)
    key_terms = []
    value_terms = []
    for head_index in range(head_total):
        query_head = head_slice(query_rows, head_index, head_dim)
        grad_head = head_slice(grad_rows, head_index, head_dim)
        key_head = head_slice(key_all, head_index, head_dim)
        value_head = head_slice(value_all, head_index, head_dim)
        probs_low, grad_scores = score_terms(
            query_head,
            grad_head,
            lse_rows[head_index],
            delta_rows[head_index],
            key_head,
            value_head,
            scaling,
        )
        value_terms.append(contract_rows(probs_low, grad_head))
        key_terms.append(contract_rows(grad_scores, query_head))
    key_term = jnp.concatenate(key_terms, axis=1)
    value_term = jnp.concatenate(value_terms, axis=1)
    query_term = None
    return (key_term, value_term, query_term)


def split_blocks(query_all, grad_all, lse_all, delta_all):
    row_total, features = query_all.shape
    block_rows = block_size(row_total)
    steps_total = row_total // block_rows
    head_total = lse_all.shape[0]
    query_blocks = query_all.reshape(steps_total, block_rows, features)
    grad_blocks = grad_all.reshape(steps_total, block_rows, features)
    lse_blocks = lse_all.reshape(head_total, steps_total, block_rows).transpose(1, 0, 2)
    delta_blocks = delta_all.reshape(head_total, steps_total, block_rows).transpose(1, 0, 2)
    return (query_blocks, grad_blocks, lse_blocks, delta_blocks)


def query_pass(query_all, grad_all, lse_all, delta_all, key_all, value_all, head_dim):
    row_total, features = query_all.shape
    block_inputs = split_blocks(query_all, grad_all, lse_all, delta_all)
    empty_sums = jnp.zeros((key_all.shape[0], features), jnp.float32)

    def advance(running, inputs):
        key_sum, value_sum = running
        query_rows, grad_rows, lse_rows, delta_rows = inputs
        key_term, value_term, query_term = block_grads(
            query_rows, grad_rows, lse_rows, delta_rows, key_all, value_all, head_dim
        )
        return ((key_sum + key_term, value_sum + value_term), query_term)

    (key_sum, value_sum), query_terms = lax.scan(advance, (empty_sums, empty_sums), block_inputs)
    return (key_sum, value_sum, query_terms)


def query_only(query_rows, grad_rows, lse_rows, delta_rows, key_all, value_all, head_dim):
    row_total, features = query_rows.shape
    head_total = lse_rows.shape[0]
    scaling = head_dim ** (-0.5)
    block_inputs = split_blocks(query_rows, grad_rows, lse_rows, delta_rows)

    def one_block(inputs):
        query_part, grad_part, lse_part, delta_part = inputs
        pieces = []
        for head_index in range(head_total):
            query_head = head_slice(query_part, head_index, head_dim)
            grad_head = head_slice(grad_part, head_index, head_dim)
            key_head = head_slice(key_all, head_index, head_dim)
            value_head = head_slice(value_all, head_index, head_dim)
            probs_low, grad_scores = score_terms(
                query_head,
                grad_head,
                lse_part[head_index],
                delta_part[head_index],
                key_head,
                value_head,
                scaling,
            )
            pieces.append(jnp.dot(grad_scores, key_head, preferred_element_type=jnp.float32))
        return jnp.concatenate(pieces, axis=1)

    return lax.map(one_block, block_inputs).reshape(row_total, features)


def head_delta(d_out, outputs, head_total, head_dim):
    product = d_out.astype(jnp.float32) * outputs.astype(jnp.float32)
    return jnp.sum(product.reshape(product.shape[0], head_total, head_dim), axis=2).T


def per_device(queries, keys, values, outputs, d_out, lse):
    head_total = lse.shape[0]
    head_dim = queries.shape[1] // head_total
    scaling = head_dim ** (-0.5)
    delta = head_delta(d_out, outputs, head_total, head_dim)
    key_all, value_all = (
        lax.all_gather(keys, "row", axis=1, tiled=True),
        lax.all_gather(values, "row", axis=1, tiled=True),
    )
    query_all, grad_all = (
        lax.all_gather(queries, "col", axis=0, tiled=True),
        lax.all_gather(d_out, "col", axis=0, tiled=True),
    )
    lse_all, delta_all = (
        lax.all_gather(lse, "col", axis=1, tiled=True),
        lax.all_gather(delta, "col", axis=1, tiled=True),
    )
    key_sum, value_sum, unused_terms = query_pass(
        query_all, grad_all, lse_all, delta_all, key_all, value_all, head_dim
    )

    def query_term(first_row, row_total):
        return query_only(query_all, grad_all, lse_all, delta_all, key_all, value_all, head_dim)

    query_grad = lax.psum_scatter(
        query_term(jnp.int32(0), queries.shape[0] * lax.axis_size("col")),
        "col",
        scatter_dimension=0,
        tiled=True,
    )
    key_grad, value_grad = (
        lax.psum_scatter(key_sum, "row", scatter_dimension=1, tiled=True),
        lax.psum_scatter(value_sum, "row", scatter_dimension=1, tiled=True),
    )
    d_queries = (query_grad * scaling).astype(jnp.bfloat16)
    d_keys = (key_grad * scaling).astype(jnp.bfloat16)
    d_values = value_grad.astype(jnp.bfloat16)
    return (d_queries, d_keys, d_values)

LOG2E = 1.4426950408889634


def flip(index, bits):
    if bits == 1:
        return index + 1 - 2 * lax.rem(index, 2)
    if bits == 2:
        return lax.rem(index + 2, 4)
    if bits == 3:
        return 3 - index
    return index


def fused_kernel(
    head_total,
    q_ref,
    k_ref,
    v_ref,
    o_ref,
    g_ref,
    lse_ref,
    dq_ref,
    dk_ref,
    dv_ref,
    qd_out,
    qd_in,
    st_out,
    st_in,
    kv_in,
    kt_in,
    dk_acc,
    dv_acc,
    dq_out,
    dq_in,
    dkv_out,
    dkv_in,
    qd_ssem,
    qd_rsem,
    st_ssem,
    st_rsem,
    kv_ssem,
    kv_rsem,
    dq_ssem,
    dq_rsem,
    dkv_ssem,
    dkv_rsem,
    o_in,
    lse_in,
    in_sem,
    relay_ssem,
):
    row = lax.axis_index("row")
    col = lax.axis_index("col")
    zone = col // 4
    lane = lax.rem(col, 4)
    inner = lax.rem(zone + 1, 4) // 2 == 1
    other = 1 - row
    dim = k_ref.shape[1]
    scaling = dim ** (-0.5)
    MESH = pl.DeviceIdType.MESH

    def at(r, z, m):
        return (r, z * 4 + m)

    loads = []
    for h in range(head_total):
        cols = pl.ds(h * dim, dim)
        loads.append(pltpu.make_async_copy(q_ref.at[:, cols], qd_out.at[h, 0], in_sem.at[2 * h]))
        loads.append(pltpu.make_async_copy(g_ref.at[:, cols], qd_out.at[h, 1], in_sem.at[2 * h + 1]))
    key_loads = [
        pltpu.make_async_copy(k_ref, kv_in.at[lane, 0], in_sem.at[4]),
        pltpu.make_async_copy(v_ref, kv_in.at[lane, 1], in_sem.at[5]),
    ]
    row_loads = [
        pltpu.make_async_copy(o_ref, o_in, in_sem.at[6]),
        pltpu.make_async_copy(lse_ref, lse_in, in_sem.at[7]),
    ]
    for load in loads + key_loads + row_loads:
        load.start()

    mates = [at(row, zone, flip(lane, j)) for j in (1, 2)]
    owners = [at(other, zone, lane)]
    for s in (1, 2, 3):
        owners += [at(r, flip(zone, s), lane) for r in range(head_total)]
    barrier = pltpu.get_barrier_semaphore()
    for peer in mates + owners:
        pl.semaphore_signal(barrier, inc=1, device_id=peer, device_id_type=MESH)

    def kv_copy(j, slot):
        return pltpu.make_async_remote_copy(
            src_ref=kv_in.at[lane],
            dst_ref=kv_in.at[slot],
            send_sem=kv_ssem.at[j],
            recv_sem=kv_rsem.at[slot],
            device_id=at(row, zone, flip(lane, j)),
            device_id_type=MESH,
        )

    def kv_pass():
        slot = flip(lane, 2)
        return pltpu.make_async_remote_copy(
            src_ref=kv_in.at[slot],
            dst_ref=kv_in.at[slot],
            send_sem=kv_ssem.at[3],
            recv_sem=kv_rsem.at[slot],
            device_id=at(row, zone, flip(lane, 1)),
            device_id_type=MESH,
        )

    def st_copy(s, r, slot_zone, slot_row):
        return pltpu.make_async_remote_copy(
            src_ref=st_out.at[r],
            dst_ref=st_in.at[slot_zone, slot_row],
            send_sem=st_ssem.at[s, r],
            recv_sem=st_rsem.at[slot_zone, slot_row],
            device_id=at(r, flip(zone, s), lane),
            device_id_type=MESH,
        )

    def qd_copy(s, r, slot_zone, slot_row):
        return pltpu.make_async_remote_copy(
            src_ref=qd_out.at[r],
            dst_ref=qd_in.at[slot_zone, :, slot_row],
            send_sem=qd_ssem.at[s, r],
            recv_sem=qd_rsem.at[slot_zone, slot_row],
            device_id=at(r, flip(zone, s), lane),
            device_id_type=MESH,
        )

    def relay_copy(r):
        slot_zone = flip(zone, 2)
        return pltpu.make_async_remote_copy(
            src_ref=qd_in.at[slot_zone, :, r],
            dst_ref=qd_in.at[slot_zone, :, r],
            send_sem=relay_ssem.at[r],
            recv_sem=qd_rsem.at[slot_zone, r],
            device_id=at(row, flip(zone, 1), lane),
            device_id_type=MESH,
        )

    def rows_of(s):
        return [other] if s == 0 else list(range(head_total))

    sends = []

    def launch(copy):
        copy.start()
        sends.append(copy)

    for load in loads:
        load.wait()
    pl.semaphore_wait(barrier, len(mates) + len(owners))
    for r in rows_of(2):
        launch(qd_copy(2, r, zone, row))
    for load in key_loads:
        load.wait()
    for j in (2, 1):
        launch(kv_copy(j, lane))
    for s in (0, 1):
        for r in rows_of(s):
            launch(qd_copy(s, r, zone, row))
    qd_in[zone, 0, row] = qd_out[row, 0]
    qd_in[zone, 1, row] = qd_out[row, 1]

    for load in row_loads:
        load.wait()
    for h in range(head_total):
        cols = slice(h * dim, (h + 1) * dim)
        product = qd_out[h, 1].astype(jnp.float32) * o_in[:, cols].astype(jnp.float32)
        delta = lax.dot_general(
            jnp.ones((8, dim), jnp.float32),
            product,
            (((1,), (1,)), ((), ())),
            precision=lax.Precision.HIGHEST,
            preferred_element_type=jnp.float32,
        )
        lse_rows = jnp.broadcast_to(lse_in[h : h + 1, :] * LOG2E, delta.shape)
        upper = lax.broadcasted_iota(jnp.int32, delta.shape, 0) < 4
        st_out[h] = jnp.where(upper, lse_rows, delta)
    st_in[zone, row] = st_out[row]
    for s in (2, 0, 3, 1):
        for r in rows_of(s):
            launch(st_copy(s, r, zone, row))

    def dq_copy(s, r, slot_row, slot_zone):
        there = flip(zone, s)
        return pltpu.make_async_remote_copy(
            src_ref=dq_out.at[there, r],
            dst_ref=dq_in.at[slot_row, slot_zone],
            send_sem=dq_ssem.at[s, r],
            recv_sem=dq_rsem.at[slot_row, slot_zone],
            device_id=at(r, there, lane),
            device_id_type=MESH,
        )

    def dkv_copy(j):
        return pltpu.make_async_remote_copy(
            src_ref=dkv_out.at[j],
            dst_ref=dkv_in.at[j],
            send_sem=dkv_ssem.at[j],
            recv_sem=dkv_rsem.at[j],
            device_id=at(row, zone, flip(lane, 2 if j == 2 else 1)),
            device_id_type=MESH,
        )

    steps = (0, 2, 1, 3)
    for s in steps:
        there = flip(zone, s)
        for r in rows_of(s):
            qd_copy(s, r, there, r).wait_recv()
        if s == 2:

            @pl.when(inner)
            def _():
                for r in rows_of(2):
                    relay_copy(r).start()

        for r in rows_of(s):
            st_copy(s, r, there, r).wait_recv()
        rows2 = head_total * q_ref.shape[0]
        query = qd_in[there, 0].reshape(rows2, dim)
        grad = qd_in[there, 1].reshape(rows2, dim)
        lse_row = jnp.concatenate([st_in[there, r, 0:1, :] for r in range(head_total)], axis=1)
        delta_row = jnp.concatenate([st_in[there, r, 4:5, :] for r in range(head_total)], axis=1)
        query_sum = None
        order = (0, 1, 2, 3) if s < 3 else (3, 2, 1, 0)
        for j in order:
            slot = flip(lane, j)
            if s == 0:
                if j > 0:
                    kv_copy(j, slot).wait_recv()
                if j == 2:
                    launch(kv_pass())
                kt_in[slot] = kv_in[slot, 0].T
            key = kv_in[slot, 0]
            value = kv_in[slot, 1]
            dims = (((1,), (1,)), ((), ()))
            scores = lax.dot_general(key, query, dims, preferred_element_type=jnp.float32)
            grad_probs = lax.dot_general(value, grad, dims, preferred_element_type=jnp.float32)
            probs = jnp.exp2(scores * (scaling * LOG2E) - lse_row)
            probs_low = probs.astype(jnp.bfloat16)
            grad_scores = (probs * (grad_probs - delta_row)).astype(jnp.bfloat16)
            value_term = jnp.dot(probs_low, grad, preferred_element_type=jnp.float32)
            key_term = jnp.dot(grad_scores, query, preferred_element_type=jnp.float32)
            query_term = jnp.dot(kt_in[slot], grad_scores, preferred_element_type=jnp.float32)
            query_sum = query_term if query_sum is None else query_sum + query_term
            if s > 0:
                key_term = dk_acc[slot] + key_term
                value_term = dv_acc[slot] + value_term
            if s == 3 and j in (1, 3):
                dkv_out[j, 0] = key_term.astype(jnp.bfloat16)
                dkv_out[j, 1] = value_term.astype(jnp.bfloat16)
                launch(dkv_copy(j))
            else:
                dk_acc[slot] = key_term
                dv_acc[slot] = value_term
            if s == 3 and j == 1:
                beside = flip(lane, 2)
                dkv_copy(3).wait_recv()
                key_pair = dk_acc[beside] + dkv_in[3, 0].astype(jnp.float32)
                value_pair = dv_acc[beside] + dkv_in[3, 1].astype(jnp.float32)
                dkv_out[2, 0] = key_pair.astype(jnp.bfloat16)
                dkv_out[2, 1] = value_pair.astype(jnp.bfloat16)
                launch(dkv_copy(2))
            if s == 0 and j == 0:

                @pl.when(inner)
                def _():
                    for r in rows_of(3):
                        qd_copy(3, r, zone, row).start()

        query_low = query_sum.astype(jnp.bfloat16)
        block = q_ref.shape[0]
        for r in range(head_total):
            dq_out[there, r] = query_low[:, r * block : (r + 1) * block]
        if s == 0:
            dq_in[row, zone] = dq_out[zone, row]
        for r in rows_of(s):
            launch(dq_copy(s, r, row, zone))

    for s in steps:
        for r in rows_of(s):
            dq_copy(s, r, r, flip(zone, s)).wait_recv()
    for h in range(head_total):
        total = dq_in[h, 0].astype(jnp.float32)
        for z in range(1, 4):
            total = total + dq_in[h, z].astype(jnp.float32)
        dq_ref[:, h * dim : (h + 1) * dim] = (total * scaling).T.astype(jnp.bfloat16)

    key_sum = dk_acc[lane]
    value_sum = dv_acc[lane]
    for j in (1, 2):
        dkv_copy(j).wait_recv()
        key_sum = key_sum + dkv_in[j, 0].astype(jnp.float32)
        value_sum = value_sum + dkv_in[j, 1].astype(jnp.float32)
    dk_ref[...] = (key_sum * scaling).astype(jnp.bfloat16)
    dv_ref[...] = value_sum.astype(jnp.bfloat16)
    for copy in sends:
        copy.wait_send()

    @pl.when(inner)
    def _():
        for r in rows_of(3):
            qd_copy(3, r, zone, row).wait_send()
            relay_copy(r).wait_send()


def write_kernel(dq_ref, dk_ref, dv_ref, dq_out, dk_out, dv_out, dq_held, dk_held, dv_held, sems):
    groups = ((dq_ref, dq_held, dq_out), (dk_ref, dk_held, dk_out), (dv_ref, dv_held, dv_out))
    loads = [pltpu.make_async_copy(g[0], g[1], sems.at[0, i]) for i, g in enumerate(groups)]
    stores = [pltpu.make_async_copy(g[1], g[2], sems.at[1, i]) for i, g in enumerate(groups)]
    for load in loads:
        load.start()
    for load, store in zip(loads, stores):
        load.wait()
        store.start()
    for store in stores:
        store.wait()


def fused_device(queries, keys, values, outputs, d_out, lse):
    head_total = lse.shape[0]
    block = queries.shape[0]
    key_rows, dim = keys.shape
    zones, lanes = 4, 4
    bf16, f32 = jnp.bfloat16, jnp.float32
    dma = pltpu.SemaphoreType.DMA
    vmem = pl.BlockSpec(memory_space=pltpu.VMEM)
    pairs = head_total * block * zones * key_rows * lanes
    hbm = pl.BlockSpec(memory_space=pltpu.HBM)
    results = pl.pallas_call(
        functools.partial(fused_kernel, head_total),
        out_shape=(
            jax.ShapeDtypeStruct(queries.shape, bf16),
            jax.ShapeDtypeStruct(keys.shape, bf16),
            jax.ShapeDtypeStruct(values.shape, bf16),
        ),
        in_specs=[hbm] * 6,
        out_specs=(vmem, vmem, vmem),
        scratch_shapes=[
            pltpu.VMEM((head_total, 2, block, dim), bf16),
            pltpu.VMEM((zones, 2, head_total, block, dim), bf16),
            pltpu.VMEM((head_total, 8, block), f32),
            pltpu.VMEM((zones, head_total, 8, block), f32),
            pltpu.VMEM((lanes, 2, key_rows, dim), bf16),
            pltpu.VMEM((lanes, dim, key_rows), bf16),
            pltpu.VMEM((lanes, key_rows, dim), f32),
            pltpu.VMEM((lanes, key_rows, dim), f32),
            pltpu.VMEM((zones, head_total, dim, block), bf16),
            pltpu.VMEM((head_total, zones, dim, block), bf16),
            pltpu.VMEM((lanes, 2, key_rows, dim), bf16),
            pltpu.VMEM((lanes, 2, key_rows, dim), bf16),
            dma((zones, head_total)),
            dma((zones, head_total)),
            dma((zones, head_total)),
            dma((zones, head_total)),
            dma((lanes,)),
            dma((lanes,)),
            dma((zones, head_total)),
            dma((head_total, zones)),
            dma((lanes,)),
            dma((lanes,)),
            pltpu.VMEM(outputs.shape, bf16),
            pltpu.VMEM(lse.shape, f32),
            dma((8,)),
            dma((head_total,)),
        ],
        compiler_params=pltpu.CompilerParams(
            collective_id=0, has_side_effects=True, vmem_limit_bytes=63 * 1024 * 1024
        ),
        cost_estimate=pl.CostEstimate(
            flops=10 * pairs * dim, bytes_accessed=9 * block * 2 * dim * 2, transcendentals=pairs
        ),
    )(queries, keys, values, outputs, d_out, lse)
    return pl.pallas_call(
        write_kernel,
        out_shape=tuple(jax.ShapeDtypeStruct(x.shape, x.dtype) for x in results),
        in_specs=[hbm] * 3,
        out_specs=(hbm, hbm, hbm),
        scratch_shapes=[pltpu.VMEM(x.shape, x.dtype) for x in results] + [dma((2, 3))],
        compiler_params=pltpu.CompilerParams(vmem_limit_bytes=63 * 1024 * 1024),
    )(*results)


def solution(mesh):
    placed = (
        P(("row", "col"), None),
        P("col", "row"),
        P("col", "row"),
        P(("row", "col"), None),
        P(("row", "col"), None),
        P(None, ("row", "col")),
    )
    fused = mesh.shape["row"] == 2 and mesh.shape["col"] == 16

    def local(queries, keys, values, outputs, d_out, lse):
        head_dim = queries.shape[1] // lse.shape[0]
        fits = lse.shape[0] == mesh.shape["row"] and head_dim == 128 and queries.shape[0] == 128
        chosen = fused_device if fused and fits else per_device
        return chosen(queries, keys, values, outputs, d_out, lse)

    return jax.shard_map(
        local,
        mesh=mesh,
        in_specs=placed,
        out_specs=(P(("row", "col"), None), P("col", "row"), P("col", "row")),
        check_vma=False,
    )
```

```python
import functools

import jax
import jax.numpy as jnp
from jax import lax
from jax.experimental import pallas as pl
from jax.experimental.pallas import tpu as pltpu
from jax.sharding import PartitionSpec as P


def block_size(row_total):
    block_rows = row_total
    while block_rows > 512 and block_rows % 2 == 0:
        block_rows = block_rows // 2
    return block_rows


def head_slice(matrix, head_index, head_dim):
    return matrix[:, head_index * head_dim : (head_index + 1) * head_dim]


def contract_rows(left, right):
    return lax.dot_general(
        left, right, (((0,), (0,)), ((), ())), preferred_element_type=jnp.float32
    )


def score_terms(query_head, grad_head, lse_row, delta_row, key_head, value_head, scaling):
    scores = jnp.dot(query_head, key_head.T, preferred_element_type=jnp.float32)
    probs = jnp.exp(scores * scaling - lse_row[:, None])
    probs_low = probs.astype(jnp.bfloat16)
    grad_probs = jnp.dot(grad_head, value_head.T, preferred_element_type=jnp.float32)
    grad_scores = (probs * (grad_probs - delta_row[:, None])).astype(jnp.bfloat16)
    return (probs_low, grad_scores)


def block_grads(query_rows, grad_rows, lse_rows, delta_rows, key_all, value_all, head_dim):
    head_total = lse_rows.shape[0]
    scaling = head_dim ** (-0.5)
    key_terms = []
    value_terms = []
    for head_index in range(head_total):
        query_head = head_slice(query_rows, head_index, head_dim)
        grad_head = head_slice(grad_rows, head_index, head_dim)
        key_head = head_slice(key_all, head_index, head_dim)
        value_head = head_slice(value_all, head_index, head_dim)
        probs_low, grad_scores = score_terms(
            query_head,
            grad_head,
            lse_rows[head_index],
            delta_rows[head_index],
            key_head,
            value_head,
            scaling,
        )
        value_terms.append(contract_rows(probs_low, grad_head))
        key_terms.append(contract_rows(grad_scores, query_head))
    key_term = jnp.concatenate(key_terms, axis=1)
    value_term = jnp.concatenate(value_terms, axis=1)
    query_term = None
    return (key_term, value_term, query_term)


def split_blocks(query_all, grad_all, lse_all, delta_all):
    row_total, features = query_all.shape
    block_rows = block_size(row_total)
    steps_total = row_total // block_rows
    head_total = lse_all.shape[0]
    query_blocks = query_all.reshape(steps_total, block_rows, features)
    grad_blocks = grad_all.reshape(steps_total, block_rows, features)
    lse_blocks = lse_all.reshape(head_total, steps_total, block_rows).transpose(1, 0, 2)
    delta_blocks = delta_all.reshape(head_total, steps_total, block_rows).transpose(1, 0, 2)
    return (query_blocks, grad_blocks, lse_blocks, delta_blocks)


def query_pass(query_all, grad_all, lse_all, delta_all, key_all, value_all, head_dim):
    row_total, features = query_all.shape
    block_inputs = split_blocks(query_all, grad_all, lse_all, delta_all)
    empty_sums = jnp.zeros((key_all.shape[0], features), jnp.float32)

    def advance(running, inputs):
        key_sum, value_sum = running
        query_rows, grad_rows, lse_rows, delta_rows = inputs
        key_term, value_term, query_term = block_grads(
            query_rows, grad_rows, lse_rows, delta_rows, key_all, value_all, head_dim
        )
        return ((key_sum + key_term, value_sum + value_term), query_term)

    (key_sum, value_sum), query_terms = lax.scan(advance, (empty_sums, empty_sums), block_inputs)
    return (key_sum, value_sum, query_terms)


def query_only(query_rows, grad_rows, lse_rows, delta_rows, key_all, value_all, head_dim):
    row_total, features = query_rows.shape
    head_total = lse_rows.shape[0]
    scaling = head_dim ** (-0.5)
    block_inputs = split_blocks(query_rows, grad_rows, lse_rows, delta_rows)

    def one_block(inputs):
        query_part, grad_part, lse_part, delta_part = inputs
        pieces = []
        for head_index in range(head_total):
            query_head = head_slice(query_part, head_index, head_dim)
            grad_head = head_slice(grad_part, head_index, head_dim)
            key_head = head_slice(key_all, head_index, head_dim)
            value_head = head_slice(value_all, head_index, head_dim)
            probs_low, grad_scores = score_terms(
                query_head,
                grad_head,
                lse_part[head_index],
                delta_part[head_index],
                key_head,
                value_head,
                scaling,
            )
            pieces.append(jnp.dot(grad_scores, key_head, preferred_element_type=jnp.float32))
        return jnp.concatenate(pieces, axis=1)

    return lax.map(one_block, block_inputs).reshape(row_total, features)


def head_delta(d_out, outputs, head_total, head_dim):
    product = d_out.astype(jnp.float32) * outputs.astype(jnp.float32)
    return jnp.sum(product.reshape(product.shape[0], head_total, head_dim), axis=2).T


def per_device(queries, keys, values, outputs, d_out, lse):
    head_total = lse.shape[0]
    head_dim = queries.shape[1] // head_total
    scaling = head_dim ** (-0.5)
    delta = head_delta(d_out, outputs, head_total, head_dim)
    key_all, value_all = (
        lax.all_gather(keys, "row", axis=1, tiled=True),
        lax.all_gather(values, "row", axis=1, tiled=True),
    )
    query_all, grad_all = (
        lax.all_gather(queries, "col", axis=0, tiled=True),
        lax.all_gather(d_out, "col", axis=0, tiled=True),
    )
    lse_all, delta_all = (
        lax.all_gather(lse, "col", axis=1, tiled=True),
        lax.all_gather(delta, "col", axis=1, tiled=True),
    )
    key_sum, value_sum, unused_terms = query_pass(
        query_all, grad_all, lse_all, delta_all, key_all, value_all, head_dim
    )

    def query_term(first_row, row_total):
        return query_only(query_all, grad_all, lse_all, delta_all, key_all, value_all, head_dim)

    query_grad = lax.psum_scatter(
        query_term(jnp.int32(0), queries.shape[0] * lax.axis_size("col")),
        "col",
        scatter_dimension=0,
        tiled=True,
    )
    key_grad, value_grad = (
        lax.psum_scatter(key_sum, "row", scatter_dimension=1, tiled=True),
        lax.psum_scatter(value_sum, "row", scatter_dimension=1, tiled=True),
    )
    d_queries = (query_grad * scaling).astype(jnp.bfloat16)
    d_keys = (key_grad * scaling).astype(jnp.bfloat16)
    d_values = value_grad.astype(jnp.bfloat16)
    return (d_queries, d_keys, d_values)

LOG2E = 1.4426950408889634


def flip(index, bits):
    if bits == 1:
        return index + 1 - 2 * lax.rem(index, 2)
    if bits == 2:
        return lax.rem(index + 2, 4)
    if bits == 3:
        return 3 - index
    return index


def fused_kernel(
    head_total,
    q_ref,
    k_ref,
    v_ref,
    o_ref,
    g_ref,
    lse_ref,
    dq_ref,
    dk_ref,
    dv_ref,
    qd_out,
    qd_in,
    st_out,
    st_in,
    kv_in,
    kt_in,
    dk_acc,
    dv_acc,
    dq_out,
    dq_in,
    dkv_out,
    dkv_in,
    qd_ssem,
    qd_rsem,
    st_ssem,
    st_rsem,
    kv_ssem,
    kv_rsem,
    dq_ssem,
    dq_rsem,
    dkv_ssem,
    dkv_rsem,
    o_in,
    lse_in,
    in_sem,
    relay_ssem,
):
    row = lax.axis_index("row")
    col = lax.axis_index("col")
    zone = col // 4
    lane = lax.rem(col, 4)
    inner = lax.rem(zone + 1, 4) // 2 == 1
    dim = k_ref.shape[1]
    block = q_ref.shape[0]
    scaling = dim ** (-0.5)
    MESH = pl.DeviceIdType.MESH
    bf16, f32 = jnp.bfloat16, jnp.float32
    rows = (row, 1 - row)
    steps = (0, 2, 1, 3)

    def at(k, s, j):
        return (rows[k], flip(zone, s) * 4 + flip(lane, j))

    def rows_of(s):
        return (1,) if s == 0 else (0, 1)

    loads = []
    row_loads = [pltpu.make_async_copy(lse_ref, lse_in, in_sem.at[8])]
    for k in range(head_total):
        cols = pl.ds(pl.multiple_of(rows[k] * dim, dim), dim)
        loads.append(pltpu.make_async_copy(q_ref.at[:, cols], qd_out.at[k, 0], in_sem.at[k]))
        loads.append(pltpu.make_async_copy(g_ref.at[:, cols], qd_out.at[k, 1], in_sem.at[2 + k]))
        row_loads.append(pltpu.make_async_copy(o_ref.at[:, cols], o_in.at[k], in_sem.at[4 + k]))
    key_loads = [
        pltpu.make_async_copy(k_ref, kv_in.at[0, 0], in_sem.at[6]),
        pltpu.make_async_copy(v_ref, kv_in.at[0, 1], in_sem.at[7]),
    ]
    for load in loads + key_loads + row_loads:
        load.start()

    peers = [at(0, 0, 1), at(0, 0, 2)] + [at(k, s, 0) for s in steps for k in rows_of(s)]
    barrier = pltpu.get_barrier_semaphore()
    for peer in peers:
        pl.semaphore_signal(barrier, inc=1, device_id=peer, device_id_type=MESH)

    def remote(src, dst, ssem, rsem, peer):
        return pltpu.make_async_remote_copy(
            src_ref=src,
            dst_ref=dst,
            send_sem=ssem,
            recv_sem=rsem,
            device_id=peer,
            device_id_type=MESH,
        )

    def kv_copy(j):
        if j == 3:
            return remote(kv_in.at[2], kv_in.at[3], kv_ssem.at[3], kv_rsem.at[3], at(0, 0, 1))
        return remote(kv_in.at[0], kv_in.at[j], kv_ssem.at[j], kv_rsem.at[j], at(0, 0, j))

    def st_copy(s, k):
        return remote(st_out.at[k], st_in.at[s, k], st_ssem.at[s, k], st_rsem.at[s, k], at(k, s, 0))

    def qd_copy(s, k):
        return remote(
            qd_out.at[k], qd_in.at[s, :, k], qd_ssem.at[s, k], qd_rsem.at[s, k], at(k, s, 0)
        )

    def relay_copy(k):
        return remote(
            qd_in.at[2, :, k], qd_in.at[3, :, k], relay_ssem.at[k], qd_rsem.at[3, k], at(0, 1, 0)
        )

    def dq_copy(s, k):
        return remote(dq_out.at[s, k], dq_in.at[s, k], dq_ssem.at[s, k], dq_rsem.at[s, k], at(k, s, 0))

    def dkv_copy(j):
        peer = at(0, 0, 2 if j == 2 else 1)
        return remote(dkv_out.at[j], dkv_in.at[j], dkv_ssem.at[j], dkv_rsem.at[j], peer)

    sends = []

    def launch(copy):
        copy.start()
        sends.append(copy)

    for load in loads:
        load.wait()
    pl.semaphore_wait(barrier, len(peers))
    for k in rows_of(2):
        launch(qd_copy(2, k))
    for load in key_loads:
        load.wait()
    for j in (2, 1):
        launch(kv_copy(j))
    for s in (0, 1):
        for k in rows_of(s):
            launch(qd_copy(s, k))
    qd_in[0, 0, 0] = qd_out[0, 0]
    qd_in[0, 1, 0] = qd_out[0, 1]

    for load in row_loads:
        load.wait()
    for k in range(head_total):
        product = qd_out[k, 1].astype(f32) * o_in[k].astype(f32)
        delta = lax.dot_general(
            jnp.ones((8, dim), f32),
            product,
            (((1,), (1,)), ((), ())),
            precision=lax.Precision.HIGHEST,
            preferred_element_type=f32,
        )
        lse_row = jnp.where(rows[k] == 0, lse_in[0:1, :], lse_in[1:2, :]) * LOG2E
        upper = lax.broadcasted_iota(jnp.int32, delta.shape, 0) < 4
        st_out[k] = jnp.where(upper, jnp.broadcast_to(lse_row, delta.shape), delta)
    st_in[0, 0] = st_out[0]
    for s in (2, 0, 3, 1):
        for k in rows_of(s):
            launch(st_copy(s, k))

    for s in steps:
        for k in rows_of(s):
            qd_copy(s, k).wait_recv()
        if s == 2:

            @pl.when(inner)
            def _():
                for k in rows_of(2):
                    relay_copy(k).start()

        for k in rows_of(s):
            st_copy(s, k).wait_recv()
        query = qd_in[s, 0].reshape(head_total * block, dim)
        grad = qd_in[s, 1].reshape(head_total * block, dim)
        query_t = query.T
        grad_t = grad.T
        lse_row = jnp.concatenate([st_in[s, k, 0:1, :] for k in range(head_total)], axis=1)
        delta_row = jnp.concatenate([st_in[s, k, 4:5, :] for k in range(head_total)], axis=1)
        query_sum = None
        order = (0, 1, 2, 3) if s < 3 else (3, 2, 1, 0)
        for j in order:
            if s == 0:
                if j > 0:
                    kv_copy(j).wait_recv()
                if j == 2:
                    launch(kv_copy(3))
                kt_in[j] = kv_in[j, 0].T
            scores = jnp.dot(kv_in[j, 0], query_t, preferred_element_type=f32)
            grad_probs = jnp.dot(kv_in[j, 1], grad_t, preferred_element_type=f32)
            probs = jnp.exp2(scores * (scaling * LOG2E) - lse_row)
            probs_low = probs.astype(bf16)
            grad_scores = (probs * (grad_probs - delta_row)).astype(bf16)
            value_term = jnp.dot(probs_low, grad, preferred_element_type=f32)
            key_term = jnp.dot(grad_scores, query, preferred_element_type=f32)
            query_term = jnp.dot(kt_in[j], grad_scores, preferred_element_type=f32)
            query_sum = query_term if query_sum is None else query_sum + query_term
            if s > 0:
                key_term = dk_acc[j] + key_term
                value_term = dv_acc[j] + value_term
            if s == 3 and j in (1, 3):
                dkv_out[j, 0] = key_term.astype(bf16)
                dkv_out[j, 1] = value_term.astype(bf16)
                launch(dkv_copy(j))
            else:
                dk_acc[j] = key_term
                dv_acc[j] = value_term
            if s == 3 and j == 1:
                dkv_copy(3).wait_recv()
                dkv_out[2, 0] = (dk_acc[2] + dkv_in[3, 0].astype(f32)).astype(bf16)
                dkv_out[2, 1] = (dv_acc[2] + dkv_in[3, 1].astype(f32)).astype(bf16)
                launch(dkv_copy(2))
            if s == 0 and j == 0:

                @pl.when(inner)
                def _():
                    for k in rows_of(3):
                        qd_copy(3, k).start()

        query_low = query_sum.astype(bf16)
        for k in range(head_total):
            dq_out[s, k] = query_low[:, k * block : (k + 1) * block]
        for k in rows_of(s):
            launch(dq_copy(s, k))

    for s in steps:
        for k in rows_of(s):
            dq_copy(s, k).wait_recv()
    totals = []
    for k in range(head_total):
        total = (dq_out[0, 0] if k == 0 else dq_in[0, k]).astype(f32)
        for s in (1, 2, 3):
            total = total + dq_in[s, k].astype(f32)
        totals.append((total * scaling).T)
    dq_ref[:, :dim] = jnp.where(row == 0, totals[0], totals[1]).astype(bf16)
    dq_ref[:, dim:] = jnp.where(row == 0, totals[1], totals[0]).astype(bf16)

    key_sum = dk_acc[0]
    value_sum = dv_acc[0]
    for j in (1, 2):
        dkv_copy(j).wait_recv()
        key_sum = key_sum + dkv_in[j, 0].astype(f32)
        value_sum = value_sum + dkv_in[j, 1].astype(f32)
    dk_ref[...] = (key_sum * scaling).astype(bf16)
    dv_ref[...] = value_sum.astype(bf16)
    for copy in sends:
        copy.wait_send()

    @pl.when(inner)
    def _():
        for k in rows_of(3):
            qd_copy(3, k).wait_send()
            relay_copy(k).wait_send()


def write_kernel(dq_ref, dk_ref, dv_ref, dq_out, dk_out, dv_out, dq_held, dk_held, dv_held, sems):
    groups = ((dq_ref, dq_held, dq_out), (dk_ref, dk_held, dk_out), (dv_ref, dv_held, dv_out))
    loads = [pltpu.make_async_copy(g[0], g[1], sems.at[0, i]) for i, g in enumerate(groups)]
    stores = [pltpu.make_async_copy(g[1], g[2], sems.at[1, i]) for i, g in enumerate(groups)]
    for load in loads:
        load.start()
    for load, store in zip(loads, stores):
        load.wait()
        store.start()
    for store in stores:
        store.wait()


def fused_device(queries, keys, values, outputs, d_out, lse):
    head_total = lse.shape[0]
    block = queries.shape[0]
    key_rows, dim = keys.shape
    zones, lanes = 4, 4
    bf16, f32 = jnp.bfloat16, jnp.float32
    dma = pltpu.SemaphoreType.DMA
    vmem = pl.BlockSpec(memory_space=pltpu.VMEM)
    pairs = head_total * block * zones * key_rows * lanes
    hbm = pl.BlockSpec(memory_space=pltpu.HBM)
    results = pl.pallas_call(
        functools.partial(fused_kernel, head_total),
        out_shape=(
            jax.ShapeDtypeStruct(queries.shape, bf16),
            jax.ShapeDtypeStruct(keys.shape, bf16),
            jax.ShapeDtypeStruct(values.shape, bf16),
        ),
        in_specs=[hbm] * 6,
        out_specs=(vmem, vmem, vmem),
        scratch_shapes=[
            pltpu.VMEM((head_total, 2, block, dim), bf16),
            pltpu.VMEM((zones, 2, head_total, block, dim), bf16),
            pltpu.VMEM((head_total, 8, block), f32),
            pltpu.VMEM((zones, head_total, 8, block), f32),
            pltpu.VMEM((lanes, 2, key_rows, dim), bf16),
            pltpu.VMEM((lanes, dim, key_rows), bf16),
            pltpu.VMEM((lanes, key_rows, dim), f32),
            pltpu.VMEM((lanes, key_rows, dim), f32),
            pltpu.VMEM((zones, head_total, dim, block), bf16),
            pltpu.VMEM((zones, head_total, dim, block), bf16),
            pltpu.VMEM((lanes, 2, key_rows, dim), bf16),
            pltpu.VMEM((lanes, 2, key_rows, dim), bf16),
            dma((zones, head_total)),
            dma((zones, head_total)),
            dma((zones, head_total)),
            dma((zones, head_total)),
            dma((lanes,)),
            dma((lanes,)),
            dma((zones, head_total)),
            dma((zones, head_total)),
            dma((lanes,)),
            dma((lanes,)),
            pltpu.VMEM((head_total, block, dim), bf16),
            pltpu.VMEM(lse.shape, f32),
            dma((9,)),
            dma((head_total,)),
        ],
        compiler_params=pltpu.CompilerParams(
            collective_id=0, has_side_effects=True, vmem_limit_bytes=63 * 1024 * 1024
        ),
        cost_estimate=pl.CostEstimate(
            flops=10 * pairs * dim, bytes_accessed=9 * block * 2 * dim * 2, transcendentals=pairs
        ),
    )(queries, keys, values, outputs, d_out, lse)
    return pl.pallas_call(
        write_kernel,
        out_shape=tuple(jax.ShapeDtypeStruct(x.shape, x.dtype) for x in results),
        in_specs=[hbm] * 3,
        out_specs=(hbm, hbm, hbm),
        scratch_shapes=[pltpu.VMEM(x.shape, x.dtype) for x in results] + [dma((2, 3))],
        compiler_params=pltpu.CompilerParams(vmem_limit_bytes=63 * 1024 * 1024),
    )(*results)


def solution(mesh):
    placed = (
        P(("row", "col"), None),
        P("col", "row"),
        P("col", "row"),
        P(("row", "col"), None),
        P(("row", "col"), None),
        P(None, ("row", "col")),
    )
    fused = mesh.shape["row"] == 2 and mesh.shape["col"] == 16

    def local(queries, keys, values, outputs, d_out, lse):
        head_dim = queries.shape[1] // lse.shape[0]
        fits = lse.shape[0] == mesh.shape["row"] and head_dim == 128 and queries.shape[0] == 128
        chosen = fused_device if fused and fits else per_device
        return chosen(queries, keys, values, outputs, d_out, lse)

    return jax.shard_map(
        local,
        mesh=mesh,
        in_specs=placed,
        out_specs=(P(("row", "col"), None), P("col", "row"), P("col", "row")),
        check_vma=False,
    )
```

```python
import functools

import jax
import jax.numpy as jnp
from jax import lax
from jax.experimental import pallas as pl
from jax.experimental.pallas import tpu as pltpu
from jax.sharding import PartitionSpec as P


def block_size(row_total):
    block_rows = row_total
    while block_rows > 512 and block_rows % 2 == 0:
        block_rows = block_rows // 2
    return block_rows


def head_slice(matrix, head_index, head_dim):
    return matrix[:, head_index * head_dim : (head_index + 1) * head_dim]


def contract_rows(left, right):
    return lax.dot_general(
        left, right, (((0,), (0,)), ((), ())), preferred_element_type=jnp.float32
    )


def score_terms(query_head, grad_head, lse_row, delta_row, key_head, value_head, scaling):
    scores = jnp.dot(query_head, key_head.T, preferred_element_type=jnp.float32)
    probs = jnp.exp(scores * scaling - lse_row[:, None])
    probs_low = probs.astype(jnp.bfloat16)
    grad_probs = jnp.dot(grad_head, value_head.T, preferred_element_type=jnp.float32)
    grad_scores = (probs * (grad_probs - delta_row[:, None])).astype(jnp.bfloat16)
    return (probs_low, grad_scores)


def block_grads(query_rows, grad_rows, lse_rows, delta_rows, key_all, value_all, head_dim):
    head_total = lse_rows.shape[0]
    scaling = head_dim ** (-0.5)
    key_terms = []
    value_terms = []
    for head_index in range(head_total):
        query_head = head_slice(query_rows, head_index, head_dim)
        grad_head = head_slice(grad_rows, head_index, head_dim)
        key_head = head_slice(key_all, head_index, head_dim)
        value_head = head_slice(value_all, head_index, head_dim)
        probs_low, grad_scores = score_terms(
            query_head,
            grad_head,
            lse_rows[head_index],
            delta_rows[head_index],
            key_head,
            value_head,
            scaling,
        )
        value_terms.append(contract_rows(probs_low, grad_head))
        key_terms.append(contract_rows(grad_scores, query_head))
    key_term = jnp.concatenate(key_terms, axis=1)
    value_term = jnp.concatenate(value_terms, axis=1)
    query_term = None
    return (key_term, value_term, query_term)


def split_blocks(query_all, grad_all, lse_all, delta_all):
    row_total, features = query_all.shape
    block_rows = block_size(row_total)
    steps_total = row_total // block_rows
    head_total = lse_all.shape[0]
    query_blocks = query_all.reshape(steps_total, block_rows, features)
    grad_blocks = grad_all.reshape(steps_total, block_rows, features)
    lse_blocks = lse_all.reshape(head_total, steps_total, block_rows).transpose(1, 0, 2)
    delta_blocks = delta_all.reshape(head_total, steps_total, block_rows).transpose(1, 0, 2)
    return (query_blocks, grad_blocks, lse_blocks, delta_blocks)


def query_pass(query_all, grad_all, lse_all, delta_all, key_all, value_all, head_dim):
    row_total, features = query_all.shape
    block_inputs = split_blocks(query_all, grad_all, lse_all, delta_all)
    empty_sums = jnp.zeros((key_all.shape[0], features), jnp.float32)

    def advance(running, inputs):
        key_sum, value_sum = running
        query_rows, grad_rows, lse_rows, delta_rows = inputs
        key_term, value_term, query_term = block_grads(
            query_rows, grad_rows, lse_rows, delta_rows, key_all, value_all, head_dim
        )
        return ((key_sum + key_term, value_sum + value_term), query_term)

    (key_sum, value_sum), query_terms = lax.scan(advance, (empty_sums, empty_sums), block_inputs)
    return (key_sum, value_sum, query_terms)


def query_only(query_rows, grad_rows, lse_rows, delta_rows, key_all, value_all, head_dim):
    row_total, features = query_rows.shape
    head_total = lse_rows.shape[0]
    scaling = head_dim ** (-0.5)
    block_inputs = split_blocks(query_rows, grad_rows, lse_rows, delta_rows)

    def one_block(inputs):
        query_part, grad_part, lse_part, delta_part = inputs
        pieces = []
        for head_index in range(head_total):
            query_head = head_slice(query_part, head_index, head_dim)
            grad_head = head_slice(grad_part, head_index, head_dim)
            key_head = head_slice(key_all, head_index, head_dim)
            value_head = head_slice(value_all, head_index, head_dim)
            probs_low, grad_scores = score_terms(
                query_head,
                grad_head,
                lse_part[head_index],
                delta_part[head_index],
                key_head,
                value_head,
                scaling,
            )
            pieces.append(jnp.dot(grad_scores, key_head, preferred_element_type=jnp.float32))
        return jnp.concatenate(pieces, axis=1)

    return lax.map(one_block, block_inputs).reshape(row_total, features)


def head_delta(d_out, outputs, head_total, head_dim):
    product = d_out.astype(jnp.float32) * outputs.astype(jnp.float32)
    return jnp.sum(product.reshape(product.shape[0], head_total, head_dim), axis=2).T


def per_device(queries, keys, values, outputs, d_out, lse):
    head_total = lse.shape[0]
    head_dim = queries.shape[1] // head_total
    scaling = head_dim ** (-0.5)
    delta = head_delta(d_out, outputs, head_total, head_dim)
    key_all, value_all = (
        lax.all_gather(keys, "row", axis=1, tiled=True),
        lax.all_gather(values, "row", axis=1, tiled=True),
    )
    query_all, grad_all = (
        lax.all_gather(queries, "col", axis=0, tiled=True),
        lax.all_gather(d_out, "col", axis=0, tiled=True),
    )
    lse_all, delta_all = (
        lax.all_gather(lse, "col", axis=1, tiled=True),
        lax.all_gather(delta, "col", axis=1, tiled=True),
    )
    key_sum, value_sum, unused_terms = query_pass(
        query_all, grad_all, lse_all, delta_all, key_all, value_all, head_dim
    )

    def query_term(first_row, row_total):
        return query_only(query_all, grad_all, lse_all, delta_all, key_all, value_all, head_dim)

    query_grad = lax.psum_scatter(
        query_term(jnp.int32(0), queries.shape[0] * lax.axis_size("col")),
        "col",
        scatter_dimension=0,
        tiled=True,
    )
    key_grad, value_grad = (
        lax.psum_scatter(key_sum, "row", scatter_dimension=1, tiled=True),
        lax.psum_scatter(value_sum, "row", scatter_dimension=1, tiled=True),
    )
    d_queries = (query_grad * scaling).astype(jnp.bfloat16)
    d_keys = (key_grad * scaling).astype(jnp.bfloat16)
    d_values = value_grad.astype(jnp.bfloat16)
    return (d_queries, d_keys, d_values)

LOG2E = 1.4426950408889634


def flip(index, bits):
    if bits == 1:
        return index + 1 - 2 * lax.rem(index, 2)
    if bits == 2:
        return lax.rem(index + 2, 4)
    if bits == 3:
        return 3 - index
    return index


def fused_kernel(
    head_total,
    q_ref,
    k_ref,
    v_ref,
    o_ref,
    g_ref,
    lse_ref,
    dq_in,
    dkv_in,
    own_out,
    qd_out,
    qd_in,
    st_out,
    st_in,
    kv_in,
    kt_in,
    dk_acc,
    dv_acc,
    dq_out,
    dkv_out,
    pair_in,
    qd_ssem,
    qd_rsem,
    st_ssem,
    st_rsem,
    kv_ssem,
    kv_rsem,
    dq_ssem,
    dq_rsem,
    dkv_ssem,
    dkv_rsem,
    o_in,
    lse_in,
    in_sem,
    relay_ssem,
):
    row = lax.axis_index("row")
    col = lax.axis_index("col")
    zone = col // 4
    lane = lax.rem(col, 4)
    inner = lax.rem(zone + 1, 4) // 2 == 1
    dim = k_ref.shape[1]
    block = q_ref.shape[0]
    scaling = dim ** (-0.5)
    MESH = pl.DeviceIdType.MESH
    bf16, f32 = jnp.bfloat16, jnp.float32
    rows = (row, 1 - row)
    steps = (0, 2, 1, 3)

    def at(k, s, j):
        return (rows[k], flip(zone, s) * 4 + flip(lane, j))

    def rows_of(s):
        return (1,) if s == 0 else (0, 1)

    loads = []
    row_loads = [pltpu.make_async_copy(lse_ref, lse_in, in_sem.at[8])]
    for k in range(head_total):
        cols = pl.ds(pl.multiple_of(rows[k] * dim, dim), dim)
        loads.append(pltpu.make_async_copy(q_ref.at[:, cols], qd_out.at[k, 0], in_sem.at[k]))
        loads.append(pltpu.make_async_copy(g_ref.at[:, cols], qd_out.at[k, 1], in_sem.at[2 + k]))
        row_loads.append(pltpu.make_async_copy(o_ref.at[:, cols], o_in.at[k], in_sem.at[4 + k]))
    key_loads = [
        pltpu.make_async_copy(k_ref, kv_in.at[0, 0], in_sem.at[6]),
        pltpu.make_async_copy(v_ref, kv_in.at[0, 1], in_sem.at[7]),
    ]
    for load in loads + key_loads + row_loads:
        load.start()

    peers = [at(0, 0, 1), at(0, 0, 2)] + [at(k, s, 0) for s in steps for k in rows_of(s)]
    barrier = pltpu.get_barrier_semaphore()
    for peer in peers:
        pl.semaphore_signal(barrier, inc=1, device_id=peer, device_id_type=MESH)

    def remote(src, dst, ssem, rsem, peer):
        return pltpu.make_async_remote_copy(
            src_ref=src,
            dst_ref=dst,
            send_sem=ssem,
            recv_sem=rsem,
            device_id=peer,
            device_id_type=MESH,
        )

    def kv_copy(j):
        if j == 3:
            return remote(kv_in.at[2], kv_in.at[3], kv_ssem.at[3], kv_rsem.at[3], at(0, 0, 1))
        return remote(kv_in.at[0], kv_in.at[j], kv_ssem.at[j], kv_rsem.at[j], at(0, 0, j))

    def st_copy(s, k):
        return remote(st_out.at[k], st_in.at[s, k], st_ssem.at[s, k], st_rsem.at[s, k], at(k, s, 0))

    def qd_copy(s, k):
        return remote(
            qd_out.at[k], qd_in.at[s, :, k], qd_ssem.at[s, k], qd_rsem.at[s, k], at(k, s, 0)
        )

    def relay_copy(k):
        return remote(
            qd_in.at[2, :, k], qd_in.at[3, :, k], relay_ssem.at[k], qd_rsem.at[3, k], at(0, 1, 0)
        )

    def dq_copy(s, k):
        return remote(dq_out.at[s, k], dq_in.at[s, row], dq_ssem.at[s, k], dq_rsem.at[s, k], at(k, s, 0))

    def dkv_copy(j):
        peer = at(0, 0, 2 if j == 2 else 1)
        target = pair_in if j == 3 else dkv_in.at[j - 1]
        return remote(dkv_out.at[j], target, dkv_ssem.at[j], dkv_rsem.at[j], peer)

    sends = []

    def launch(copy):
        copy.start()
        sends.append(copy)

    for load in loads:
        load.wait()
    pl.semaphore_wait(barrier, len(peers))
    for k in rows_of(2):
        launch(qd_copy(2, k))
    for load in key_loads:
        load.wait()
    for j in (2, 1):
        launch(kv_copy(j))
    for s in (0, 1):
        for k in rows_of(s):
            launch(qd_copy(s, k))
    qd_in[0, 0, 0] = qd_out[0, 0]
    qd_in[0, 1, 0] = qd_out[0, 1]

    for load in row_loads:
        load.wait()
    for k in range(head_total):
        product = qd_out[k, 1].astype(f32) * o_in[k].astype(f32)
        delta = lax.dot_general(
            jnp.ones((8, dim), f32),
            product,
            (((1,), (1,)), ((), ())),
            precision=lax.Precision.HIGHEST,
            preferred_element_type=f32,
        )
        lse_row = jnp.where(rows[k] == 0, lse_in[0:1, :], lse_in[1:2, :]) * LOG2E
        upper = lax.broadcasted_iota(jnp.int32, delta.shape, 0) < 4
        st_out[k] = jnp.where(upper, jnp.broadcast_to(lse_row, delta.shape), delta)
    st_in[0, 0] = st_out[0]
    for s in (2, 0, 3, 1):
        for k in rows_of(s):
            launch(st_copy(s, k))

    for s in steps:
        for k in rows_of(s):
            qd_copy(s, k).wait_recv()
        if s == 2:

            @pl.when(inner)
            def _():
                for k in rows_of(2):
                    relay_copy(k).start()

        for k in rows_of(s):
            st_copy(s, k).wait_recv()
        query = qd_in[s, 0].reshape(head_total * block, dim)
        grad = qd_in[s, 1].reshape(head_total * block, dim)
        lse_row = jnp.concatenate([st_in[s, k, 0:1, :] for k in range(head_total)], axis=1)
        delta_row = jnp.concatenate([st_in[s, k, 4:5, :] for k in range(head_total)], axis=1)
        query_sum = None
        order = (0, 1, 2, 3) if s < 3 else (3, 2, 1, 0)
        for j in order:
            if s == 0:
                if j > 0:
                    kv_copy(j).wait_recv()
                if j == 2:
                    launch(kv_copy(3))
                kt_in[j] = kv_in[j, 0].T
            dims = (((1,), (1,)), ((), ()))
            scores = lax.dot_general(kv_in[j, 0], query, dims, preferred_element_type=f32)
            grad_probs = lax.dot_general(kv_in[j, 1], grad, dims, preferred_element_type=f32)
            probs = jnp.exp2(scores * (scaling * LOG2E) - lse_row)
            probs_low = probs.astype(bf16)
            grad_scores = (probs * (grad_probs - delta_row)).astype(bf16)
            value_term = jnp.dot(probs_low, grad, preferred_element_type=f32)
            key_term = jnp.dot(grad_scores, query, preferred_element_type=f32)
            query_term = jnp.dot(kt_in[j], grad_scores, preferred_element_type=f32)
            query_sum = query_term if query_sum is None else query_sum + query_term
            if s > 0:
                key_term = dk_acc[j] + key_term
                value_term = dv_acc[j] + value_term
            if s == 3 and j in (1, 3):
                dkv_out[j, 0] = key_term.astype(bf16)
                dkv_out[j, 1] = value_term.astype(bf16)
                launch(dkv_copy(j))
            else:
                dk_acc[j] = key_term
                dv_acc[j] = value_term
            if s == 3 and j == 1:
                dkv_copy(3).wait_recv()
                dkv_out[2, 0] = (dk_acc[2] + pair_in[0].astype(f32)).astype(bf16)
                dkv_out[2, 1] = (dv_acc[2] + pair_in[1].astype(f32)).astype(bf16)
                launch(dkv_copy(2))
            if s == 0 and j == 0:

                @pl.when(inner)
                def _():
                    for k in rows_of(3):
                        qd_copy(3, k).start()

        query_low = query_sum.astype(bf16)
        for k in range(head_total):
            dq_out[s, k] = query_low[:, k * block : (k + 1) * block]
        for k in rows_of(s):
            launch(dq_copy(s, k))

    own = [
        pltpu.make_async_copy(dk_acc.at[0], own_out.at[0], in_sem.at[0]),
        pltpu.make_async_copy(dv_acc.at[0], own_out.at[1], in_sem.at[1]),
        pltpu.make_async_copy(dq_out.at[0, 0], dq_in.at[0, row], in_sem.at[2]),
    ]
    for copy in own:
        copy.start()
    for s in steps:
        for k in rows_of(s):
            dq_copy(s, k).wait_recv()
    for j in (1, 2):
        dkv_copy(j).wait_recv()
    for copy in own:
        copy.wait()
    for copy in sends:
        copy.wait_send()

    @pl.when(inner)
    def _():
        for k in rows_of(3):
            qd_copy(3, k).wait_send()
            relay_copy(k).wait_send()


def sum_kernel(dq_parts, dkv_parts, own, dq_ref, dk_ref, dv_ref):
    bf16, f32 = jnp.bfloat16, jnp.float32
    dim = own.shape[2]
    scaling = dim ** (-0.5)
    for h in range(dq_parts.shape[1]):
        total = dq_parts[0, h].astype(f32)
        for s in range(1, dq_parts.shape[0]):
            total = total + dq_parts[s, h].astype(f32)
        dq_ref[:, h * dim : (h + 1) * dim] = (total * scaling).T.astype(bf16)
    key_sum = own[0] + dkv_parts[0, 0].astype(f32) + dkv_parts[1, 0].astype(f32)
    value_sum = own[1] + dkv_parts[0, 1].astype(f32) + dkv_parts[1, 1].astype(f32)
    dk_ref[...] = (key_sum * scaling).astype(bf16)
    dv_ref[...] = value_sum.astype(bf16)


def fused_device(queries, keys, values, outputs, d_out, lse):
    head_total = lse.shape[0]
    block = queries.shape[0]
    key_rows, dim = keys.shape
    zones, lanes = 4, 4
    bf16, f32 = jnp.bfloat16, jnp.float32
    dma = pltpu.SemaphoreType.DMA
    vmem = pl.BlockSpec(memory_space=pltpu.VMEM)
    pairs = head_total * block * zones * key_rows * lanes
    hbm = pl.BlockSpec(memory_space=pltpu.HBM)
    results = pl.pallas_call(
        functools.partial(fused_kernel, head_total),
        out_shape=(
            jax.ShapeDtypeStruct((zones, head_total, dim, block), bf16),
            jax.ShapeDtypeStruct((2, 2, key_rows, dim), bf16),
            jax.ShapeDtypeStruct((2, key_rows, dim), f32),
        ),
        in_specs=[hbm] * 6,
        out_specs=(hbm, hbm, hbm),
        scratch_shapes=[
            pltpu.VMEM((head_total, 2, block, dim), bf16),
            pltpu.VMEM((zones, 2, head_total, block, dim), bf16),
            pltpu.VMEM((head_total, 8, block), f32),
            pltpu.VMEM((zones, head_total, 8, block), f32),
            pltpu.VMEM((lanes, 2, key_rows, dim), bf16),
            pltpu.VMEM((lanes, dim, key_rows), bf16),
            pltpu.VMEM((lanes, key_rows, dim), f32),
            pltpu.VMEM((lanes, key_rows, dim), f32),
            pltpu.VMEM((zones, head_total, dim, block), bf16),
            pltpu.VMEM((lanes, 2, key_rows, dim), bf16),
            pltpu.VMEM((2, key_rows, dim), bf16),
            dma((zones, head_total)),
            dma((zones, head_total)),
            dma((zones, head_total)),
            dma((zones, head_total)),
            dma((lanes,)),
            dma((lanes,)),
            dma((zones, head_total)),
            dma((zones, head_total)),
            dma((lanes,)),
            dma((lanes,)),
            pltpu.VMEM((head_total, block, dim), bf16),
            pltpu.VMEM(lse.shape, f32),
            dma((9,)),
            dma((head_total,)),
        ],
        compiler_params=pltpu.CompilerParams(
            collective_id=0, has_side_effects=True, vmem_limit_bytes=63 * 1024 * 1024
        ),
        cost_estimate=pl.CostEstimate(
            flops=10 * pairs * dim, bytes_accessed=9 * block * 2 * dim * 2, transcendentals=pairs
        ),
    )(queries, keys, values, outputs, d_out, lse)
    return pl.pallas_call(
        sum_kernel,
        out_shape=tuple(jax.ShapeDtypeStruct(x.shape, bf16) for x in (queries, keys, values)),
        in_specs=[vmem] * 3,
        out_specs=(vmem, vmem, vmem),
        compiler_params=pltpu.CompilerParams(vmem_limit_bytes=63 * 1024 * 1024),
    )(*results)


def solution(mesh):
    placed = (
        P(("row", "col"), None),
        P("col", "row"),
        P("col", "row"),
        P(("row", "col"), None),
        P(("row", "col"), None),
        P(None, ("row", "col")),
    )
    fused = mesh.shape["row"] == 2 and mesh.shape["col"] == 16

    def local(queries, keys, values, outputs, d_out, lse):
        head_dim = queries.shape[1] // lse.shape[0]
        fits = lse.shape[0] == mesh.shape["row"] and head_dim == 128 and queries.shape[0] == 128
        chosen = fused_device if fused and fits else per_device
        return chosen(queries, keys, values, outputs, d_out, lse)

    return jax.shard_map(
        local,
        mesh=mesh,
        in_specs=placed,
        out_specs=(P(("row", "col"), None), P("col", "row"), P("col", "row")),
        check_vma=False,
    )
```

```python
import functools

import jax
import jax.numpy as jnp
from jax import lax
from jax.experimental import pallas as pl
from jax.experimental.pallas import tpu as pltpu
from jax.sharding import PartitionSpec as P


def block_size(row_total):
    block_rows = row_total
    while block_rows > 512 and block_rows % 2 == 0:
        block_rows = block_rows // 2
    return block_rows


def head_slice(matrix, head_index, head_dim):
    return matrix[:, head_index * head_dim : (head_index + 1) * head_dim]


def contract_rows(left, right):
    return lax.dot_general(
        left, right, (((0,), (0,)), ((), ())), preferred_element_type=jnp.float32
    )


def score_terms(query_head, grad_head, lse_row, delta_row, key_head, value_head, scaling):
    scores = jnp.dot(query_head, key_head.T, preferred_element_type=jnp.float32)
    probs = jnp.exp(scores * scaling - lse_row[:, None])
    probs_low = probs.astype(jnp.bfloat16)
    grad_probs = jnp.dot(grad_head, value_head.T, preferred_element_type=jnp.float32)
    grad_scores = (probs * (grad_probs - delta_row[:, None])).astype(jnp.bfloat16)
    return (probs_low, grad_scores)


def block_grads(query_rows, grad_rows, lse_rows, delta_rows, key_all, value_all, head_dim):
    head_total = lse_rows.shape[0]
    scaling = head_dim ** (-0.5)
    key_terms = []
    value_terms = []
    for head_index in range(head_total):
        query_head = head_slice(query_rows, head_index, head_dim)
        grad_head = head_slice(grad_rows, head_index, head_dim)
        key_head = head_slice(key_all, head_index, head_dim)
        value_head = head_slice(value_all, head_index, head_dim)
        probs_low, grad_scores = score_terms(
            query_head,
            grad_head,
            lse_rows[head_index],
            delta_rows[head_index],
            key_head,
            value_head,
            scaling,
        )
        value_terms.append(contract_rows(probs_low, grad_head))
        key_terms.append(contract_rows(grad_scores, query_head))
    key_term = jnp.concatenate(key_terms, axis=1)
    value_term = jnp.concatenate(value_terms, axis=1)
    query_term = None
    return (key_term, value_term, query_term)


def split_blocks(query_all, grad_all, lse_all, delta_all):
    row_total, features = query_all.shape
    block_rows = block_size(row_total)
    steps_total = row_total // block_rows
    head_total = lse_all.shape[0]
    query_blocks = query_all.reshape(steps_total, block_rows, features)
    grad_blocks = grad_all.reshape(steps_total, block_rows, features)
    lse_blocks = lse_all.reshape(head_total, steps_total, block_rows).transpose(1, 0, 2)
    delta_blocks = delta_all.reshape(head_total, steps_total, block_rows).transpose(1, 0, 2)
    return (query_blocks, grad_blocks, lse_blocks, delta_blocks)


def query_pass(query_all, grad_all, lse_all, delta_all, key_all, value_all, head_dim):
    row_total, features = query_all.shape
    block_inputs = split_blocks(query_all, grad_all, lse_all, delta_all)
    empty_sums = jnp.zeros((key_all.shape[0], features), jnp.float32)

    def advance(running, inputs):
        key_sum, value_sum = running
        query_rows, grad_rows, lse_rows, delta_rows = inputs
        key_term, value_term, query_term = block_grads(
            query_rows, grad_rows, lse_rows, delta_rows, key_all, value_all, head_dim
        )
        return ((key_sum + key_term, value_sum + value_term), query_term)

    (key_sum, value_sum), query_terms = lax.scan(advance, (empty_sums, empty_sums), block_inputs)
    return (key_sum, value_sum, query_terms)


def query_only(query_rows, grad_rows, lse_rows, delta_rows, key_all, value_all, head_dim):
    row_total, features = query_rows.shape
    head_total = lse_rows.shape[0]
    scaling = head_dim ** (-0.5)
    block_inputs = split_blocks(query_rows, grad_rows, lse_rows, delta_rows)

    def one_block(inputs):
        query_part, grad_part, lse_part, delta_part = inputs
        pieces = []
        for head_index in range(head_total):
            query_head = head_slice(query_part, head_index, head_dim)
            grad_head = head_slice(grad_part, head_index, head_dim)
            key_head = head_slice(key_all, head_index, head_dim)
            value_head = head_slice(value_all, head_index, head_dim)
            probs_low, grad_scores = score_terms(
                query_head,
                grad_head,
                lse_part[head_index],
                delta_part[head_index],
                key_head,
                value_head,
                scaling,
            )
            pieces.append(jnp.dot(grad_scores, key_head, preferred_element_type=jnp.float32))
        return jnp.concatenate(pieces, axis=1)

    return lax.map(one_block, block_inputs).reshape(row_total, features)


def head_delta(d_out, outputs, head_total, head_dim):
    product = d_out.astype(jnp.float32) * outputs.astype(jnp.float32)
    return jnp.sum(product.reshape(product.shape[0], head_total, head_dim), axis=2).T


def per_device(queries, keys, values, outputs, d_out, lse):
    head_total = lse.shape[0]
    head_dim = queries.shape[1] // head_total
    scaling = head_dim ** (-0.5)
    delta = head_delta(d_out, outputs, head_total, head_dim)
    key_all, value_all = (
        lax.all_gather(keys, "row", axis=1, tiled=True),
        lax.all_gather(values, "row", axis=1, tiled=True),
    )
    query_all, grad_all = (
        lax.all_gather(queries, "col", axis=0, tiled=True),
        lax.all_gather(d_out, "col", axis=0, tiled=True),
    )
    lse_all, delta_all = (
        lax.all_gather(lse, "col", axis=1, tiled=True),
        lax.all_gather(delta, "col", axis=1, tiled=True),
    )
    key_sum, value_sum, unused_terms = query_pass(
        query_all, grad_all, lse_all, delta_all, key_all, value_all, head_dim
    )

    def query_term(first_row, row_total):
        return query_only(query_all, grad_all, lse_all, delta_all, key_all, value_all, head_dim)

    query_grad = lax.psum_scatter(
        query_term(jnp.int32(0), queries.shape[0] * lax.axis_size("col")),
        "col",
        scatter_dimension=0,
        tiled=True,
    )
    key_grad, value_grad = (
        lax.psum_scatter(key_sum, "row", scatter_dimension=1, tiled=True),
        lax.psum_scatter(value_sum, "row", scatter_dimension=1, tiled=True),
    )
    d_queries = (query_grad * scaling).astype(jnp.bfloat16)
    d_keys = (key_grad * scaling).astype(jnp.bfloat16)
    d_values = value_grad.astype(jnp.bfloat16)
    return (d_queries, d_keys, d_values)

LOG2E = 1.4426950408889634


def flip(index, bits):
    if bits == 1:
        return index + 1 - 2 * lax.rem(index, 2)
    if bits == 2:
        return lax.rem(index + 2, 4)
    if bits == 3:
        return 3 - index
    return index


def fused_kernel(
    head_total,
    q_ref,
    k_ref,
    v_ref,
    o_ref,
    g_ref,
    lse_ref,
    dq_in,
    dkv_in,
    own_out,
    qd_out,
    qd_in,
    st_out,
    st_in,
    kv_in,
    kt_in,
    dk_acc,
    dv_acc,
    dq_out,
    dkv_out,
    pair_in,
    qd_ssem,
    qd_rsem,
    st_ssem,
    st_rsem,
    kv_ssem,
    kv_rsem,
    dq_ssem,
    dq_rsem,
    dkv_ssem,
    dkv_rsem,
    o_in,
    lse_in,
    in_sem,
    relay_ssem,
):
    row = lax.axis_index("row")
    col = lax.axis_index("col")
    zone = col // 4
    lane = lax.rem(col, 4)
    inner = lax.rem(zone + 1, 4) // 2 == 1
    dim = k_ref.shape[1]
    block = q_ref.shape[0]
    scaling = dim ** (-0.5)
    MESH = pl.DeviceIdType.MESH
    bf16, f32 = jnp.bfloat16, jnp.float32
    rows = (row, 1 - row)
    steps = (0, 2, 1, 3)

    def at(k, s, j):
        return (rows[k], flip(zone, s) * 4 + flip(lane, j))

    def rows_of(s):
        return (1,) if s == 0 else (0, 1)

    loads = []
    row_loads = [pltpu.make_async_copy(lse_ref, lse_in, in_sem.at[8])]
    for k in range(head_total):
        cols = pl.ds(pl.multiple_of(rows[k] * dim, dim), dim)
        loads.append(pltpu.make_async_copy(q_ref.at[:, cols], qd_out.at[k, 0], in_sem.at[k]))
        loads.append(pltpu.make_async_copy(g_ref.at[:, cols], qd_out.at[k, 1], in_sem.at[2 + k]))
        row_loads.append(pltpu.make_async_copy(o_ref.at[:, cols], o_in.at[k], in_sem.at[4 + k]))
    key_loads = [
        pltpu.make_async_copy(k_ref, kv_in.at[0, 0], in_sem.at[6]),
        pltpu.make_async_copy(v_ref, kv_in.at[0, 1], in_sem.at[7]),
    ]
    for load in loads + key_loads + row_loads:
        load.start()

    peers = [at(0, 0, 1), at(0, 0, 2)] + [at(k, s, 0) for s in steps for k in rows_of(s)]
    barrier = pltpu.get_barrier_semaphore()
    for peer in peers:
        pl.semaphore_signal(barrier, inc=1, device_id=peer, device_id_type=MESH)

    def remote(src, dst, ssem, rsem, peer):
        return pltpu.make_async_remote_copy(
            src_ref=src,
            dst_ref=dst,
            send_sem=ssem,
            recv_sem=rsem,
            device_id=peer,
            device_id_type=MESH,
        )

    def kv_copy(j):
        if j == 3:
            return remote(kv_in.at[2], kv_in.at[3], kv_ssem.at[3], kv_rsem.at[3], at(0, 0, 1))
        return remote(kv_in.at[0], kv_in.at[j], kv_ssem.at[j], kv_rsem.at[j], at(0, 0, j))

    def st_copy(s, k):
        return remote(st_out.at[k], st_in.at[s, k], st_ssem.at[s, k], st_rsem.at[s, k], at(k, s, 0))

    def qd_copy(s, k):
        return remote(
            qd_out.at[k], qd_in.at[s, :, k], qd_ssem.at[s, k], qd_rsem.at[s, k], at(k, s, 0)
        )

    def relay_copy(k):
        return remote(
            qd_in.at[2, :, k], qd_in.at[3, :, k], relay_ssem.at[k], qd_rsem.at[3, k], at(0, 1, 0)
        )

    def dq_copy(s, k):
        return remote(dq_out.at[s, k], dq_in.at[s, row], dq_ssem.at[s, k], dq_rsem.at[s, k], at(k, s, 0))

    def dkv_copy(j):
        peer = at(0, 0, 2 if j == 2 else 1)
        target = pair_in if j == 3 else dkv_in.at[j - 1]
        return remote(dkv_out.at[j], target, dkv_ssem.at[j], dkv_rsem.at[j], peer)

    sends = []

    def launch(copy):
        copy.start()
        sends.append(copy)

    for load in loads:
        load.wait()
    pl.semaphore_wait(barrier, len(peers))
    for k in rows_of(2):
        launch(qd_copy(2, k))
    for load in key_loads:
        load.wait()
    for j in (2, 1):
        launch(kv_copy(j))
    launch(qd_copy(0, 1))
    qd_in[0, 0, 0] = qd_out[0, 0]
    qd_in[0, 1, 0] = qd_out[0, 1]

    for load in row_loads:
        load.wait()
    for k in range(head_total):
        product = qd_out[k, 1].astype(f32) * o_in[k].astype(f32)
        delta = lax.dot_general(
            jnp.ones((8, dim), f32),
            product,
            (((1,), (1,)), ((), ())),
            precision=lax.Precision.HIGHEST,
            preferred_element_type=f32,
        )
        lse_row = jnp.where(rows[k] == 0, lse_in[0:1, :], lse_in[1:2, :]) * LOG2E
        upper = lax.broadcasted_iota(jnp.int32, delta.shape, 0) < 4
        st_out[k] = jnp.where(upper, jnp.broadcast_to(lse_row, delta.shape), delta)
    st_in[0, 0] = st_out[0]
    for s in (2, 0, 3, 1):
        for k in rows_of(s):
            launch(st_copy(s, k))

    for s in steps:
        if s == 2:

            @pl.when(jnp.logical_not(inner))
            def _():
                for k in rows_of(2):
                    qd_copy(2, k).wait_recv()

        else:
            for k in rows_of(s):
                qd_copy(s, k).wait_recv()
        for k in rows_of(s):
            st_copy(s, k).wait_recv()
        query = qd_in[s, 0].reshape(head_total * block, dim)
        grad = qd_in[s, 1].reshape(head_total * block, dim)
        lse_row = jnp.concatenate([st_in[s, k, 0:1, :] for k in range(head_total)], axis=1)
        delta_row = jnp.concatenate([st_in[s, k, 4:5, :] for k in range(head_total)], axis=1)
        query_sum = None
        order = (0, 1, 2, 3) if s < 3 else (3, 2, 1, 0)
        for j in order:
            if s == 0:
                if j > 0:
                    kv_copy(j).wait_recv()
                if j == 2:
                    launch(kv_copy(3))

                    @pl.when(inner)
                    def _():
                        for k in rows_of(3):
                            qd_copy(3, k).start()
                        for k in rows_of(2):
                            qd_copy(2, k).wait_recv()
                            relay_copy(k).start()

                kt_in[j] = kv_in[j, 0].T
            dims = (((1,), (1,)), ((), ()))
            scores = lax.dot_general(kv_in[j, 0], query, dims, preferred_element_type=f32)
            grad_probs = lax.dot_general(kv_in[j, 1], grad, dims, preferred_element_type=f32)
            probs = jnp.exp2(scores * (scaling * LOG2E) - lse_row)
            probs_low = probs.astype(bf16)
            grad_scores = (probs * (grad_probs - delta_row)).astype(bf16)
            value_term = jnp.dot(probs_low, grad, preferred_element_type=f32)
            key_term = jnp.dot(grad_scores, query, preferred_element_type=f32)
            query_term = jnp.dot(kt_in[j], grad_scores, preferred_element_type=f32)
            query_sum = query_term if query_sum is None else query_sum + query_term
            if s > 0:
                key_term = dk_acc[j] + key_term
                value_term = dv_acc[j] + value_term
            if s == 3 and j in (1, 3):
                dkv_out[j, 0] = key_term.astype(bf16)
                dkv_out[j, 1] = value_term.astype(bf16)
                launch(dkv_copy(j))
            else:
                dk_acc[j] = key_term
                dv_acc[j] = value_term
            if s == 0 and j == 0:
                for k in rows_of(1):
                    launch(qd_copy(1, k))
        query_low = query_sum.astype(bf16)
        for k in range(head_total):
            dq_out[s, k] = query_low[:, k * block : (k + 1) * block]
        for k in rows_of(s):
            launch(dq_copy(s, k))

    dkv_copy(3).wait_recv()
    dkv_out[2, 0] = (dk_acc[2] + pair_in[0].astype(f32)).astype(bf16)
    dkv_out[2, 1] = (dv_acc[2] + pair_in[1].astype(f32)).astype(bf16)
    launch(dkv_copy(2))
    own = [
        pltpu.make_async_copy(dk_acc.at[0], own_out.at[0], in_sem.at[0]),
        pltpu.make_async_copy(dv_acc.at[0], own_out.at[1], in_sem.at[1]),
        pltpu.make_async_copy(dq_out.at[0, 0], dq_in.at[0, row], in_sem.at[2]),
    ]
    for copy in own:
        copy.start()
    for s in steps:
        for k in rows_of(s):
            dq_copy(s, k).wait_recv()
    for j in (1, 2):
        dkv_copy(j).wait_recv()
    for copy in own:
        copy.wait()
    for copy in sends:
        copy.wait_send()

    @pl.when(inner)
    def _():
        for k in rows_of(3):
            qd_copy(3, k).wait_send()
            relay_copy(k).wait_send()


def sum_kernel(dq_parts, dkv_parts, own, dq_ref, dk_ref, dv_ref):
    bf16, f32 = jnp.bfloat16, jnp.float32
    dim = own.shape[2]
    scaling = dim ** (-0.5)
    for h in range(dq_parts.shape[1]):
        total = dq_parts[0, h].astype(f32)
        for s in range(1, dq_parts.shape[0]):
            total = total + dq_parts[s, h].astype(f32)
        dq_ref[:, h * dim : (h + 1) * dim] = (total * scaling).T.astype(bf16)
    key_sum = own[0] + dkv_parts[0, 0].astype(f32) + dkv_parts[1, 0].astype(f32)
    value_sum = own[1] + dkv_parts[0, 1].astype(f32) + dkv_parts[1, 1].astype(f32)
    dk_ref[...] = (key_sum * scaling).astype(bf16)
    dv_ref[...] = value_sum.astype(bf16)


def fused_device(queries, keys, values, outputs, d_out, lse):
    head_total = lse.shape[0]
    block = queries.shape[0]
    key_rows, dim = keys.shape
    zones, lanes = 4, 4
    bf16, f32 = jnp.bfloat16, jnp.float32
    dma = pltpu.SemaphoreType.DMA
    vmem = pl.BlockSpec(memory_space=pltpu.VMEM)
    pairs = head_total * block * zones * key_rows * lanes
    hbm = pl.BlockSpec(memory_space=pltpu.HBM)
    results = pl.pallas_call(
        functools.partial(fused_kernel, head_total),
        out_shape=(
            jax.ShapeDtypeStruct((zones, head_total, dim, block), bf16),
            jax.ShapeDtypeStruct((2, 2, key_rows, dim), bf16),
            jax.ShapeDtypeStruct((2, key_rows, dim), f32),
        ),
        in_specs=[hbm] * 6,
        out_specs=(hbm, hbm, hbm),
        scratch_shapes=[
            pltpu.VMEM((head_total, 2, block, dim), bf16),
            pltpu.VMEM((zones, 2, head_total, block, dim), bf16),
            pltpu.VMEM((head_total, 8, block), f32),
            pltpu.VMEM((zones, head_total, 8, block), f32),
            pltpu.VMEM((lanes, 2, key_rows, dim), bf16),
            pltpu.VMEM((lanes, dim, key_rows), bf16),
            pltpu.VMEM((lanes, key_rows, dim), f32),
            pltpu.VMEM((lanes, key_rows, dim), f32),
            pltpu.VMEM((zones, head_total, dim, block), bf16),
            pltpu.VMEM((lanes, 2, key_rows, dim), bf16),
            pltpu.VMEM((2, key_rows, dim), bf16),
            dma((zones, head_total)),
            dma((zones, head_total)),
            dma((zones, head_total)),
            dma((zones, head_total)),
            dma((lanes,)),
            dma((lanes,)),
            dma((zones, head_total)),
            dma((zones, head_total)),
            dma((lanes,)),
            dma((lanes,)),
            pltpu.VMEM((head_total, block, dim), bf16),
            pltpu.VMEM(lse.shape, f32),
            dma((9,)),
            dma((head_total,)),
        ],
        compiler_params=pltpu.CompilerParams(
            collective_id=0, has_side_effects=True, vmem_limit_bytes=63 * 1024 * 1024
        ),
        cost_estimate=pl.CostEstimate(
            flops=10 * pairs * dim, bytes_accessed=9 * block * 2 * dim * 2, transcendentals=pairs
        ),
    )(queries, keys, values, outputs, d_out, lse)
    return pl.pallas_call(
        sum_kernel,
        out_shape=tuple(jax.ShapeDtypeStruct(x.shape, bf16) for x in (queries, keys, values)),
        in_specs=[vmem] * 3,
        out_specs=(vmem, vmem, vmem),
        compiler_params=pltpu.CompilerParams(vmem_limit_bytes=63 * 1024 * 1024),
    )(*results)


def solution(mesh):
    placed = (
        P(("row", "col"), None),
        P("col", "row"),
        P("col", "row"),
        P(("row", "col"), None),
        P(("row", "col"), None),
        P(None, ("row", "col")),
    )
    fused = mesh.shape["row"] == 2 and mesh.shape["col"] == 16

    def local(queries, keys, values, outputs, d_out, lse):
        head_dim = queries.shape[1] // lse.shape[0]
        fits = lse.shape[0] == mesh.shape["row"] and head_dim == 128 and queries.shape[0] == 128
        chosen = fused_device if fused and fits else per_device
        return chosen(queries, keys, values, outputs, d_out, lse)

    return jax.shard_map(
        local,
        mesh=mesh,
        in_specs=placed,
        out_specs=(P(("row", "col"), None), P("col", "row"), P("col", "row")),
        check_vma=False,
    )
```

```python
import functools

import jax
import jax.numpy as jnp
from jax import lax
from jax.experimental import pallas as pl
from jax.experimental.pallas import tpu as pltpu
from jax.sharding import PartitionSpec as P


def block_size(row_total):
    block_rows = row_total
    while block_rows > 512 and block_rows % 2 == 0:
        block_rows = block_rows // 2
    return block_rows


def head_slice(matrix, head_index, head_dim):
    return matrix[:, head_index * head_dim : (head_index + 1) * head_dim]


def contract_rows(left, right):
    return lax.dot_general(
        left, right, (((0,), (0,)), ((), ())), preferred_element_type=jnp.float32
    )


def score_terms(query_head, grad_head, lse_row, delta_row, key_head, value_head, scaling):
    scores = jnp.dot(query_head, key_head.T, preferred_element_type=jnp.float32)
    probs = jnp.exp(scores * scaling - lse_row[:, None])
    probs_low = probs.astype(jnp.bfloat16)
    grad_probs = jnp.dot(grad_head, value_head.T, preferred_element_type=jnp.float32)
    grad_scores = (probs * (grad_probs - delta_row[:, None])).astype(jnp.bfloat16)
    return (probs_low, grad_scores)


def block_grads(query_rows, grad_rows, lse_rows, delta_rows, key_all, value_all, head_dim):
    head_total = lse_rows.shape[0]
    scaling = head_dim ** (-0.5)
    key_terms = []
    value_terms = []
    for head_index in range(head_total):
        query_head = head_slice(query_rows, head_index, head_dim)
        grad_head = head_slice(grad_rows, head_index, head_dim)
        key_head = head_slice(key_all, head_index, head_dim)
        value_head = head_slice(value_all, head_index, head_dim)
        probs_low, grad_scores = score_terms(
            query_head,
            grad_head,
            lse_rows[head_index],
            delta_rows[head_index],
            key_head,
            value_head,
            scaling,
        )
        value_terms.append(contract_rows(probs_low, grad_head))
        key_terms.append(contract_rows(grad_scores, query_head))
    key_term = jnp.concatenate(key_terms, axis=1)
    value_term = jnp.concatenate(value_terms, axis=1)
    query_term = None
    return (key_term, value_term, query_term)


def split_blocks(query_all, grad_all, lse_all, delta_all):
    row_total, features = query_all.shape
    block_rows = block_size(row_total)
    steps_total = row_total // block_rows
    head_total = lse_all.shape[0]
    query_blocks = query_all.reshape(steps_total, block_rows, features)
    grad_blocks = grad_all.reshape(steps_total, block_rows, features)
    lse_blocks = lse_all.reshape(head_total, steps_total, block_rows).transpose(1, 0, 2)
    delta_blocks = delta_all.reshape(head_total, steps_total, block_rows).transpose(1, 0, 2)
    return (query_blocks, grad_blocks, lse_blocks, delta_blocks)


def query_pass(query_all, grad_all, lse_all, delta_all, key_all, value_all, head_dim):
    row_total, features = query_all.shape
    block_inputs = split_blocks(query_all, grad_all, lse_all, delta_all)
    empty_sums = jnp.zeros((key_all.shape[0], features), jnp.float32)

    def advance(running, inputs):
        key_sum, value_sum = running
        query_rows, grad_rows, lse_rows, delta_rows = inputs
        key_term, value_term, query_term = block_grads(
            query_rows, grad_rows, lse_rows, delta_rows, key_all, value_all, head_dim
        )
        return ((key_sum + key_term, value_sum + value_term), query_term)

    (key_sum, value_sum), query_terms = lax.scan(advance, (empty_sums, empty_sums), block_inputs)
    return (key_sum, value_sum, query_terms)


def query_only(query_rows, grad_rows, lse_rows, delta_rows, key_all, value_all, head_dim):
    row_total, features = query_rows.shape
    head_total = lse_rows.shape[0]
    scaling = head_dim ** (-0.5)
    block_inputs = split_blocks(query_rows, grad_rows, lse_rows, delta_rows)

    def one_block(inputs):
        query_part, grad_part, lse_part, delta_part = inputs
        pieces = []
        for head_index in range(head_total):
            query_head = head_slice(query_part, head_index, head_dim)
            grad_head = head_slice(grad_part, head_index, head_dim)
            key_head = head_slice(key_all, head_index, head_dim)
            value_head = head_slice(value_all, head_index, head_dim)
            probs_low, grad_scores = score_terms(
                query_head,
                grad_head,
                lse_part[head_index],
                delta_part[head_index],
                key_head,
                value_head,
                scaling,
            )
            pieces.append(jnp.dot(grad_scores, key_head, preferred_element_type=jnp.float32))
        return jnp.concatenate(pieces, axis=1)

    return lax.map(one_block, block_inputs).reshape(row_total, features)


def head_delta(d_out, outputs, head_total, head_dim):
    product = d_out.astype(jnp.float32) * outputs.astype(jnp.float32)
    return jnp.sum(product.reshape(product.shape[0], head_total, head_dim), axis=2).T


def per_device(queries, keys, values, outputs, d_out, lse):
    head_total = lse.shape[0]
    head_dim = queries.shape[1] // head_total
    scaling = head_dim ** (-0.5)
    delta = head_delta(d_out, outputs, head_total, head_dim)
    key_all, value_all = (
        lax.all_gather(keys, "row", axis=1, tiled=True),
        lax.all_gather(values, "row", axis=1, tiled=True),
    )
    query_all, grad_all = (
        lax.all_gather(queries, "col", axis=0, tiled=True),
        lax.all_gather(d_out, "col", axis=0, tiled=True),
    )
    lse_all, delta_all = (
        lax.all_gather(lse, "col", axis=1, tiled=True),
        lax.all_gather(delta, "col", axis=1, tiled=True),
    )
    key_sum, value_sum, unused_terms = query_pass(
        query_all, grad_all, lse_all, delta_all, key_all, value_all, head_dim
    )

    def query_term(first_row, row_total):
        return query_only(query_all, grad_all, lse_all, delta_all, key_all, value_all, head_dim)

    query_grad = lax.psum_scatter(
        query_term(jnp.int32(0), queries.shape[0] * lax.axis_size("col")),
        "col",
        scatter_dimension=0,
        tiled=True,
    )
    key_grad, value_grad = (
        lax.psum_scatter(key_sum, "row", scatter_dimension=1, tiled=True),
        lax.psum_scatter(value_sum, "row", scatter_dimension=1, tiled=True),
    )
    d_queries = (query_grad * scaling).astype(jnp.bfloat16)
    d_keys = (key_grad * scaling).astype(jnp.bfloat16)
    d_values = value_grad.astype(jnp.bfloat16)
    return (d_queries, d_keys, d_values)

LOG2E = 1.4426950408889634


def flip(index, bits):
    if bits == 1:
        return index + 1 - 2 * lax.rem(index, 2)
    if bits == 2:
        return lax.rem(index + 2, 4)
    if bits == 3:
        return 3 - index
    return index


def fused_kernel(
    head_total,
    q_ref,
    k_ref,
    v_ref,
    o_ref,
    g_ref,
    lse_ref,
    dq_ref,
    dk_ref,
    dv_ref,
    qd_out,
    qd_in,
    st_out,
    st_in,
    kv_in,
    kt_in,
    dk_acc,
    dv_acc,
    dq_out,
    dq_in,
    dkv_out,
    dkv_in,
    qd_ssem,
    qd_rsem,
    st_ssem,
    st_rsem,
    kv_ssem,
    kv_rsem,
    dq_ssem,
    dq_rsem,
    dkv_ssem,
    dkv_rsem,
    o_in,
    lse_in,
    in_sem,
    relay_ssem,
):
    row = lax.axis_index("row")
    col = lax.axis_index("col")
    zone = col // 4
    lane = lax.rem(col, 4)
    inner = lax.rem(zone + 1, 4) // 2 == 1
    other = 1 - row
    dim = k_ref.shape[1]
    scaling = dim ** (-0.5)
    MESH = pl.DeviceIdType.MESH

    def at(r, z, m):
        return (r, z * 4 + m)

    loads = []
    for h in range(head_total):
        cols = pl.ds(h * dim, dim)
        loads.append(pltpu.make_async_copy(q_ref.at[:, cols], qd_out.at[h, 0], in_sem.at[2 * h]))
        loads.append(pltpu.make_async_copy(g_ref.at[:, cols], qd_out.at[h, 1], in_sem.at[2 * h + 1]))
    key_loads = [
        pltpu.make_async_copy(k_ref, kv_in.at[lane, 0], in_sem.at[4]),
        pltpu.make_async_copy(v_ref, kv_in.at[lane, 1], in_sem.at[5]),
    ]
    row_loads = [
        pltpu.make_async_copy(o_ref, o_in, in_sem.at[6]),
        pltpu.make_async_copy(lse_ref, lse_in, in_sem.at[7]),
    ]
    for load in loads + key_loads + row_loads:
        load.start()

    mates = [at(row, zone, flip(lane, j)) for j in (1, 2)]
    owners = [at(other, zone, lane)]
    for s in (1, 2, 3):
        owners += [at(r, flip(zone, s), lane) for r in range(head_total)]
    barrier = pltpu.get_barrier_semaphore()
    for peer in mates + owners:
        pl.semaphore_signal(barrier, inc=1, device_id=peer, device_id_type=MESH)

    def kv_copy(j, slot):
        return pltpu.make_async_remote_copy(
            src_ref=kv_in.at[lane],
            dst_ref=kv_in.at[slot],
            send_sem=kv_ssem.at[j],
            recv_sem=kv_rsem.at[slot],
            device_id=at(row, zone, flip(lane, j)),
            device_id_type=MESH,
        )

    def kv_pass():
        slot = flip(lane, 2)
        return pltpu.make_async_remote_copy(
            src_ref=kv_in.at[slot],
            dst_ref=kv_in.at[slot],
            send_sem=kv_ssem.at[3],
            recv_sem=kv_rsem.at[slot],
            device_id=at(row, zone, flip(lane, 1)),
            device_id_type=MESH,
        )

    def st_copy(s, r, slot_zone, slot_row):
        return pltpu.make_async_remote_copy(
            src_ref=st_out.at[r],
            dst_ref=st_in.at[slot_zone, slot_row],
            send_sem=st_ssem.at[s, r],
            recv_sem=st_rsem.at[slot_zone, slot_row],
            device_id=at(r, flip(zone, s), lane),
            device_id_type=MESH,
        )

    def qd_copy(s, r, slot_zone, slot_row):
        return pltpu.make_async_remote_copy(
            src_ref=qd_out.at[r],
            dst_ref=qd_in.at[slot_zone, :, slot_row],
            send_sem=qd_ssem.at[s, r],
            recv_sem=qd_rsem.at[slot_zone, slot_row],
            device_id=at(r, flip(zone, s), lane),
            device_id_type=MESH,
        )

    def relay_copy(r):
        slot_zone = flip(zone, 2)
        return pltpu.make_async_remote_copy(
            src_ref=qd_in.at[slot_zone, :, r],
            dst_ref=qd_in.at[slot_zone, :, r],
            send_sem=relay_ssem.at[r],
            recv_sem=qd_rsem.at[slot_zone, r],
            device_id=at(row, flip(zone, 1), lane),
            device_id_type=MESH,
        )

    def rows_of(s):
        return [other] if s == 0 else list(range(head_total))

    sends = []

    def launch(copy):
        copy.start()
        sends.append(copy)

    for load in loads:
        load.wait()
    pl.semaphore_wait(barrier, len(mates) + len(owners))
    for r in rows_of(2):
        launch(qd_copy(2, r, zone, row))
    for load in key_loads:
        load.wait()
    for j in (2, 1):
        launch(kv_copy(j, lane))
    for s in (0, 1):
        for r in rows_of(s):
            launch(qd_copy(s, r, zone, row))
    qd_in[zone, 0, row] = qd_out[row, 0]
    qd_in[zone, 1, row] = qd_out[row, 1]

    for load in row_loads:
        load.wait()
    for h in range(head_total):
        cols = slice(h * dim, (h + 1) * dim)
        product = qd_out[h, 1].astype(jnp.float32) * o_in[:, cols].astype(jnp.float32)
        delta = lax.dot_general(
            jnp.ones((8, dim), jnp.float32),
            product,
            (((1,), (1,)), ((), ())),
            precision=lax.Precision.HIGHEST,
            preferred_element_type=jnp.float32,
        )
        lse_rows = jnp.broadcast_to(lse_in[h : h + 1, :] * LOG2E, delta.shape)
        upper = lax.broadcasted_iota(jnp.int32, delta.shape, 0) < 4
        st_out[h] = jnp.where(upper, lse_rows, delta)
    st_in[zone, row] = st_out[row]
    for s in (2, 0, 3, 1):
        for r in rows_of(s):
            launch(st_copy(s, r, zone, row))

    def dq_copy(s, r, slot_row, slot_zone):
        there = flip(zone, s)
        return pltpu.make_async_remote_copy(
            src_ref=dq_out.at[there, r],
            dst_ref=dq_in.at[slot_row, slot_zone],
            send_sem=dq_ssem.at[s, r],
            recv_sem=dq_rsem.at[slot_row, slot_zone],
            device_id=at(r, there, lane),
            device_id_type=MESH,
        )

    def dkv_copy(j):
        return pltpu.make_async_remote_copy(
            src_ref=dkv_out.at[j],
            dst_ref=dkv_in.at[j],
            send_sem=dkv_ssem.at[j],
            recv_sem=dkv_rsem.at[j],
            device_id=at(row, zone, flip(lane, 2 if j == 2 else 1)),
            device_id_type=MESH,
        )

    steps = (0, 1, 2, 3)
    for s in steps:
        there = flip(zone, s)
        for r in rows_of(s):
            qd_copy(s, r, there, r).wait_recv()
        if s == 2:

            @pl.when(inner)
            def _():
                for r in rows_of(2):
                    relay_copy(r).start()

        for r in rows_of(s):
            st_copy(s, r, there, r).wait_recv()
        rows2 = head_total * q_ref.shape[0]
        query = qd_in[there, 0].reshape(rows2, dim)
        grad = qd_in[there, 1].reshape(rows2, dim)
        lse_row = jnp.concatenate([st_in[there, r, 0:1, :] for r in range(head_total)], axis=1)
        delta_row = jnp.concatenate([st_in[there, r, 4:5, :] for r in range(head_total)], axis=1)
        query_sum = None
        order = (0, 1, 2, 3) if s < 3 else (3, 2, 1, 0)
        for j in order:
            slot = flip(lane, j)
            if s == 0:
                if j > 0:
                    kv_copy(j, slot).wait_recv()
                if j == 2:
                    launch(kv_pass())
                kt_in[slot] = kv_in[slot, 0].T
            key = kv_in[slot, 0]
            value = kv_in[slot, 1]
            dims = (((1,), (1,)), ((), ()))
            scores = lax.dot_general(key, query, dims, preferred_element_type=jnp.float32)
            grad_probs = lax.dot_general(value, grad, dims, preferred_element_type=jnp.float32)
            probs = jnp.exp2(scores * (scaling * LOG2E) - lse_row)
            probs_low = probs.astype(jnp.bfloat16)
            grad_scores = (probs * (grad_probs - delta_row)).astype(jnp.bfloat16)
            value_term = jnp.dot(probs_low, grad, preferred_element_type=jnp.float32)
            key_term = jnp.dot(grad_scores, query, preferred_element_type=jnp.float32)
            query_term = jnp.dot(kt_in[slot], grad_scores, preferred_element_type=jnp.float32)
            query_sum = query_term if query_sum is None else query_sum + query_term
            if s > 0:
                key_term = dk_acc[slot] + key_term
                value_term = dv_acc[slot] + value_term
            if s == 3 and j in (1, 3):
                dkv_out[j, 0] = key_term.astype(jnp.bfloat16)
                dkv_out[j, 1] = value_term.astype(jnp.bfloat16)
                launch(dkv_copy(j))
            else:
                dk_acc[slot] = key_term
                dv_acc[slot] = value_term
            if s == 3 and j == 1:
                beside = flip(lane, 2)
                dkv_copy(3).wait_recv()
                key_pair = dk_acc[beside] + dkv_in[3, 0].astype(jnp.float32)
                value_pair = dv_acc[beside] + dkv_in[3, 1].astype(jnp.float32)
                dkv_out[2, 0] = key_pair.astype(jnp.bfloat16)
                dkv_out[2, 1] = value_pair.astype(jnp.bfloat16)
                launch(dkv_copy(2))
            if s == 0 and j == 0:

                @pl.when(inner)
                def _():
                    for r in rows_of(3):
                        qd_copy(3, r, zone, row).start()

        query_low = query_sum.astype(jnp.bfloat16)
        block = q_ref.shape[0]
        for r in range(head_total):
            dq_out[there, r] = query_low[:, r * block : (r + 1) * block]
        if s == 0:
            dq_in[row, zone] = dq_out[zone, row]
        for r in rows_of(s):
            launch(dq_copy(s, r, row, zone))

    for s in steps:
        for r in rows_of(s):
            dq_copy(s, r, r, flip(zone, s)).wait_recv()
    for h in range(head_total):
        total = dq_in[h, 0].astype(jnp.float32)
        for z in range(1, 4):
            total = total + dq_in[h, z].astype(jnp.float32)
        dq_ref[:, h * dim : (h + 1) * dim] = (total * scaling).T.astype(jnp.bfloat16)

    key_sum = dk_acc[lane]
    value_sum = dv_acc[lane]
    for j in (1, 2):
        dkv_copy(j).wait_recv()
        key_sum = key_sum + dkv_in[j, 0].astype(jnp.float32)
        value_sum = value_sum + dkv_in[j, 1].astype(jnp.float32)
    dk_ref[...] = (key_sum * scaling).astype(jnp.bfloat16)
    dv_ref[...] = value_sum.astype(jnp.bfloat16)
    for copy in sends:
        copy.wait_send()

    @pl.when(inner)
    def _():
        for r in rows_of(3):
            qd_copy(3, r, zone, row).wait_send()
            relay_copy(r).wait_send()


def write_kernel(dq_ref, dk_ref, dv_ref, dq_out, dk_out, dv_out, dq_held, dk_held, dv_held, sems):
    groups = ((dq_ref, dq_held, dq_out), (dk_ref, dk_held, dk_out), (dv_ref, dv_held, dv_out))
    loads = [pltpu.make_async_copy(g[0], g[1], sems.at[0, i]) for i, g in enumerate(groups)]
    stores = [pltpu.make_async_copy(g[1], g[2], sems.at[1, i]) for i, g in enumerate(groups)]
    for load in loads:
        load.start()
    for load, store in zip(loads, stores):
        load.wait()
        store.start()
    for store in stores:
        store.wait()


def fused_device(queries, keys, values, outputs, d_out, lse):
    head_total = lse.shape[0]
    block = queries.shape[0]
    key_rows, dim = keys.shape
    zones, lanes = 4, 4
    bf16, f32 = jnp.bfloat16, jnp.float32
    dma = pltpu.SemaphoreType.DMA
    vmem = pl.BlockSpec(memory_space=pltpu.VMEM)
    pairs = head_total * block * zones * key_rows * lanes
    hbm = pl.BlockSpec(memory_space=pltpu.HBM)
    results = pl.pallas_call(
        functools.partial(fused_kernel, head_total),
        out_shape=(
            jax.ShapeDtypeStruct(queries.shape, bf16),
            jax.ShapeDtypeStruct(keys.shape, bf16),
            jax.ShapeDtypeStruct(values.shape, bf16),
        ),
        in_specs=[hbm] * 6,
        out_specs=(vmem, vmem, vmem),
        scratch_shapes=[
            pltpu.VMEM((head_total, 2, block, dim), bf16),
            pltpu.VMEM((zones, 2, head_total, block, dim), bf16),
            pltpu.VMEM((head_total, 8, block), f32),
            pltpu.VMEM((zones, head_total, 8, block), f32),
            pltpu.VMEM((lanes, 2, key_rows, dim), bf16),
            pltpu.VMEM((lanes, dim, key_rows), bf16),
            pltpu.VMEM((lanes, key_rows, dim), f32),
            pltpu.VMEM((lanes, key_rows, dim), f32),
            pltpu.VMEM((zones, head_total, dim, block), bf16),
            pltpu.VMEM((head_total, zones, dim, block), bf16),
            pltpu.VMEM((lanes, 2, key_rows, dim), bf16),
            pltpu.VMEM((lanes, 2, key_rows, dim), bf16),
            dma((zones, head_total)),
            dma((zones, head_total)),
            dma((zones, head_total)),
            dma((zones, head_total)),
            dma((lanes,)),
            dma((lanes,)),
            dma((zones, head_total)),
            dma((head_total, zones)),
            dma((lanes,)),
            dma((lanes,)),
            pltpu.VMEM(outputs.shape, bf16),
            pltpu.VMEM(lse.shape, f32),
            dma((8,)),
            dma((head_total,)),
        ],
        compiler_params=pltpu.CompilerParams(
            collective_id=0, has_side_effects=True, vmem_limit_bytes=63 * 1024 * 1024
        ),
        cost_estimate=pl.CostEstimate(
            flops=10 * pairs * dim, bytes_accessed=9 * block * 2 * dim * 2, transcendentals=pairs
        ),
    )(queries, keys, values, outputs, d_out, lse)
    return pl.pallas_call(
        write_kernel,
        out_shape=tuple(jax.ShapeDtypeStruct(x.shape, x.dtype) for x in results),
        in_specs=[hbm] * 3,
        out_specs=(hbm, hbm, hbm),
        scratch_shapes=[pltpu.VMEM(x.shape, x.dtype) for x in results] + [dma((2, 3))],
        compiler_params=pltpu.CompilerParams(vmem_limit_bytes=63 * 1024 * 1024),
    )(*results)


def solution(mesh):
    placed = (
        P(("row", "col"), None),
        P("col", "row"),
        P("col", "row"),
        P(("row", "col"), None),
        P(("row", "col"), None),
        P(None, ("row", "col")),
    )
    fused = mesh.shape["row"] == 2 and mesh.shape["col"] == 16

    def local(queries, keys, values, outputs, d_out, lse):
        head_dim = queries.shape[1] // lse.shape[0]
        fits = lse.shape[0] == mesh.shape["row"] and head_dim == 128 and queries.shape[0] == 128
        chosen = fused_device if fused and fits else per_device
        return chosen(queries, keys, values, outputs, d_out, lse)

    return jax.shard_map(
        local,
        mesh=mesh,
        in_specs=placed,
        out_specs=(P(("row", "col"), None), P("col", "row"), P("col", "row")),
        check_vma=False,
    )
```

```python
import functools

import jax
import jax.numpy as jnp
from jax import lax
from jax.experimental import pallas as pl
from jax.experimental.pallas import tpu as pltpu
from jax.sharding import PartitionSpec as P


def block_size(row_total):
    block_rows = row_total
    while block_rows > 512 and block_rows % 2 == 0:
        block_rows = block_rows // 2
    return block_rows


def head_slice(matrix, head_index, head_dim):
    return matrix[:, head_index * head_dim : (head_index + 1) * head_dim]


def contract_rows(left, right):
    return lax.dot_general(
        left, right, (((0,), (0,)), ((), ())), preferred_element_type=jnp.float32
    )


def score_terms(query_head, grad_head, lse_row, delta_row, key_head, value_head, scaling):
    scores = jnp.dot(query_head, key_head.T, preferred_element_type=jnp.float32)
    probs = jnp.exp(scores * scaling - lse_row[:, None])
    probs_low = probs.astype(jnp.bfloat16)
    grad_probs = jnp.dot(grad_head, value_head.T, preferred_element_type=jnp.float32)
    grad_scores = (probs * (grad_probs - delta_row[:, None])).astype(jnp.bfloat16)
    return (probs_low, grad_scores)


def block_grads(query_rows, grad_rows, lse_rows, delta_rows, key_all, value_all, head_dim):
    head_total = lse_rows.shape[0]
    scaling = head_dim ** (-0.5)
    key_terms = []
    value_terms = []
    for head_index in range(head_total):
        query_head = head_slice(query_rows, head_index, head_dim)
        grad_head = head_slice(grad_rows, head_index, head_dim)
        key_head = head_slice(key_all, head_index, head_dim)
        value_head = head_slice(value_all, head_index, head_dim)
        probs_low, grad_scores = score_terms(
            query_head,
            grad_head,
            lse_rows[head_index],
            delta_rows[head_index],
            key_head,
            value_head,
            scaling,
        )
        value_terms.append(contract_rows(probs_low, grad_head))
        key_terms.append(contract_rows(grad_scores, query_head))
    key_term = jnp.concatenate(key_terms, axis=1)
    value_term = jnp.concatenate(value_terms, axis=1)
    query_term = None
    return (key_term, value_term, query_term)


def split_blocks(query_all, grad_all, lse_all, delta_all):
    row_total, features = query_all.shape
    block_rows = block_size(row_total)
    steps_total = row_total // block_rows
    head_total = lse_all.shape[0]
    query_blocks = query_all.reshape(steps_total, block_rows, features)
    grad_blocks = grad_all.reshape(steps_total, block_rows, features)
    lse_blocks = lse_all.reshape(head_total, steps_total, block_rows).transpose(1, 0, 2)
    delta_blocks = delta_all.reshape(head_total, steps_total, block_rows).transpose(1, 0, 2)
    return (query_blocks, grad_blocks, lse_blocks, delta_blocks)


def query_pass(query_all, grad_all, lse_all, delta_all, key_all, value_all, head_dim):
    row_total, features = query_all.shape
    block_inputs = split_blocks(query_all, grad_all, lse_all, delta_all)
    empty_sums = jnp.zeros((key_all.shape[0], features), jnp.float32)

    def advance(running, inputs):
        key_sum, value_sum = running
        query_rows, grad_rows, lse_rows, delta_rows = inputs
        key_term, value_term, query_term = block_grads(
            query_rows, grad_rows, lse_rows, delta_rows, key_all, value_all, head_dim
        )
        return ((key_sum + key_term, value_sum + value_term), query_term)

    (key_sum, value_sum), query_terms = lax.scan(advance, (empty_sums, empty_sums), block_inputs)
    return (key_sum, value_sum, query_terms)


def query_only(query_rows, grad_rows, lse_rows, delta_rows, key_all, value_all, head_dim):
    row_total, features = query_rows.shape
    head_total = lse_rows.shape[0]
    scaling = head_dim ** (-0.5)
    block_inputs = split_blocks(query_rows, grad_rows, lse_rows, delta_rows)

    def one_block(inputs):
        query_part, grad_part, lse_part, delta_part = inputs
        pieces = []
        for head_index in range(head_total):
            query_head = head_slice(query_part, head_index, head_dim)
            grad_head = head_slice(grad_part, head_index, head_dim)
            key_head = head_slice(key_all, head_index, head_dim)
            value_head = head_slice(value_all, head_index, head_dim)
            probs_low, grad_scores = score_terms(
                query_head,
                grad_head,
                lse_part[head_index],
                delta_part[head_index],
                key_head,
                value_head,
                scaling,
            )
            pieces.append(jnp.dot(grad_scores, key_head, preferred_element_type=jnp.float32))
        return jnp.concatenate(pieces, axis=1)

    return lax.map(one_block, block_inputs).reshape(row_total, features)


def head_delta(d_out, outputs, head_total, head_dim):
    product = d_out.astype(jnp.float32) * outputs.astype(jnp.float32)
    return jnp.sum(product.reshape(product.shape[0], head_total, head_dim), axis=2).T


def per_device(queries, keys, values, outputs, d_out, lse):
    head_total = lse.shape[0]
    head_dim = queries.shape[1] // head_total
    scaling = head_dim ** (-0.5)
    delta = head_delta(d_out, outputs, head_total, head_dim)
    key_all, value_all = (
        lax.all_gather(keys, "row", axis=1, tiled=True),
        lax.all_gather(values, "row", axis=1, tiled=True),
    )
    query_all, grad_all = (
        lax.all_gather(queries, "col", axis=0, tiled=True),
        lax.all_gather(d_out, "col", axis=0, tiled=True),
    )
    lse_all, delta_all = (
        lax.all_gather(lse, "col", axis=1, tiled=True),
        lax.all_gather(delta, "col", axis=1, tiled=True),
    )
    key_sum, value_sum, unused_terms = query_pass(
        query_all, grad_all, lse_all, delta_all, key_all, value_all, head_dim
    )

    def query_term(first_row, row_total):
        return query_only(query_all, grad_all, lse_all, delta_all, key_all, value_all, head_dim)

    query_grad = lax.psum_scatter(
        query_term(jnp.int32(0), queries.shape[0] * lax.axis_size("col")),
        "col",
        scatter_dimension=0,
        tiled=True,
    )
    key_grad, value_grad = (
        lax.psum_scatter(key_sum, "row", scatter_dimension=1, tiled=True),
        lax.psum_scatter(value_sum, "row", scatter_dimension=1, tiled=True),
    )
    d_queries = (query_grad * scaling).astype(jnp.bfloat16)
    d_keys = (key_grad * scaling).astype(jnp.bfloat16)
    d_values = value_grad.astype(jnp.bfloat16)
    return (d_queries, d_keys, d_values)

LOG2E = 1.4426950408889634


def flip(index, bits):
    if bits == 1:
        return index + 1 - 2 * lax.rem(index, 2)
    if bits == 2:
        return lax.rem(index + 2, 4)
    if bits == 3:
        return 3 - index
    return index


def fused_kernel(
    head_total,
    q_ref,
    k_ref,
    v_ref,
    o_ref,
    g_ref,
    lse_ref,
    dq_ref,
    dk_ref,
    dv_ref,
    qd_out,
    qd_in,
    st_out,
    st_in,
    kv_in,
    kt_in,
    dk_acc,
    dv_acc,
    dq_out,
    dq_in,
    dkv_out,
    dkv_in,
    qd_ssem,
    qd_rsem,
    st_ssem,
    st_rsem,
    kv_ssem,
    kv_rsem,
    dq_ssem,
    dq_rsem,
    dkv_ssem,
    dkv_rsem,
    o_in,
    lse_in,
    in_sem,
):
    row = lax.axis_index("row")
    col = lax.axis_index("col")
    zone = col // 4
    lane = lax.rem(col, 4)
    inner = lax.rem(zone + 1, 4) // 2 == 1
    other = 1 - row
    dim = k_ref.shape[1]
    scaling = dim ** (-0.5)
    MESH = pl.DeviceIdType.MESH

    def at(r, z, m):
        return (r, z * 4 + m)

    loads = []
    for h in range(head_total):
        cols = pl.ds(h * dim, dim)
        loads.append(pltpu.make_async_copy(q_ref.at[:, cols], qd_out.at[h, 0], in_sem.at[2 * h]))
        loads.append(pltpu.make_async_copy(g_ref.at[:, cols], qd_out.at[h, 1], in_sem.at[2 * h + 1]))
    key_loads = [
        pltpu.make_async_copy(k_ref, kv_in.at[lane, 0], in_sem.at[4]),
        pltpu.make_async_copy(v_ref, kv_in.at[lane, 1], in_sem.at[5]),
    ]
    row_loads = [
        pltpu.make_async_copy(o_ref, o_in, in_sem.at[6]),
        pltpu.make_async_copy(lse_ref, lse_in, in_sem.at[7]),
    ]
    for load in loads + key_loads + row_loads:
        load.start()

    mates = [at(row, zone, flip(lane, j)) for j in (1, 2)]
    owners = [at(other, zone, lane)]
    for s in (1, 2, 3):
        owners += [at(r, flip(zone, s), lane) for r in range(head_total)]
    barrier = pltpu.get_barrier_semaphore()
    for peer in mates + owners:
        pl.semaphore_signal(barrier, inc=1, device_id=peer, device_id_type=MESH)

    def kv_copy(j, slot):
        return pltpu.make_async_remote_copy(
            src_ref=kv_in.at[lane],
            dst_ref=kv_in.at[slot],
            send_sem=kv_ssem.at[j],
            recv_sem=kv_rsem.at[slot],
            device_id=at(row, zone, flip(lane, j)),
            device_id_type=MESH,
        )

    def kv_pass():
        slot = flip(lane, 2)
        return pltpu.make_async_remote_copy(
            src_ref=kv_in.at[slot],
            dst_ref=kv_in.at[slot],
            send_sem=kv_ssem.at[3],
            recv_sem=kv_rsem.at[slot],
            device_id=at(row, zone, flip(lane, 1)),
            device_id_type=MESH,
        )

    def st_copy(s, r, slot_zone, slot_row):
        return pltpu.make_async_remote_copy(
            src_ref=st_out.at[r],
            dst_ref=st_in.at[slot_zone, slot_row],
            send_sem=st_ssem.at[s, r],
            recv_sem=st_rsem.at[slot_zone, slot_row],
            device_id=at(r, flip(zone, s), lane),
            device_id_type=MESH,
        )

    def qd_copy(s, r, slot_zone, slot_row):
        return pltpu.make_async_remote_copy(
            src_ref=qd_out.at[r],
            dst_ref=qd_in.at[slot_zone, :, slot_row],
            send_sem=qd_ssem.at[s, r],
            recv_sem=qd_rsem.at[slot_zone, slot_row],
            device_id=at(r, flip(zone, s), lane),
            device_id_type=MESH,
        )

    def rows_of(s):
        return [other] if s == 0 else list(range(head_total))

    sends = []

    def launch(copy):
        copy.start()
        sends.append(copy)

    for load in loads:
        load.wait()
    pl.semaphore_wait(barrier, len(mates) + len(owners))
    @pl.when(jnp.logical_not(inner))
    def _():
        for r in rows_of(3):
            qd_copy(3, r, zone, row).start()

    for r in rows_of(2):
        launch(qd_copy(2, r, zone, row))
    for load in key_loads:
        load.wait()
    for j in (2, 1):
        launch(kv_copy(j, lane))
    for s in (0, 1):
        for r in rows_of(s):
            launch(qd_copy(s, r, zone, row))
    qd_in[zone, 0, row] = qd_out[row, 0]
    qd_in[zone, 1, row] = qd_out[row, 1]

    for load in row_loads:
        load.wait()
    for h in range(head_total):
        cols = slice(h * dim, (h + 1) * dim)
        product = qd_out[h, 1].astype(jnp.float32) * o_in[:, cols].astype(jnp.float32)
        delta = lax.dot_general(
            jnp.ones((8, dim), jnp.float32),
            product,
            (((1,), (1,)), ((), ())),
            precision=lax.Precision.HIGHEST,
            preferred_element_type=jnp.float32,
        )
        lse_rows = jnp.broadcast_to(lse_in[h : h + 1, :] * LOG2E, delta.shape)
        upper = lax.broadcasted_iota(jnp.int32, delta.shape, 0) < 4
        st_out[h] = jnp.where(upper, lse_rows, delta)
    st_in[zone, row] = st_out[row]
    for s in (2, 0, 3, 1):
        for r in rows_of(s):
            launch(st_copy(s, r, zone, row))

    def dq_copy(s, r, slot_row, slot_zone):
        there = flip(zone, s)
        return pltpu.make_async_remote_copy(
            src_ref=dq_out.at[there, r],
            dst_ref=dq_in.at[slot_row, slot_zone],
            send_sem=dq_ssem.at[s, r],
            recv_sem=dq_rsem.at[slot_row, slot_zone],
            device_id=at(r, there, lane),
            device_id_type=MESH,
        )

    def dkv_copy(j):
        return pltpu.make_async_remote_copy(
            src_ref=dkv_out.at[j],
            dst_ref=dkv_in.at[j],
            send_sem=dkv_ssem.at[j],
            recv_sem=dkv_rsem.at[j],
            device_id=at(row, zone, flip(lane, 2 if j == 2 else 1)),
            device_id_type=MESH,
        )

    steps = (0, 1, 2, 3)
    for s in steps:
        there = flip(zone, s)
        for r in rows_of(s):
            qd_copy(s, r, there, r).wait_recv()
        for r in rows_of(s):
            st_copy(s, r, there, r).wait_recv()
        rows2 = head_total * q_ref.shape[0]
        query = qd_in[there, 0].reshape(rows2, dim)
        grad = qd_in[there, 1].reshape(rows2, dim)
        lse_row = jnp.concatenate([st_in[there, r, 0:1, :] for r in range(head_total)], axis=1)
        delta_row = jnp.concatenate([st_in[there, r, 4:5, :] for r in range(head_total)], axis=1)
        query_sum = None
        order = (0, 1, 2, 3) if s < 3 else (3, 2, 1, 0)
        for j in order:
            slot = flip(lane, j)
            if s == 0:
                if j > 0:
                    kv_copy(j, slot).wait_recv()
                if j == 2:
                    launch(kv_pass())
                kt_in[slot] = kv_in[slot, 0].T
            key = kv_in[slot, 0]
            value = kv_in[slot, 1]
            dims = (((1,), (1,)), ((), ()))
            scores = lax.dot_general(key, query, dims, preferred_element_type=jnp.float32)
            grad_probs = lax.dot_general(value, grad, dims, preferred_element_type=jnp.float32)
            probs = jnp.exp2(scores * (scaling * LOG2E) - lse_row)
            probs_low = probs.astype(jnp.bfloat16)
            grad_scores = (probs * (grad_probs - delta_row)).astype(jnp.bfloat16)
            value_term = jnp.dot(probs_low, grad, preferred_element_type=jnp.float32)
            key_term = jnp.dot(grad_scores, query, preferred_element_type=jnp.float32)
            query_term = jnp.dot(kt_in[slot], grad_scores, preferred_element_type=jnp.float32)
            query_sum = query_term if query_sum is None else query_sum + query_term
            if s > 0:
                key_term = dk_acc[slot] + key_term
                value_term = dv_acc[slot] + value_term
            if s == 3 and j in (1, 3):
                dkv_out[j, 0] = key_term.astype(jnp.bfloat16)
                dkv_out[j, 1] = value_term.astype(jnp.bfloat16)
                launch(dkv_copy(j))
            else:
                dk_acc[slot] = key_term
                dv_acc[slot] = value_term
            if s == 3 and j == 1:
                beside = flip(lane, 2)
                dkv_copy(3).wait_recv()
                key_pair = dk_acc[beside] + dkv_in[3, 0].astype(jnp.float32)
                value_pair = dv_acc[beside] + dkv_in[3, 1].astype(jnp.float32)
                dkv_out[2, 0] = key_pair.astype(jnp.bfloat16)
                dkv_out[2, 1] = value_pair.astype(jnp.bfloat16)
                launch(dkv_copy(2))
            if s == 0 and j == 0:

                @pl.when(inner)
                def _():
                    for r in rows_of(3):
                        qd_copy(3, r, zone, row).start()

        query_low = query_sum.astype(jnp.bfloat16)
        block = q_ref.shape[0]
        for r in range(head_total):
            dq_out[there, r] = query_low[:, r * block : (r + 1) * block]
        if s == 0:
            dq_in[row, zone] = dq_out[zone, row]
        for r in rows_of(s):
            launch(dq_copy(s, r, row, zone))

    for s in steps:
        for r in rows_of(s):
            dq_copy(s, r, r, flip(zone, s)).wait_recv()
    for h in range(head_total):
        total = dq_in[h, 0].astype(jnp.float32)
        for z in range(1, 4):
            total = total + dq_in[h, z].astype(jnp.float32)
        dq_ref[:, h * dim : (h + 1) * dim] = (total * scaling).T.astype(jnp.bfloat16)

    key_sum = dk_acc[lane]
    value_sum = dv_acc[lane]
    for j in (1, 2):
        dkv_copy(j).wait_recv()
        key_sum = key_sum + dkv_in[j, 0].astype(jnp.float32)
        value_sum = value_sum + dkv_in[j, 1].astype(jnp.float32)
    dk_ref[...] = (key_sum * scaling).astype(jnp.bfloat16)
    dv_ref[...] = value_sum.astype(jnp.bfloat16)
    for copy in sends:
        copy.wait_send()
    for r in rows_of(3):
        qd_copy(3, r, zone, row).wait_send()


def write_kernel(dq_ref, dk_ref, dv_ref, dq_out, dk_out, dv_out, dq_held, dk_held, dv_held, sems):
    groups = ((dq_ref, dq_held, dq_out), (dk_ref, dk_held, dk_out), (dv_ref, dv_held, dv_out))
    loads = [pltpu.make_async_copy(g[0], g[1], sems.at[0, i]) for i, g in enumerate(groups)]
    stores = [pltpu.make_async_copy(g[1], g[2], sems.at[1, i]) for i, g in enumerate(groups)]
    for load in loads:
        load.start()
    for load, store in zip(loads, stores):
        load.wait()
        store.start()
    for store in stores:
        store.wait()


def fused_device(queries, keys, values, outputs, d_out, lse):
    head_total = lse.shape[0]
    block = queries.shape[0]
    key_rows, dim = keys.shape
    zones, lanes = 4, 4
    bf16, f32 = jnp.bfloat16, jnp.float32
    dma = pltpu.SemaphoreType.DMA
    vmem = pl.BlockSpec(memory_space=pltpu.VMEM)
    pairs = head_total * block * zones * key_rows * lanes
    hbm = pl.BlockSpec(memory_space=pltpu.HBM)
    results = pl.pallas_call(
        functools.partial(fused_kernel, head_total),
        out_shape=(
            jax.ShapeDtypeStruct(queries.shape, bf16),
            jax.ShapeDtypeStruct(keys.shape, bf16),
            jax.ShapeDtypeStruct(values.shape, bf16),
        ),
        in_specs=[hbm] * 6,
        out_specs=(vmem, vmem, vmem),
        scratch_shapes=[
            pltpu.VMEM((head_total, 2, block, dim), bf16),
            pltpu.VMEM((zones, 2, head_total, block, dim), bf16),
            pltpu.VMEM((head_total, 8, block), f32),
            pltpu.VMEM((zones, head_total, 8, block), f32),
            pltpu.VMEM((lanes, 2, key_rows, dim), bf16),
            pltpu.VMEM((lanes, dim, key_rows), bf16),
            pltpu.VMEM((lanes, key_rows, dim), f32),
            pltpu.VMEM((lanes, key_rows, dim), f32),
            pltpu.VMEM((zones, head_total, dim, block), bf16),
            pltpu.VMEM((head_total, zones, dim, block), bf16),
            pltpu.VMEM((lanes, 2, key_rows, dim), bf16),
            pltpu.VMEM((lanes, 2, key_rows, dim), bf16),
            dma((zones, head_total)),
            dma((zones, head_total)),
            dma((zones, head_total)),
            dma((zones, head_total)),
            dma((lanes,)),
            dma((lanes,)),
            dma((zones, head_total)),
            dma((head_total, zones)),
            dma((lanes,)),
            dma((lanes,)),
            pltpu.VMEM(outputs.shape, bf16),
            pltpu.VMEM(lse.shape, f32),
            dma((8,)),
        ],
        compiler_params=pltpu.CompilerParams(
            collective_id=0, has_side_effects=True, vmem_limit_bytes=63 * 1024 * 1024
        ),
        cost_estimate=pl.CostEstimate(
            flops=10 * pairs * dim, bytes_accessed=9 * block * 2 * dim * 2, transcendentals=pairs
        ),
    )(queries, keys, values, outputs, d_out, lse)
    return pl.pallas_call(
        write_kernel,
        out_shape=tuple(jax.ShapeDtypeStruct(x.shape, x.dtype) for x in results),
        in_specs=[hbm] * 3,
        out_specs=(hbm, hbm, hbm),
        scratch_shapes=[pltpu.VMEM(x.shape, x.dtype) for x in results] + [dma((2, 3))],
        compiler_params=pltpu.CompilerParams(vmem_limit_bytes=63 * 1024 * 1024),
    )(*results)


def solution(mesh):
    placed = (
        P(("row", "col"), None),
        P("col", "row"),
        P("col", "row"),
        P(("row", "col"), None),
        P(("row", "col"), None),
        P(None, ("row", "col")),
    )
    fused = mesh.shape["row"] == 2 and mesh.shape["col"] == 16

    def local(queries, keys, values, outputs, d_out, lse):
        head_dim = queries.shape[1] // lse.shape[0]
        fits = lse.shape[0] == mesh.shape["row"] and head_dim == 128 and queries.shape[0] == 128
        chosen = fused_device if fused and fits else per_device
        return chosen(queries, keys, values, outputs, d_out, lse)

    return jax.shard_map(
        local,
        mesh=mesh,
        in_specs=placed,
        out_specs=(P(("row", "col"), None), P("col", "row"), P("col", "row")),
        check_vma=False,
    )
```

```python
import functools

import jax
import jax.numpy as jnp
from jax import lax
from jax.experimental import pallas as pl
from jax.experimental.pallas import tpu as pltpu
from jax.sharding import PartitionSpec as P


def block_size(row_total):
    block_rows = row_total
    while block_rows > 512 and block_rows % 2 == 0:
        block_rows = block_rows // 2
    return block_rows


def head_slice(matrix, head_index, head_dim):
    return matrix[:, head_index * head_dim : (head_index + 1) * head_dim]


def contract_rows(left, right):
    return lax.dot_general(
        left, right, (((0,), (0,)), ((), ())), preferred_element_type=jnp.float32
    )


def score_terms(query_head, grad_head, lse_row, delta_row, key_head, value_head, scaling):
    scores = jnp.dot(query_head, key_head.T, preferred_element_type=jnp.float32)
    probs = jnp.exp(scores * scaling - lse_row[:, None])
    probs_low = probs.astype(jnp.bfloat16)
    grad_probs = jnp.dot(grad_head, value_head.T, preferred_element_type=jnp.float32)
    grad_scores = (probs * (grad_probs - delta_row[:, None])).astype(jnp.bfloat16)
    return (probs_low, grad_scores)


def block_grads(query_rows, grad_rows, lse_rows, delta_rows, key_all, value_all, head_dim):
    head_total = lse_rows.shape[0]
    scaling = head_dim ** (-0.5)
    key_terms = []
    value_terms = []
    for head_index in range(head_total):
        query_head = head_slice(query_rows, head_index, head_dim)
        grad_head = head_slice(grad_rows, head_index, head_dim)
        key_head = head_slice(key_all, head_index, head_dim)
        value_head = head_slice(value_all, head_index, head_dim)
        probs_low, grad_scores = score_terms(
            query_head,
            grad_head,
            lse_rows[head_index],
            delta_rows[head_index],
            key_head,
            value_head,
            scaling,
        )
        value_terms.append(contract_rows(probs_low, grad_head))
        key_terms.append(contract_rows(grad_scores, query_head))
    key_term = jnp.concatenate(key_terms, axis=1)
    value_term = jnp.concatenate(value_terms, axis=1)
    query_term = None
    return (key_term, value_term, query_term)


def split_blocks(query_all, grad_all, lse_all, delta_all):
    row_total, features = query_all.shape
    block_rows = block_size(row_total)
    steps_total = row_total // block_rows
    head_total = lse_all.shape[0]
    query_blocks = query_all.reshape(steps_total, block_rows, features)
    grad_blocks = grad_all.reshape(steps_total, block_rows, features)
    lse_blocks = lse_all.reshape(head_total, steps_total, block_rows).transpose(1, 0, 2)
    delta_blocks = delta_all.reshape(head_total, steps_total, block_rows).transpose(1, 0, 2)
    return (query_blocks, grad_blocks, lse_blocks, delta_blocks)


def query_pass(query_all, grad_all, lse_all, delta_all, key_all, value_all, head_dim):
    row_total, features = query_all.shape
    block_inputs = split_blocks(query_all, grad_all, lse_all, delta_all)
    empty_sums = jnp.zeros((key_all.shape[0], features), jnp.float32)

    def advance(running, inputs):
        key_sum, value_sum = running
        query_rows, grad_rows, lse_rows, delta_rows = inputs
        key_term, value_term, query_term = block_grads(
            query_rows, grad_rows, lse_rows, delta_rows, key_all, value_all, head_dim
        )
        return ((key_sum + key_term, value_sum + value_term), query_term)

    (key_sum, value_sum), query_terms = lax.scan(advance, (empty_sums, empty_sums), block_inputs)
    return (key_sum, value_sum, query_terms)


def query_only(query_rows, grad_rows, lse_rows, delta_rows, key_all, value_all, head_dim):
    row_total, features = query_rows.shape
    head_total = lse_rows.shape[0]
    scaling = head_dim ** (-0.5)
    block_inputs = split_blocks(query_rows, grad_rows, lse_rows, delta_rows)

    def one_block(inputs):
        query_part, grad_part, lse_part, delta_part = inputs
        pieces = []
        for head_index in range(head_total):
            query_head = head_slice(query_part, head_index, head_dim)
            grad_head = head_slice(grad_part, head_index, head_dim)
            key_head = head_slice(key_all, head_index, head_dim)
            value_head = head_slice(value_all, head_index, head_dim)
            probs_low, grad_scores = score_terms(
                query_head,
                grad_head,
                lse_part[head_index],
                delta_part[head_index],
                key_head,
                value_head,
                scaling,
            )
            pieces.append(jnp.dot(grad_scores, key_head, preferred_element_type=jnp.float32))
        return jnp.concatenate(pieces, axis=1)

    return lax.map(one_block, block_inputs).reshape(row_total, features)


def head_delta(d_out, outputs, head_total, head_dim):
    product = d_out.astype(jnp.float32) * outputs.astype(jnp.float32)
    return jnp.sum(product.reshape(product.shape[0], head_total, head_dim), axis=2).T


def per_device(queries, keys, values, outputs, d_out, lse):
    head_total = lse.shape[0]
    head_dim = queries.shape[1] // head_total
    scaling = head_dim ** (-0.5)
    delta = head_delta(d_out, outputs, head_total, head_dim)
    key_all, value_all = (
        lax.all_gather(keys, "row", axis=1, tiled=True),
        lax.all_gather(values, "row", axis=1, tiled=True),
    )
    query_all, grad_all = (
        lax.all_gather(queries, "col", axis=0, tiled=True),
        lax.all_gather(d_out, "col", axis=0, tiled=True),
    )
    lse_all, delta_all = (
        lax.all_gather(lse, "col", axis=1, tiled=True),
        lax.all_gather(delta, "col", axis=1, tiled=True),
    )
    key_sum, value_sum, unused_terms = query_pass(
        query_all, grad_all, lse_all, delta_all, key_all, value_all, head_dim
    )

    def query_term(first_row, row_total):
        return query_only(query_all, grad_all, lse_all, delta_all, key_all, value_all, head_dim)

    query_grad = lax.psum_scatter(
        query_term(jnp.int32(0), queries.shape[0] * lax.axis_size("col")),
        "col",
        scatter_dimension=0,
        tiled=True,
    )
    key_grad, value_grad = (
        lax.psum_scatter(key_sum, "row", scatter_dimension=1, tiled=True),
        lax.psum_scatter(value_sum, "row", scatter_dimension=1, tiled=True),
    )
    d_queries = (query_grad * scaling).astype(jnp.bfloat16)
    d_keys = (key_grad * scaling).astype(jnp.bfloat16)
    d_values = value_grad.astype(jnp.bfloat16)
    return (d_queries, d_keys, d_values)

LOG2E = 1.4426950408889634


def flip(index, bits):
    if bits == 1:
        return index + 1 - 2 * lax.rem(index, 2)
    if bits == 2:
        return lax.rem(index + 2, 4)
    if bits == 3:
        return 3 - index
    return index


def fused_kernel(
    head_total,
    q_ref,
    k_ref,
    v_ref,
    o_ref,
    g_ref,
    lse_ref,
    dq_ref,
    dk_ref,
    dv_ref,
    qd_out,
    qd_in,
    st_out,
    st_in,
    kv_in,
    kt_in,
    dk_acc,
    dv_acc,
    dq_out,
    dq_in,
    dkv_out,
    dkv_in,
    qd_ssem,
    qd_rsem,
    st_ssem,
    st_rsem,
    kv_ssem,
    kv_rsem,
    dq_ssem,
    dq_rsem,
    dkv_ssem,
    dkv_rsem,
    o_in,
    lse_in,
    in_sem,
    relay_ssem,
):
    row = lax.axis_index("row")
    col = lax.axis_index("col")
    zone = col // 4
    lane = lax.rem(col, 4)
    inner = lax.rem(zone + 1, 4) // 2 == 1
    other = 1 - row
    dim = k_ref.shape[1]
    scaling = dim ** (-0.5)
    MESH = pl.DeviceIdType.MESH

    def at(r, z, m):
        return (r, z * 4 + m)

    loads = []
    for h in range(head_total):
        cols = pl.ds(h * dim, dim)
        loads.append(pltpu.make_async_copy(q_ref.at[:, cols], qd_out.at[h, 0], in_sem.at[2 * h]))
        loads.append(pltpu.make_async_copy(g_ref.at[:, cols], qd_out.at[h, 1], in_sem.at[2 * h + 1]))
    key_loads = [
        pltpu.make_async_copy(k_ref, kv_in.at[lane, 0], in_sem.at[4]),
        pltpu.make_async_copy(v_ref, kv_in.at[lane, 1], in_sem.at[5]),
    ]
    row_loads = [
        pltpu.make_async_copy(o_ref, o_in, in_sem.at[6]),
        pltpu.make_async_copy(lse_ref, lse_in, in_sem.at[7]),
    ]
    for load in loads + key_loads + row_loads:
        load.start()

    mates = [at(row, zone, flip(lane, j)) for j in (1, 2)]
    owners = [at(other, zone, lane)]
    for s in (1, 2, 3):
        owners += [at(r, flip(zone, s), lane) for r in range(head_total)]
    barrier = pltpu.get_barrier_semaphore()
    for peer in mates + owners:
        pl.semaphore_signal(barrier, inc=1, device_id=peer, device_id_type=MESH)

    def kv_copy(j, slot):
        return pltpu.make_async_remote_copy(
            src_ref=kv_in.at[lane],
            dst_ref=kv_in.at[slot],
            send_sem=kv_ssem.at[j],
            recv_sem=kv_rsem.at[slot],
            device_id=at(row, zone, flip(lane, j)),
            device_id_type=MESH,
        )

    def kv_pass():
        slot = flip(lane, 2)
        return pltpu.make_async_remote_copy(
            src_ref=kv_in.at[slot],
            dst_ref=kv_in.at[slot],
            send_sem=kv_ssem.at[3],
            recv_sem=kv_rsem.at[slot],
            device_id=at(row, zone, flip(lane, 1)),
            device_id_type=MESH,
        )

    def st_copy(s, r, slot_zone, slot_row):
        return pltpu.make_async_remote_copy(
            src_ref=st_out.at[r],
            dst_ref=st_in.at[slot_zone, slot_row],
            send_sem=st_ssem.at[s, r],
            recv_sem=st_rsem.at[slot_zone, slot_row],
            device_id=at(r, flip(zone, s), lane),
            device_id_type=MESH,
        )

    def qd_copy(s, r, slot_zone, slot_row):
        return pltpu.make_async_remote_copy(
            src_ref=qd_out.at[r],
            dst_ref=qd_in.at[slot_zone, :, slot_row],
            send_sem=qd_ssem.at[s, r],
            recv_sem=qd_rsem.at[slot_zone, slot_row],
            device_id=at(r, flip(zone, s), lane),
            device_id_type=MESH,
        )

    def relay_copy(r):
        slot_zone = flip(zone, 2)
        return pltpu.make_async_remote_copy(
            src_ref=qd_in.at[slot_zone, :, r],
            dst_ref=qd_in.at[slot_zone, :, r],
            send_sem=relay_ssem.at[r],
            recv_sem=qd_rsem.at[slot_zone, r],
            device_id=at(row, flip(zone, 1), lane),
            device_id_type=MESH,
        )

    def rows_of(s):
        return [other] if s == 0 else list(range(head_total))

    sends = []

    def launch(copy):
        copy.start()
        sends.append(copy)

    for load in loads:
        load.wait()
    pl.semaphore_wait(barrier, len(mates) + len(owners))
    for s in (2, 1):
        for r in rows_of(s):
            launch(qd_copy(s, r, zone, row))
    for load in key_loads:
        load.wait()
    for j in (2, 1):
        launch(kv_copy(j, lane))
    for r in rows_of(0):
        launch(qd_copy(0, r, zone, row))
    qd_in[zone, 0, row] = qd_out[row, 0]
    qd_in[zone, 1, row] = qd_out[row, 1]

    for load in row_loads:
        load.wait()
    for h in range(head_total):
        cols = slice(h * dim, (h + 1) * dim)
        product = qd_out[h, 1].astype(jnp.float32) * o_in[:, cols].astype(jnp.float32)
        delta = lax.dot_general(
            jnp.ones((8, dim), jnp.float32),
            product,
            (((1,), (1,)), ((), ())),
            precision=lax.Precision.HIGHEST,
            preferred_element_type=jnp.float32,
        )
        lse_rows = jnp.broadcast_to(lse_in[h : h + 1, :] * LOG2E, delta.shape)
        upper = lax.broadcasted_iota(jnp.int32, delta.shape, 0) < 4
        st_out[h] = jnp.where(upper, lse_rows, delta)
    st_in[zone, row] = st_out[row]
    for s in (2, 0, 3, 1):
        for r in rows_of(s):
            launch(st_copy(s, r, zone, row))

    def dq_copy(s, r, slot_row, slot_zone):
        there = flip(zone, s)
        return pltpu.make_async_remote_copy(
            src_ref=dq_out.at[there, r],
            dst_ref=dq_in.at[slot_row, slot_zone],
            send_sem=dq_ssem.at[s, r],
            recv_sem=dq_rsem.at[slot_row, slot_zone],
            device_id=at(r, there, lane),
            device_id_type=MESH,
        )

    def dkv_copy(j):
        return pltpu.make_async_remote_copy(
            src_ref=dkv_out.at[j],
            dst_ref=dkv_in.at[j],
            send_sem=dkv_ssem.at[j],
            recv_sem=dkv_rsem.at[j],
            device_id=at(row, zone, flip(lane, 2 if j == 2 else 1)),
            device_id_type=MESH,
        )

    steps = (0, 2, 1, 3)
    for s in steps:
        there = flip(zone, s)
        if s == 2:

            @pl.when(jnp.logical_not(inner))
            def _():
                for r in rows_of(2):
                    qd_copy(2, r, flip(zone, 2), r).wait_recv()

        else:
            for r in rows_of(s):
                qd_copy(s, r, there, r).wait_recv()
        for r in rows_of(s):
            st_copy(s, r, there, r).wait_recv()
        rows2 = head_total * q_ref.shape[0]
        query = qd_in[there, 0].reshape(rows2, dim)
        grad = qd_in[there, 1].reshape(rows2, dim)
        lse_row = jnp.concatenate([st_in[there, r, 0:1, :] for r in range(head_total)], axis=1)
        delta_row = jnp.concatenate([st_in[there, r, 4:5, :] for r in range(head_total)], axis=1)
        query_sum = None
        order = (0, 1, 2, 3) if s < 3 else (3, 2, 1, 0)
        for j in order:
            slot = flip(lane, j)
            if s == 0:
                if j > 0:
                    kv_copy(j, slot).wait_recv()
                if j == 2:
                    launch(kv_pass())

                    @pl.when(inner)
                    def _():
                        for r in rows_of(2):
                            qd_copy(2, r, flip(zone, 2), r).wait_recv()
                            relay_copy(r).start()

                kt_in[slot] = kv_in[slot, 0].T
            key = kv_in[slot, 0]
            value = kv_in[slot, 1]
            dims = (((1,), (1,)), ((), ()))
            scores = lax.dot_general(key, query, dims, preferred_element_type=jnp.float32)
            grad_probs = lax.dot_general(value, grad, dims, preferred_element_type=jnp.float32)
            probs = jnp.exp2(scores * (scaling * LOG2E) - lse_row)
            probs_low = probs.astype(jnp.bfloat16)
            grad_scores = (probs * (grad_probs - delta_row)).astype(jnp.bfloat16)
            value_term = jnp.dot(probs_low, grad, preferred_element_type=jnp.float32)
            key_term = jnp.dot(grad_scores, query, preferred_element_type=jnp.float32)
            query_term = jnp.dot(kt_in[slot], grad_scores, preferred_element_type=jnp.float32)
            query_sum = query_term if query_sum is None else query_sum + query_term
            if s > 0:
                key_term = dk_acc[slot] + key_term
                value_term = dv_acc[slot] + value_term
            if s == 3 and j in (1, 3):
                dkv_out[j, 0] = key_term.astype(jnp.bfloat16)
                dkv_out[j, 1] = value_term.astype(jnp.bfloat16)
                launch(dkv_copy(j))
            else:
                dk_acc[slot] = key_term
                dv_acc[slot] = value_term
            if s == 3 and j == 1:
                beside = flip(lane, 2)
                dkv_copy(3).wait_recv()
                key_pair = dk_acc[beside] + dkv_in[3, 0].astype(jnp.float32)
                value_pair = dv_acc[beside] + dkv_in[3, 1].astype(jnp.float32)
                dkv_out[2, 0] = key_pair.astype(jnp.bfloat16)
                dkv_out[2, 1] = value_pair.astype(jnp.bfloat16)
                launch(dkv_copy(2))
            if s == 0 and j == 0:

                @pl.when(inner)
                def _():
                    for r in rows_of(3):
                        qd_copy(3, r, zone, row).start()

        query_low = query_sum.astype(jnp.bfloat16)
        block = q_ref.shape[0]
        for r in range(head_total):
            dq_out[there, r] = query_low[:, r * block : (r + 1) * block]
        if s == 0:
            dq_in[row, zone] = dq_out[zone, row]
        for r in rows_of(s):
            launch(dq_copy(s, r, row, zone))

    for s in steps:
        for r in rows_of(s):
            dq_copy(s, r, r, flip(zone, s)).wait_recv()
    for h in range(head_total):
        total = dq_in[h, 0].astype(jnp.float32)
        for z in range(1, 4):
            total = total + dq_in[h, z].astype(jnp.float32)
        dq_ref[:, h * dim : (h + 1) * dim] = (total * scaling).T.astype(jnp.bfloat16)

    key_sum = dk_acc[lane]
    value_sum = dv_acc[lane]
    for j in (1, 2):
        dkv_copy(j).wait_recv()
        key_sum = key_sum + dkv_in[j, 0].astype(jnp.float32)
        value_sum = value_sum + dkv_in[j, 1].astype(jnp.float32)
    dk_ref[...] = (key_sum * scaling).astype(jnp.bfloat16)
    dv_ref[...] = value_sum.astype(jnp.bfloat16)
    for copy in sends:
        copy.wait_send()

    @pl.when(inner)
    def _():
        for r in rows_of(3):
            qd_copy(3, r, zone, row).wait_send()
            relay_copy(r).wait_send()


def write_kernel(dq_ref, dk_ref, dv_ref, dq_out, dk_out, dv_out, dq_held, dk_held, dv_held, sems):
    groups = ((dq_ref, dq_held, dq_out), (dk_ref, dk_held, dk_out), (dv_ref, dv_held, dv_out))
    loads = [pltpu.make_async_copy(g[0], g[1], sems.at[0, i]) for i, g in enumerate(groups)]
    stores = [pltpu.make_async_copy(g[1], g[2], sems.at[1, i]) for i, g in enumerate(groups)]
    for load in loads:
        load.start()
    for load, store in zip(loads, stores):
        load.wait()
        store.start()
    for store in stores:
        store.wait()


def fused_device(queries, keys, values, outputs, d_out, lse):
    head_total = lse.shape[0]
    block = queries.shape[0]
    key_rows, dim = keys.shape
    zones, lanes = 4, 4
    bf16, f32 = jnp.bfloat16, jnp.float32
    dma = pltpu.SemaphoreType.DMA
    vmem = pl.BlockSpec(memory_space=pltpu.VMEM)
    pairs = head_total * block * zones * key_rows * lanes
    hbm = pl.BlockSpec(memory_space=pltpu.HBM)
    results = pl.pallas_call(
        functools.partial(fused_kernel, head_total),
        out_shape=(
            jax.ShapeDtypeStruct(queries.shape, bf16),
            jax.ShapeDtypeStruct(keys.shape, bf16),
            jax.ShapeDtypeStruct(values.shape, bf16),
        ),
        in_specs=[hbm] * 6,
        out_specs=(vmem, vmem, vmem),
        scratch_shapes=[
            pltpu.VMEM((head_total, 2, block, dim), bf16),
            pltpu.VMEM((zones, 2, head_total, block, dim), bf16),
            pltpu.VMEM((head_total, 8, block), f32),
            pltpu.VMEM((zones, head_total, 8, block), f32),
            pltpu.VMEM((lanes, 2, key_rows, dim), bf16),
            pltpu.VMEM((lanes, dim, key_rows), bf16),
            pltpu.VMEM((lanes, key_rows, dim), f32),
            pltpu.VMEM((lanes, key_rows, dim), f32),
            pltpu.VMEM((zones, head_total, dim, block), bf16),
            pltpu.VMEM((head_total, zones, dim, block), bf16),
            pltpu.VMEM((lanes, 2, key_rows, dim), bf16),
            pltpu.VMEM((lanes, 2, key_rows, dim), bf16),
            dma((zones, head_total)),
            dma((zones, head_total)),
            dma((zones, head_total)),
            dma((zones, head_total)),
            dma((lanes,)),
            dma((lanes,)),
            dma((zones, head_total)),
            dma((head_total, zones)),
            dma((lanes,)),
            dma((lanes,)),
            pltpu.VMEM(outputs.shape, bf16),
            pltpu.VMEM(lse.shape, f32),
            dma((8,)),
            dma((head_total,)),
        ],
        compiler_params=pltpu.CompilerParams(
            collective_id=0, has_side_effects=True, vmem_limit_bytes=63 * 1024 * 1024
        ),
        cost_estimate=pl.CostEstimate(
            flops=10 * pairs * dim, bytes_accessed=9 * block * 2 * dim * 2, transcendentals=pairs
        ),
    )(queries, keys, values, outputs, d_out, lse)
    return pl.pallas_call(
        write_kernel,
        out_shape=tuple(jax.ShapeDtypeStruct(x.shape, x.dtype) for x in results),
        in_specs=[hbm] * 3,
        out_specs=(hbm, hbm, hbm),
        scratch_shapes=[pltpu.VMEM(x.shape, x.dtype) for x in results] + [dma((2, 3))],
        compiler_params=pltpu.CompilerParams(vmem_limit_bytes=63 * 1024 * 1024),
    )(*results)


def solution(mesh):
    placed = (
        P(("row", "col"), None),
        P("col", "row"),
        P("col", "row"),
        P(("row", "col"), None),
        P(("row", "col"), None),
        P(None, ("row", "col")),
    )
    fused = mesh.shape["row"] == 2 and mesh.shape["col"] == 16

    def local(queries, keys, values, outputs, d_out, lse):
        head_dim = queries.shape[1] // lse.shape[0]
        fits = lse.shape[0] == mesh.shape["row"] and head_dim == 128 and queries.shape[0] == 128
        chosen = fused_device if fused and fits else per_device
        return chosen(queries, keys, values, outputs, d_out, lse)

    return jax.shard_map(
        local,
        mesh=mesh,
        in_specs=placed,
        out_specs=(P(("row", "col"), None), P("col", "row"), P("col", "row")),
        check_vma=False,
    )
```
